32 devices in a mesh: row: 4 (over y, x), col: 8 (over z, core).
Axes of the slice: x: 2, y: 2, z: 4, core: 2. Of those that a mesh axis runs over, the one named last changes fastest.
Arguments:
- tokens: bfloat16 [16384, 1536], P(('row', 'col'))
- g_attn: bfloat16 [1536], P(('row', 'col')), may hold values from 0.5 to 1.5
- w_query: bfloat16 [1536, 1536], P('row', 'col'), may hold values from -0.15625 to 0.15625
- key_projection: bfloat16 [1536, 512], P('row', 'col'), may hold values from -0.15625 to 0.15625
- value_projection: bfloat16 [1536, 512], P('row', 'col'), may hold values from -0.15625 to 0.15625
- w_out: bfloat16 [1536, 1536], P('row', 'col'), may hold values from -0.625 to 0.625
- g_moe: bfloat16 [1536], P(('row', 'col')), may hold values from 0.5 to 1.5
- w_router: bfloat16 [1536, 32], P('row', 'col'), may hold values from -0.078125 to 0.078125
- e_gate: bfloat16 [32, 1536, 512], P('col', 'row'), may hold values from -0.15625 to 0.15625
- e_up: bfloat16 [32, 1536, 512], P('col', 'row'), may hold values from -0.15625 to 0.15625
- e_down: bfloat16 [32, 512, 1536], P('col', None, 'row'), may hold values from -0.5 to 0.5
- s_gate: bfloat16 [1536, 1024], P('row', 'col'), may hold values from -0.15625 to 0.15625
- s_up: bfloat16 [1536, 1024], P('row', 'col'), may hold values from -0.15625 to 0.15625
- s_down: bfloat16 [1024, 1536], P('row', 'col'), may hold values from -0.375 to 0.375
- routes: int32 [16384, 6], P(('row', 'col')), may hold values from 0 to 31, all different within a row; in each aligned block of 512 rows (0 to 511, 512 to 1023, ...) at most 128 rows name the same one
- deal: int32 [32, 4], P(('row', 'col')), may hold values from 0 to 3, as said below
- lengths: int32 [32, 4], replicated, may hold values from 1 to 256, as said below
- cotangent: bfloat16 [16384, 1536], P(('row', 'col')), may hold values from -6 to 6
Outputs:
- output: bfloat16 [16384, 1536], P(('row', 'col'))
- grad_tokens: float32 [16384, 1536], P(('row', 'col'))
- grad_g_attn: float32 [1536], P(('row', 'col'))
- grad_w_query: float32 [1536, 1536], P('row', 'col')
- grad_w_key: float32 [1536, 512], P('row', 'col')
- grad_w_value: float32 [1536, 512], P('row', 'col')
- grad_w_out: float32 [1536, 1536], P('row', 'col')
- grad_g_moe: float32 [1536], P(('row', 'col'))
- grad_w_router: float32 [1536, 32], P('row', 'col')
- grad_e_gate: float32 [32, 1536, 512], P('col', 'row')
- grad_e_up: float32 [32, 1536, 512], P('col', 'row')
- grad_e_down: float32 [32, 512, 1536], P('col', None, 'row')
- grad_s_gate: float32 [1536, 1024], P('row', 'col')
- grad_s_up: float32 [1536, 1024], P('row', 'col')
- grad_s_down: float32 [1024, 1536], P('row', 'col')
The draws below stay inside these ranges and needn't reach their ends.
Inputs may be any that keep to these rules, and one draw needn't show every extreme that they name: Each row is an ordering of 0 to 3: device g sends its j-th sequence to the device with the same col index whose row index is deal[g, j]. lengths[d, k] is the length of the sequence that device d receives from the device of row index k with d's col index; the 4 sequences that one device sends sum to 512 tokens, and each device sends one of exactly 256. `routes`: among the rows of one device no expert is named more than 128 times.
All inputs are finite; a program needn't handle non-finite values.
Results may differ from the reference program's by a relative error of at most 0.018.
Values may be sent and summed in bfloat16 or wider, within the bound.
A program may use at most 320 MiB of HBM per device.

```python
import math
import jax
import jax.numpy as jnp
import numpy as np
from jax import lax

MODEL_WIDTH = 1536
QUERY_HEADS = 12
KEY_VALUE_HEADS = 4
HEAD_SIZE = 128
FE = 512
FS = 1024
TOP = 6
TOK_DEV = 512
EXPERTS = 32
TOKENS = 16384
LMAX = 256
CAP = 128
N_ROW = 4
N_COL = 8


def draw_tokens(key, part):
    key_values, key_row_list, key_cols = jax.random.split(key, 3)
    row_scale = jnp.exp(jax.random.uniform(key_row_list, (TOKENS, 1), jnp.float32, -0.5, 0.5) * 2.302585)
    col_scale = jnp.exp(jax.random.uniform(key_cols, (1, MODEL_WIDTH), jnp.float32, -0.5, 0.5) * 2.302585)
    values = jax.random.normal(key_values, (TOKENS, MODEL_WIDTH), jnp.float32) * row_scale * col_scale
    return values.astype(jnp.bfloat16)


def deal_plan(key):
    key_perm, key_spot, key_weights = jax.random.split(jax.random.fold_in(key, 7), 3)
    devices = N_ROW * N_COL
    perm_keys = jax.random.split(key_perm, devices)
    deal_table = jax.vmap(lambda subkey: jax.random.permutation(subkey, N_ROW))(perm_keys).astype(jnp.int32)
    rest_tokens = TOK_DEV - LMAX
    spread_tokens = rest_tokens - (N_ROW - 1)
    raw_weights = jax.random.randint(key_weights, (devices, N_ROW - 1), 4, 9).astype(jnp.int32)
    length_parts = raw_weights * spread_tokens // jnp.sum(raw_weights, axis=1, keepdims=True) + 1
    missing = rest_tokens - jnp.sum(length_parts, axis=1, keepdims=True)
    length_parts = length_parts + (jnp.arange(N_ROW - 1, dtype=jnp.int32)[None, :] < missing).astype(jnp.int32)
    all_lengths = jnp.concatenate([length_parts, jnp.full((devices, 1), LMAX, jnp.int32)], axis=1)
    spot_keys = jax.random.split(key_spot, devices)
    length_order = jax.vmap(lambda subkey: jax.random.permutation(subkey, N_ROW))(spot_keys).astype(jnp.int32)
    seq_lens = jnp.take_along_axis(all_lengths, length_order, axis=1).astype(jnp.int32)
    device_ids = jnp.arange(devices, dtype=jnp.int32)
    dest_rows = deal_table * N_COL + (device_ids % N_COL)[:, None]
    source_rows = jnp.broadcast_to((device_ids // N_COL)[:, None], (devices, N_ROW))
    length_table = jnp.zeros((devices, N_ROW), jnp.int32).at[dest_rows, source_rows].set(seq_lens)
    return (deal_table, length_table)


def draw_deal(key, part):
    return deal_plan(key)[0]


def draw_lengths(key, part):
    return deal_plan(key)[1]


def with_spikes(entries, key, source, target, shards_of, factor):
    owner, partner = [(jnp.arange(entries.shape[dim]) // (entries.shape[dim] // shards_of)).reshape([-1 if axis == dim else 1 for axis in range(entries.ndim)]) for dim in (source, target)]
    chosen = jax.random.permutation(key, shards_of)[partner]
    strong = (owner == chosen) | (owner == (partner + shards_of // 2) % shards_of)
    return jnp.where(strong, factor * entries, entries)


def steps_of(own_key, shape, pieces, least, largest):
    def one(axis_at, parts):
        heights = jax.random.uniform(jax.random.fold_in(jax.random.fold_in(own_key, 6), axis_at), (parts,), jnp.float32, least / len(pieces), largest / len(pieces))
        return jnp.repeat(jnp.exp(heights), shape[axis_at] // parts).reshape((-1,) + (1,) * (len(shape) - axis_at - 1))

    level = one(*pieces[0])
    for cut in pieces[1:]:
        level = level * one(*cut)
    return level


def routed_block(key, own, number, rows, count, top, bound, lean):
    order = jax.random.permutation(key, count)
    crowded, usual = load_shares(count, rows * top, bound, lean, True), load_shares(count, rows * top, bound, lean, False)
    places = jnp.arange(count)

    def named(sizes, turn):
        used = int((sizes > 0).sum())
        fixed = max(1, used // 4)
        passed = fixed + (places - fixed + turn * (used - fixed)) % max(1, count - fixed)
        return jnp.zeros((count,), jnp.int32).at[order[jnp.where(places < fixed, places, passed)]].set(jnp.asarray(sizes, jnp.int32))

    sizes = jnp.where(number % 4 == 0, named(crowded, number // 4), named(usual, number - number // 4 - 1))
    mixed = jax.random.permutation(jax.random.fold_in(own, 3), count)
    source_of, sink = mixed[0:count // 2 * 2:2], mixed[1:count // 2 * 2:2]
    margin = jnp.minimum(sizes[source_of] - 1, bound - sizes[sink]) // 2
    margin = jnp.where((source_of == order[0]) | (sink == order[0]) | (sizes[sink] == 0), 0, jnp.maximum(margin, 0))
    passed = jax.random.randint(jax.random.fold_in(own, 4), (count // 2,), 0, 1 << 20) % (margin + 1)
    sizes = sizes.at[source_of].add(-passed).at[sink].add(passed)
    labels = jnp.searchsorted(jnp.cumsum(sizes), jnp.arange(rows * top), side="right").astype(jnp.int32)
    table = labels.reshape(top, rows).T
    table = table[jax.random.permutation(jax.random.fold_in(own, 1), rows)]
    turn = jax.random.randint(jax.random.fold_in(own, 2), (rows, 1), 0, top)
    return jnp.take_along_axis(table, (jnp.arange(top)[None, :] + turn) % top, axis=1)


def load_shares(number_of, total, limit, skew, full):
    loads = [(1 << 20) // math.isqrt(grade ** skew) + 1 for grade in range(1, number_of + 1)]
    largest = limit if full else min(limit, max(-(-total // number_of), total * loads[0] // sum(loads)))
    least = 1 if total - largest >= number_of - 1 else 0
    counts, surplus = [largest] + [least] * (number_of - 1), total - largest - least * (number_of - 1)
    while surplus > 0:
        free = [i for i in range(1, number_of) if counts[i] < largest] or [i for i in range(1, number_of) if counts[i] < limit]
        whole, remaining = sum([loads[i] for i in free]), surplus
        for i in free:
            more = min(limit - counts[i], max(1, remaining * loads[i] // whole), surplus)
            counts[i] = counts[i] + more
            surplus = surplus - more
    return np.array(counts)


def gaussian(key, extent, width, reach, shards=(), kind=jnp.bfloat16):
    drawn = jax.random.normal(key, extent, jnp.float32) * width
    if len(shards) > 0:
        drawn = steps_of(key, extent, shards, -0.22, 0.18) * drawn
    return jnp.clip(drawn, min=-reach, max=reach).astype(kind)


def gaussian_with(stream_key, shape, spread, bound, pieces, heavy, held_as=jnp.bfloat16):
    entries = spread * jax.random.normal(stream_key, shape, jnp.float32)
    if pieces:
        entries = entries * steps_of(stream_key, shape, pieces, -0.22, 0.18)
    return jnp.clip(with_spikes(entries, jax.random.fold_in(stream_key, 3), *heavy), -bound, bound).astype(held_as)


def setup_inputs(seed: int = 0) -> dict:
    splits = jax.random.split(jax.random.key(seed), 19)
    tokens = draw_tokens(jax.random.fold_in(splits[18], 71), 0)
    g_attn = jnp.clip(1.0 + 0.1 * jax.random.normal(splits[1], (MODEL_WIDTH,), jnp.float32), 0.5, 1.5).astype(jnp.bfloat16)
    w_query = gaussian(splits[2], (MODEL_WIDTH, QUERY_HEADS * HEAD_SIZE), MODEL_WIDTH ** -0.5, 0.15625, ((0, 4), (1, 8)))
    key_projection = gaussian(splits[3], (MODEL_WIDTH, KEY_VALUE_HEADS * HEAD_SIZE), MODEL_WIDTH ** -0.5, 0.15625, ((0, 4), (1, 8)))
    value_projection = gaussian(splits[4], (MODEL_WIDTH, KEY_VALUE_HEADS * HEAD_SIZE), MODEL_WIDTH ** -0.5, 0.15625, ((0, 4), (1, 8)))
    w_out = gaussian(splits[5], (QUERY_HEADS * HEAD_SIZE, MODEL_WIDTH), (QUERY_HEADS * HEAD_SIZE // 16) ** -0.5, 0.625, ((0, 4), (1, 8)))
    g_moe = jnp.clip(1.0 + 0.1 * jax.random.normal(splits[6], (MODEL_WIDTH,), jnp.float32), 0.5, 1.5).astype(jnp.bfloat16)
    w_router = gaussian(splits[7], (MODEL_WIDTH, EXPERTS), (4 * MODEL_WIDTH) ** -0.5, 0.078125, ((0, 4), (1, 8)))
    e_gate = gaussian(splits[8], (EXPERTS, MODEL_WIDTH, FE), MODEL_WIDTH ** -0.5, 0.15625, ((0, 8), (1, 4)))
    e_up = gaussian(splits[9], (EXPERTS, MODEL_WIDTH, FE), MODEL_WIDTH ** -0.5, 0.15625, ((0, 8), (1, 4)))
    e_down = gaussian(splits[10], (EXPERTS, FE, MODEL_WIDTH), (FE // 4) ** -0.5, 0.5, ((0, 8), (2, 4)))
    s_gate = gaussian(splits[11], (MODEL_WIDTH, FS), MODEL_WIDTH ** -0.5, 0.15625, ((0, 4), (1, 8)))
    s_up = gaussian(splits[12], (MODEL_WIDTH, FS), MODEL_WIDTH ** -0.5, 0.15625, ((0, 4), (1, 8)))
    s_down = gaussian(splits[13], (FS, MODEL_WIDTH), (FS // 4) ** -0.5, 0.375, ((0, 4), (1, 8)))
    routes_keys = jax.random.split(jax.random.fold_in(splits[14], 1), TOKENS // TOK_DEV)
    routes_turns = jax.random.permutation(jax.random.fold_in(splits[14], 3), TOKENS // TOK_DEV)
    routes = jax.vmap(lambda own, number: routed_block(jax.random.fold_in(splits[14], 2), own, number, TOK_DEV, EXPERTS, TOP, CAP, 1))(routes_keys, routes_turns).reshape((TOKENS, TOP))
    deal = draw_deal(jax.random.fold_in(splits[18], 71), 0)
    lengths = draw_lengths(jax.random.fold_in(splits[18], 71), 0)
    cotangent = gaussian_with(splits[17], (TOKENS, MODEL_WIDTH), 1.0, 6.0, ((0, 32),), (0, 1, 32, 2.75))
    return dict(tokens=tokens, g_attn=g_attn, w_query=w_query, key_projection=key_projection, value_projection=value_projection, w_out=w_out, g_moe=g_moe, w_router=w_router, e_gate=e_gate, e_up=e_up, e_down=e_down, s_gate=s_gate, s_up=s_up, s_down=s_down, routes=routes, deal=deal, lengths=lengths, cotangent=cotangent)


@jax.custom_vjp
def low(v):
    return lax.optimization_barrier(v.astype(jnp.bfloat16)).astype(jnp.float32)

@jax.custom_vjp
def low_back(v):
    return v

def low_keep(v):
    return (low(v), None)

def low_pass(kept, grad):
    return (grad,)

def back_keep(v):
    return (v, None)

def back_low(kept, grad):
    return (low(grad),)
low.defvjp(low_keep, low_pass)
low_back.defvjp(back_keep, back_low)
top_precision = lax.Precision.HIGHEST
norm_eps = 1e-05
masked_score = -1e+30

def rms_scale(rows):
    return lax.rsqrt(lax.optimization_barrier(jnp.mean(rows * rows, axis=-1, keepdims=True)) + norm_eps)

def silu_of(values):
    return values * jax.nn.sigmoid(values)

def matmul(left, right):
    return jnp.dot(left, right, precision=top_precision)

def attention_rows(query_row_list, key_row_list, value_row_list, segment):
    token_total = query_row_list.shape[0]
    query_heads_split = query_row_list.reshape(token_total, KEY_VALUE_HEADS, QUERY_HEADS // KEY_VALUE_HEADS, HEAD_SIZE)
    key_heads_split = key_row_list.reshape(token_total, KEY_VALUE_HEADS, HEAD_SIZE)
    value_heads_split = value_row_list.reshape(token_total, KEY_VALUE_HEADS, HEAD_SIZE)
    scores = jnp.einsum('qhgd,khd->hgqk', query_heads_split, key_heads_split, precision=top_precision) * HEAD_SIZE ** (-0.5)
    scores = low_back(scores)
    places = jnp.arange(token_total, dtype=jnp.int32)
    allowed = (segment[:, None] == segment[None, :]) & (places[None, :] <= places[:, None])
    masked = jnp.where(allowed, scores, masked_score)
    row_peak = lax.optimization_barrier(jnp.max(masked, axis=-1, keepdims=True))
    raw_weights = jnp.exp(masked - row_peak)
    attn_probs = raw_weights / lax.optimization_barrier(jnp.sum(raw_weights, axis=-1, keepdims=True))
    mixed = jnp.einsum('hgqk,khd->qhgd', low(attn_probs), value_heads_split, precision=top_precision)
    return mixed.reshape(token_total, QUERY_HEADS * HEAD_SIZE)

def block_stretch(params, stretch):
    g_attn, w_query, key_projection, value_projection, w_out, g_moe, w_router, e_gate, e_up, e_down, s_gate, s_up, s_down = params
    tokens_f, routes_c, lens_c = stretch
    token_total = tokens_f.shape[0]
    experts = e_gate.shape[0]
    seq_ends = jnp.cumsum(lens_c)
    places = jnp.arange(token_total, dtype=jnp.int32)
    segment = lax.optimization_barrier(jnp.sum((places[:, None] >= seq_ends[None, :]).astype(jnp.int32), axis=1))
    normed_one = low(tokens_f * rms_scale(tokens_f) * g_attn)
    query_row_list = low(low_back(matmul(normed_one, w_query)))
    key_row_list = low(low_back(matmul(normed_one, key_projection)))
    value_row_list = low(low_back(matmul(normed_one, value_projection)))
    mixed = low(low_back(attention_rows(query_row_list, key_row_list, value_row_list, segment)))
    after_attn = tokens_f + low_back(matmul(mixed, w_out))
    normed_two = low(after_attn * rms_scale(after_attn) * g_moe)
    logits = low_back(matmul(normed_two, w_router))
    route_picks = (routes_c[:, :, None] == jnp.arange(experts, dtype=jnp.int32)[None, None, :]).astype(jnp.float32)
    chosen = jnp.einsum('tre,te->tr', route_picks, logits, precision=top_precision)
    chosen_peak = lax.optimization_barrier(jnp.max(chosen, axis=-1, keepdims=True))
    gate_raw = jnp.exp(chosen - chosen_peak)
    gate_weights = gate_raw / lax.optimization_barrier(jnp.sum(gate_raw, axis=-1, keepdims=True))
    flat_routes = routes_c.reshape(-1)
    onehot = (flat_routes[:, None] == jnp.arange(experts, dtype=jnp.int32)[None, :]).astype(jnp.int32)
    route_ranks = lax.optimization_barrier(jnp.sum((jnp.cumsum(onehot, axis=0) - 1) * onehot, axis=1))
    route_slots = flat_routes * CAP + route_ranks
    slot_owner = jnp.full((experts * CAP,), -1, jnp.int32).at[route_slots].set(jnp.arange(token_total * TOP, dtype=jnp.int32))
    filled = slot_owner >= 0
    owner_token = jnp.where(filled, slot_owner // TOP, 0).astype(jnp.int32)
    expert_input = jnp.where(filled[:, None], jnp.take(normed_two, owner_token, axis=0), 0.0)
    expert_input = low_back(expert_input).reshape(experts, CAP, MODEL_WIDTH)
    gate_part = low_back(jnp.einsum('ecd,edf->ecf', expert_input, e_gate, precision=top_precision))
    up_portion = low_back(jnp.einsum('ecd,edf->ecf', expert_input, e_up, precision=top_precision))
    hidden = low(silu_of(gate_part) * up_portion)
    expert_out = low(low_back(jnp.einsum('ecf,efd->ecd', hidden, e_down, precision=top_precision)))
    routed = jnp.take(expert_out.reshape(experts * CAP, MODEL_WIDTH), route_slots, axis=0).reshape(token_total, TOP, MODEL_WIDTH)
    moe_sum = jnp.einsum('tr,trd->td', gate_weights, routed, precision=top_precision)
    shared_gate = low_back(matmul(normed_two, s_gate))
    shared_up = low_back(matmul(normed_two, s_up))
    shared_hidden = low(silu_of(shared_gate) * shared_up)
    shared_out = matmul(shared_hidden, s_down)
    return after_attn + moe_sum + shared_out

def reference(tokens, g_attn, w_query, key_projection, value_projection, w_out, g_moe, w_router, e_gate, e_up, e_down, s_gate, s_up, s_down, routes, deal, lengths, cotangent):
    devices = N_ROW * N_COL
    device_ids = jnp.arange(devices, dtype=jnp.int32)
    dest_rows = (deal * N_COL + (device_ids % N_COL)[:, None]).astype(jnp.int32)
    source_rows = jnp.broadcast_to((device_ids // N_COL)[:, None], deal.shape).astype(jnp.int32)
    seq_lens = lengths[dest_rows, source_rows]
    params = tuple((array.astype(jnp.float32) for array in (g_attn, w_query, key_projection, value_projection, w_out, g_moe, w_router, e_gate, e_up, e_down, s_gate, s_up, s_down)))
    route_stretches = routes.reshape(devices, TOK_DEV, TOP)

    def forward(tokens_all, weights):

        def stretch_fn(stretch):
            return jax.checkpoint(block_stretch)(weights, stretch)
        results = lax.map(stretch_fn, (tokens_all.reshape(devices, TOK_DEV, MODEL_WIDTH), route_stretches, seq_lens))
        return results.reshape(devices * TOK_DEV, MODEL_WIDTH)
    output_f, pullback = jax.vjp(forward, tokens.astype(jnp.float32), params)
    grad_tokens, grad_params = pullback(cotangent.astype(jnp.float32))
    return (output_f.astype(jnp.bfloat16), grad_tokens, grad_params[0], grad_params[1], grad_params[2], grad_params[3], grad_params[4], grad_params[5], grad_params[6], grad_params[7], grad_params[8], grad_params[9], grad_params[10], grad_params[11], grad_params[12])
```

```python
import functools

import jax
import jax.numpy as jnp
from jax import lax
from jax.experimental import pallas as pl
from jax.experimental.pallas import tpu as pltpu
from jax.sharding import PartitionSpec as P

MODEL_WIDTH = 1536
QUERY_HEADS = 12
KEY_VALUE_HEADS = 4
GROUP = QUERY_HEADS // KEY_VALUE_HEADS
HEAD_SIZE = 128
TOP = 6
EXP_DEV = 4

norm_eps = 1e-05
masked_score = -1e30
BF = jnp.bfloat16
F32 = jnp.float32


def rms_scale(rows):
    return lax.rsqrt(jnp.mean(rows * rows, axis=-1, keepdims=True) + norm_eps)


def silu_parts(values):
    sigmoid_of = jax.nn.sigmoid(values)
    return (values * sigmoid_of, sigmoid_of * (1.0 + values * (1.0 - sigmoid_of)))


def norm_back(grad_normed, unit_rows, scale_rows, gain):
    grad_unit = grad_normed * gain
    grad_rows = scale_rows * (
        grad_unit - unit_rows * jnp.mean(grad_unit * unit_rows, axis=-1, keepdims=True)
    )
    return (grad_rows, jnp.sum(grad_normed * unit_rows, axis=0))


def mm(left, right):
    return jnp.dot(left, right, preferred_element_type=F32)


def mm_nt(left, right):
    return lax.dot_general(left, right, (((1,), (1,)), ((), ())), preferred_element_type=F32)


def mm_tn(left, right):
    return lax.dot_general(left, right, (((0,), (0,)), ((), ())), preferred_element_type=F32)


def ein(spec, a, b):
    return jnp.einsum(spec, a, b, preferred_element_type=F32)


def allowed_mask(seg_col, seg_row):
    total = seg_col.shape[0]
    q_at = lax.broadcasted_iota(jnp.int32, (total, total), 0)
    k_at = lax.broadcasted_iota(jnp.int32, (total, total), 1)
    return (seg_col == seg_row) & (k_at <= q_at)


def attend_forward_kernel(q_ref, k_ref, v_ref, segc_ref, segr_ref, mixed_ref, lse_ref):
    allowed = allowed_mask(segc_ref[...], segr_ref[...])
    keys = k_ref[...]
    values = v_ref[...]
    for g in range(GROUP):
        cols = slice(g * HEAD_SIZE, (g + 1) * HEAD_SIZE)
        scores = mm_nt(q_ref[:, cols], keys) * HEAD_SIZE ** (-0.5)
        scores = jnp.where(allowed, scores, masked_score)
        peak = jnp.max(scores, axis=-1, keepdims=True)
        raw = jnp.exp(scores - peak)
        total = jnp.sum(raw, axis=-1, keepdims=True)
        probs = (raw * (1.0 / total)).astype(BF)
        mixed_ref[:, cols] = mm(probs, values).astype(BF)
        lse_ref[0, :, g : g + 1] = peak + jnp.log(total)


def attend_backward_kernel(
    q_ref, k_ref, v_ref, gm_ref, segc_ref, segr_ref, lse_ref, gq_ref, gk_ref, gv_ref
):
    allowed = allowed_mask(segc_ref[...], segr_ref[...])
    keys = k_ref[...]
    values = v_ref[...]
    scale = HEAD_SIZE ** (-0.5)
    grad_key = None
    for g in range(GROUP):
        cols = slice(g * HEAD_SIZE, (g + 1) * HEAD_SIZE)
        query = q_ref[:, cols]
        grad_mixed = gm_ref[:, cols]
        scores = mm_nt(query, keys) * scale
        probs = jnp.where(allowed, jnp.exp(scores - lse_ref[0, :, g : g + 1]), 0.0)
        grad_probs = mm_nt(grad_mixed, values)
        inner = jnp.sum(probs * grad_probs, axis=-1, keepdims=True)
        grad_scores = (probs * (grad_probs - inner)).astype(BF)
        gq_ref[:, cols] = (mm(grad_scores, keys) * scale).astype(BF)
        part_key = mm_tn(grad_scores, query)
        part_value = mm_tn(probs.astype(BF), grad_mixed)
        if grad_key is None:
            grad_key, grad_value = part_key, part_value
        else:
            grad_key, grad_value = grad_key + part_key, grad_value + part_value
    gk_ref[...] = (grad_key * scale).astype(BF)
    gv_ref[...] = grad_value.astype(BF)


def attention_specs(total):
    wide = pl.BlockSpec((total, GROUP * HEAD_SIZE), lambda h: (0, h))
    narrow = pl.BlockSpec((total, HEAD_SIZE), lambda h: (0, h))
    seg_col = pl.BlockSpec((total, 1), lambda h: (0, 0))
    seg_row = pl.BlockSpec((1, total), lambda h: (0, 0))
    lse = pl.BlockSpec((1, total, GROUP), lambda h: (h, 0, 0))
    return wide, narrow, seg_col, seg_row, lse


def attend_forward(queries, keys, values, segment):
    total = queries.shape[0]
    wide, narrow, seg_col, seg_row, lse = attention_specs(total)
    return pl.pallas_call(
        attend_forward_kernel,
        grid=(KEY_VALUE_HEADS,),
        in_specs=[wide, narrow, narrow, seg_col, seg_row],
        out_specs=[wide, lse],
        out_shape=[
            jax.ShapeDtypeStruct(queries.shape, BF),
            jax.ShapeDtypeStruct((KEY_VALUE_HEADS, total, GROUP), F32),
        ],
        compiler_params=pltpu.CompilerParams(vmem_limit_bytes=48 * 1024 * 1024),
        name="attend_forward",
    )(queries, keys, values, segment[:, None], segment[None, :])


def attend_backward(queries, keys, values, grad_mixed, segment, log_totals):
    total = queries.shape[0]
    wide, narrow, seg_col, seg_row, lse = attention_specs(total)
    return pl.pallas_call(
        attend_backward_kernel,
        grid=(KEY_VALUE_HEADS,),
        in_specs=[wide, narrow, narrow, wide, seg_col, seg_row, lse],
        out_specs=[wide, narrow, narrow],
        out_shape=[
            jax.ShapeDtypeStruct(queries.shape, BF),
            jax.ShapeDtypeStruct(keys.shape, BF),
            jax.ShapeDtypeStruct(keys.shape, BF),
        ],
        compiler_params=pltpu.CompilerParams(vmem_limit_bytes=48 * 1024 * 1024),
        name="attend_backward",
    )(queries, keys, values, grad_mixed, segment[:, None], segment[None, :], log_totals)


def on_device(
    tokens,
    g_attn,
    w_query,
    key_projection,
    value_projection,
    w_out,
    g_moe,
    w_router,
    e_gate,
    e_up,
    e_down,
    s_gate,
    s_up,
    s_down,
    routes,
    deal,
    lengths,
    cotangent,
):
    rows_n = lax.axis_size("row")
    cols_n = lax.axis_size("col")
    row_here = lax.axis_index("row")
    col_here = lax.axis_index("col")
    both = ("row", "col")
    total = tokens.shape[0]
    width = MODEL_WIDTH
    experts = EXP_DEV * cols_n
    cap = 4 * total * TOP // (3 * experts)

    q_w, k_w = w_query.shape[1], key_projection.shape[1]
    bundle = jnp.concatenate([w_query.T, key_projection.T, value_projection.T, w_out.T], axis=0)
    full = lax.all_gather(bundle, both, axis=0).reshape(
        (rows_n, cols_n) + bundle.shape
    )

    def piece(lo, extent):
        part = full[:, :, lo : lo + extent]
        return part.transpose(1, 2, 0, 3).reshape(cols_n * extent, width)

    wq_t = piece(0, q_w)
    wk_t = piece(q_w, k_w)
    wv_t = piece(q_w + k_w, k_w)
    wo_t = piece(q_w + 2 * k_w, q_w)
    gain_attn = lax.all_gather(g_attn, both, axis=0, tiled=True).astype(F32)
    gain_moe = lax.all_gather(g_moe, both, axis=0, tiled=True).astype(F32)
    router = lax.all_gather(
        lax.all_gather(w_router, "col", axis=1, tiled=True), "row", axis=0, tiled=True
    )
    egate = lax.all_gather(e_gate, "row", axis=1, tiled=True)
    eup = lax.all_gather(e_up, "row", axis=1, tiled=True)
    edown = lax.all_gather(e_down, "row", axis=2, tiled=True)
    sgate = lax.all_gather(s_gate, "row", axis=0, tiled=True)
    sup = lax.all_gather(s_up, "row", axis=0, tiled=True)
    units = s_gate.shape[1]
    per_row = s_down.shape[0] // units
    sdown_cols = lax.all_gather(s_down, "col", axis=1, tiled=True)
    sdown_mine = lax.dynamic_slice_in_dim(sdown_cols, (col_here % per_row) * units, units, 0)
    sdown = lax.dynamic_index_in_dim(
        lax.all_gather(sdown_mine, "row", axis=0), col_here // per_row, 0, keepdims=False
    )
    dy_all = lax.all_gather(cotangent, "col", axis=0)
    routes_all = lax.all_gather(routes, "col", axis=0)

    own_lens = lengths[deal.reshape(-1) * cols_n + col_here, row_here]
    seq_ends = jnp.cumsum(own_lens)
    places = jnp.arange(total, dtype=jnp.int32)
    segment = jnp.sum((places[:, None] >= seq_ends[None, :]).astype(jnp.int32), axis=1)

    tokens_f = tokens.astype(F32)
    scale_one = rms_scale(tokens_f)
    unit_one = tokens_f * scale_one
    normed_one = (unit_one * gain_attn).astype(BF)
    queries = mm_nt(normed_one, wq_t).astype(BF)
    keys = mm_nt(normed_one, wk_t).astype(BF)
    values = mm_nt(normed_one, wv_t).astype(BF)
    mixed, log_totals = attend_forward(queries, keys, values, segment)
    after_attn = tokens_f + mm_nt(mixed, wo_t)
    scale_two = rms_scale(after_attn)
    unit_two = after_attn * scale_two
    normed_two = (unit_two * gain_moe).astype(BF)
    logits = mm(normed_two, router)
    route_picks = (
        routes[:, :, None] == jnp.arange(experts, dtype=jnp.int32)[None, None, :]
    ).astype(F32)
    chosen = jnp.sum(route_picks * logits[:, None, :], axis=-1)
    gate_raw = jnp.exp(chosen - jnp.max(chosen, axis=-1, keepdims=True))
    gate_weights = gate_raw / jnp.sum(gate_raw, axis=-1, keepdims=True)

    x_all = lax.all_gather(normed_two, "col", axis=0)
    gates_all = lax.all_gather(gate_weights, "col", axis=0)
    mine = col_here * EXP_DEV + jnp.arange(EXP_DEV, dtype=jnp.int32)
    hits = routes_all[:, :, :, None] == mine
    hit = jnp.any(hits, axis=2)
    gate = jnp.sum(jnp.where(hits, gates_all[:, :, :, None], 0.0), axis=2)
    rank = jnp.where(hit, jnp.cumsum(hit.astype(jnp.int32), axis=1) - 1, -1)
    rank = rank.transpose(0, 2, 1)
    gate = gate.transpose(0, 2, 1)
    pick = rank[:, :, None, :] == jnp.arange(cap, dtype=jnp.int32)[None, None, :, None]
    slot_gate = jnp.sum(jnp.where(pick, gate[:, :, None, :], 0.0), axis=-1)
    pick_b = pick.astype(BF)
    xs = ein("sept,std->sepd", pick_b, x_all).astype(BF)
    dys = ein("sept,std->sepd", pick_b, dy_all).astype(BF)
    gate_part = ein("sepd,edf->sepf", xs, egate)
    up_part = ein("sepd,edf->sepf", xs, eup)
    act, slope = silu_parts(gate_part)
    hidden_f = (act * up_part).astype(BF).astype(F32)
    gated_hidden = (hidden_f * slot_gate[..., None]).astype(BF)
    weighted = ein("sepf,efd->sepd", gated_hidden, edown).astype(BF)
    out_part = ein("sept,sepd->std", pick_b, weighted)
    grad_hidden = ein("sepd,efd->sepf", dys, edown)
    slot_ggw = jnp.sum(hidden_f * grad_hidden, axis=-1)
    ggw = jnp.sum(jnp.where(pick, slot_ggw[..., None], 0.0), axis=2)
    grad_hidden = grad_hidden * slot_gate[..., None]
    geg = (grad_hidden * up_part * slope).astype(BF)
    geu = (grad_hidden * act).astype(BF)
    grad_edown = ein("sepf,sepd->efd", gated_hidden, dys)
    grad_egate = ein("sepd,sepf->edf", xs, geg)
    grad_eup = ein("sepd,sepf->edf", xs, geu)
    grad_in = (ein("sepf,edf->sepd", geg, egate) + ein("sepf,edf->sepd", geu, eup)).astype(BF)
    gx_part = ein("sept,sepd->std", pick_b, grad_in)
    x_flat = x_all.reshape(cols_n * total, width)
    dy_flat = dy_all.reshape(cols_n * total, width)
    s_act, s_slope = silu_parts(mm(x_flat, sgate))
    s_upv = mm(x_flat, sup)
    s_hidden = (s_act * s_upv).astype(BF)
    gsh = mm_nt(dy_flat, sdown)
    gsg = (gsh * s_upv * s_slope).astype(BF)
    gsu = (gsh * s_act).astype(BF)
    out_part = out_part + mm(s_hidden, sdown).reshape(out_part.shape)
    gx_part = gx_part + (mm_nt(gsg, sgate) + mm_nt(gsu, sup)).reshape(gx_part.shape)
    grad_sgate = mm_tn(x_flat, gsg)
    grad_sup = mm_tn(x_flat, gsu)
    grad_sdown = mm_tn(s_hidden, dy_flat)

    gx = lax.psum_scatter(gx_part.astype(BF), "col", scatter_dimension=0)
    moe = lax.psum_scatter(out_part.astype(BF), "col", scatter_dimension=0)
    output = (after_attn + moe.astype(F32)).astype(BF)
    ggw_home = lax.all_to_all(ggw, "col", split_axis=0, concat_axis=0, tiled=True)
    ggw_home = ggw_home.reshape(experts, total).T

    grad_gates = jnp.sum(route_picks * ggw_home[:, None, :], axis=-1)
    grad_chosen = gate_weights * (
        grad_gates - jnp.sum(gate_weights * grad_gates, axis=-1, keepdims=True)
    )
    grad_logits = jnp.sum(route_picks * grad_chosen[:, :, None], axis=1).astype(BF)
    grad_router = mm_tn(normed_two, grad_logits)
    grad_normed_two = gx.astype(F32) + mm_nt(grad_logits, router)
    grad_two, grad_gain_moe = norm_back(grad_normed_two, unit_two, scale_two, gain_moe)
    grad_after = cotangent.astype(F32) + grad_two
    grad_attn_b = grad_after.astype(BF)
    grad_wout = mm_tn(grad_attn_b, mixed)
    grad_mixed = mm(grad_attn_b, wo_t).astype(BF)
    gq, gk, gv = attend_backward(queries, keys, values, grad_mixed, segment, log_totals)
    grad_wq = mm_tn(gq, normed_one)
    grad_wk = mm_tn(gk, normed_one)
    grad_wv = mm_tn(gv, normed_one)
    grad_normed_one = mm(gq, wq_t) + mm(gk, wk_t) + mm(gv, wv_t)
    grad_one, grad_gain_attn = norm_back(grad_normed_one, unit_one, scale_one, gain_attn)
    grad_tokens = grad_after + grad_one

    def cut(grad):
        part = grad.reshape(cols_n, grad.shape[0] // cols_n, rows_n, width // rows_n)
        return part.transpose(2, 0, 1, 3)

    grads = jnp.concatenate(
        [cut(grad_wq), cut(grad_wk), cut(grad_wv), cut(grad_wout)], axis=2
    ).astype(BF)
    grads = lax.psum_scatter(
        grads.reshape((rows_n * cols_n,) + bundle.shape), both, scatter_dimension=0
    ).astype(F32)
    out_wq = grads[:q_w].T
    out_wk = grads[q_w : q_w + k_w].T
    out_wv = grads[q_w + k_w : q_w + 2 * k_w].T
    out_wo = grads[q_w + 2 * k_w :].T
    out_g_attn = lax.psum_scatter(grad_gain_attn, both, scatter_dimension=0, tiled=True)
    out_g_moe = lax.psum_scatter(grad_gain_moe, both, scatter_dimension=0, tiled=True)
    out_router = lax.psum_scatter(
        lax.psum_scatter(grad_router, "col", scatter_dimension=1, tiled=True),
        "row",
        scatter_dimension=0,
        tiled=True,
    )

    def row_sum(grad, dim):
        return lax.psum_scatter(
            grad.astype(BF), "row", scatter_dimension=dim, tiled=True
        ).astype(F32)

    out_eg = row_sum(grad_egate, 1)
    out_eu = row_sum(grad_eup, 1)
    out_ed = row_sum(grad_edown, 2)
    out_sg = row_sum(grad_sgate, 0)
    out_su = row_sum(grad_sup, 0)
    sd_sum = lax.psum(grad_sdown.astype(BF), "row")
    sd_parts = sd_sum.reshape(units, cols_n, width // cols_n).transpose(1, 0, 2)
    sd_home = lax.all_to_all(sd_parts, "col", split_axis=0, concat_axis=0, tiled=True)
    out_sd = lax.dynamic_slice_in_dim(sd_home, row_here * per_row, per_row, 0)
    out_sd = out_sd.reshape(per_row * units, width // cols_n).astype(F32)
    return (
        output,
        grad_tokens,
        out_g_attn,
        out_wq,
        out_wk,
        out_wv,
        out_wo,
        out_g_moe,
        out_router,
        out_eg,
        out_eu,
        out_ed,
        out_sg,
        out_su,
        out_sd,
    )


def solution(mesh):
    both = P(("row", "col"), None)
    flat = P(("row", "col"))
    tile = P("row", "col")
    wide = P("col", "row", None)
    down = P("col", None, "row")
    return jax.shard_map(
        on_device,
        mesh=mesh,
        in_specs=(
            both, flat, tile, tile, tile, tile, flat, tile, wide, wide, down,
            tile, tile, tile, both, both, P(), both,
        ),
        out_specs=(
            both, both, flat, tile, tile, tile, tile, flat, tile, wide, wide, down,
            tile, tile, tile,
        ),
        check_vma=False,
    )
```

```python
import functools

import jax
import jax.numpy as jnp
from jax import lax
from jax.experimental import pallas as pl
from jax.experimental.pallas import tpu as pltpu
from jax.sharding import PartitionSpec as P

MODEL_WIDTH = 1536
QUERY_HEADS = 12
KEY_VALUE_HEADS = 4
GROUP = QUERY_HEADS // KEY_VALUE_HEADS
HEAD_SIZE = 128
TOP = 6
EXP_DEV = 4

norm_eps = 1e-05
masked_score = -1e30
BF = jnp.bfloat16
F32 = jnp.float32


def rms_scale(rows):
    return lax.rsqrt(jnp.mean(rows * rows, axis=-1, keepdims=True) + norm_eps)


def silu_parts(values):
    sigmoid_of = jax.nn.sigmoid(values)
    return (values * sigmoid_of, sigmoid_of * (1.0 + values * (1.0 - sigmoid_of)))


def norm_back(grad_normed, unit_rows, scale_rows, gain):
    grad_unit = grad_normed * gain
    grad_rows = scale_rows * (
        grad_unit - unit_rows * jnp.mean(grad_unit * unit_rows, axis=-1, keepdims=True)
    )
    return (grad_rows, jnp.sum(grad_normed * unit_rows, axis=0))


def mm(left, right):
    return jnp.dot(left, right, preferred_element_type=F32)


def mm_nt(left, right):
    return lax.dot_general(left, right, (((1,), (1,)), ((), ())), preferred_element_type=F32)


def mm_tn(left, right):
    return lax.dot_general(left, right, (((0,), (0,)), ((), ())), preferred_element_type=F32)


def ein(spec, a, b):
    return jnp.einsum(spec, a, b, preferred_element_type=F32)


def allowed_mask(seg_col, seg_row):
    total = seg_col.shape[0]
    q_at = lax.broadcasted_iota(jnp.int32, (total, total), 0)
    k_at = lax.broadcasted_iota(jnp.int32, (total, total), 1)
    return (seg_col == seg_row) & (k_at <= q_at)


def attend_forward_kernel(q_ref, k_ref, v_ref, segc_ref, segr_ref, mixed_ref, lse_ref):
    allowed = allowed_mask(segc_ref[...], segr_ref[...])
    keys = k_ref[...]
    values = v_ref[...]
    for g in range(GROUP):
        cols = slice(g * HEAD_SIZE, (g + 1) * HEAD_SIZE)
        scores = mm_nt(q_ref[:, cols], keys) * HEAD_SIZE ** (-0.5)
        scores = jnp.where(allowed, scores, masked_score)
        peak = jnp.max(scores, axis=-1, keepdims=True)
        raw = jnp.exp(scores - peak)
        total = jnp.sum(raw, axis=-1, keepdims=True)
        probs = (raw * (1.0 / total)).astype(BF)
        mixed_ref[:, cols] = mm(probs, values).astype(BF)
        lse_ref[0, :, g : g + 1] = peak + jnp.log(total)


def attend_backward_kernel(
    q_ref, k_ref, v_ref, gm_ref, segc_ref, segr_ref, lse_ref, gq_ref, gk_ref, gv_ref
):
    allowed = allowed_mask(segc_ref[...], segr_ref[...])
    keys = k_ref[...]
    values = v_ref[...]
    scale = HEAD_SIZE ** (-0.5)
    grad_key = None
    for g in range(GROUP):
        cols = slice(g * HEAD_SIZE, (g + 1) * HEAD_SIZE)
        query = q_ref[:, cols]
        grad_mixed = gm_ref[:, cols]
        scores = mm_nt(query, keys) * scale
        probs = jnp.where(allowed, jnp.exp(scores - lse_ref[0, :, g : g + 1]), 0.0)
        grad_probs = mm_nt(grad_mixed, values)
        inner = jnp.sum(probs * grad_probs, axis=-1, keepdims=True)
        grad_scores = (probs * (grad_probs - inner)).astype(BF)
        gq_ref[:, cols] = (mm(grad_scores, keys) * scale).astype(BF)
        part_key = mm_tn(grad_scores, query)
        part_value = mm_tn(probs.astype(BF), grad_mixed)
        if grad_key is None:
            grad_key, grad_value = part_key, part_value
        else:
            grad_key, grad_value = grad_key + part_key, grad_value + part_value
    gk_ref[...] = (grad_key * scale).astype(BF)
    gv_ref[...] = grad_value.astype(BF)


def attention_specs(total):
    wide = pl.BlockSpec((total, GROUP * HEAD_SIZE), lambda h: (0, h))
    narrow = pl.BlockSpec((total, HEAD_SIZE), lambda h: (0, h))
    seg_col = pl.BlockSpec((total, 1), lambda h: (0, 0))
    seg_row = pl.BlockSpec((1, total), lambda h: (0, 0))
    lse = pl.BlockSpec((1, total, GROUP), lambda h: (h, 0, 0))
    return wide, narrow, seg_col, seg_row, lse


def attend_forward(queries, keys, values, segment):
    total = queries.shape[0]
    wide, narrow, seg_col, seg_row, lse = attention_specs(total)
    return pl.pallas_call(
        attend_forward_kernel,
        grid=(KEY_VALUE_HEADS,),
        in_specs=[wide, narrow, narrow, seg_col, seg_row],
        out_specs=[wide, lse],
        out_shape=[
            jax.ShapeDtypeStruct(queries.shape, BF),
            jax.ShapeDtypeStruct((KEY_VALUE_HEADS, total, GROUP), F32),
        ],
        compiler_params=pltpu.CompilerParams(vmem_limit_bytes=48 * 1024 * 1024),
        name="attend_forward",
    )(queries, keys, values, segment[:, None], segment[None, :])


def attend_backward(queries, keys, values, grad_mixed, segment, log_totals):
    total = queries.shape[0]
    wide, narrow, seg_col, seg_row, lse = attention_specs(total)
    return pl.pallas_call(
        attend_backward_kernel,
        grid=(KEY_VALUE_HEADS,),
        in_specs=[wide, narrow, narrow, wide, seg_col, seg_row, lse],
        out_specs=[wide, narrow, narrow],
        out_shape=[
            jax.ShapeDtypeStruct(queries.shape, BF),
            jax.ShapeDtypeStruct(keys.shape, BF),
            jax.ShapeDtypeStruct(keys.shape, BF),
        ],
        compiler_params=pltpu.CompilerParams(vmem_limit_bytes=48 * 1024 * 1024),
        name="attend_backward",
    )(queries, keys, values, grad_mixed, segment[:, None], segment[None, :], log_totals)


def remote(src, dst, send_sem, recv_sem, device):
    return pltpu.make_async_remote_copy(
        src_ref=src,
        dst_ref=dst,
        send_sem=send_sem,
        recv_sem=recv_sem,
        device_id=device,
        device_id_type=pl.DeviceIdType.MESH,
    )


class Place:
    def __init__(self, rows_n, cols_n):
        self.rows_n = rows_n
        self.chips = cols_n // 2
        self.row = lax.axis_index("row")
        self.col = lax.axis_index("col")
        self.chip = lax.div(self.col, 2)
        self.core = lax.rem(self.col, 2)
        self.other = self.col + 1 - 2 * self.core

    def peer_row(self, step):
        return lax.rem(self.row + step, self.rows_n)

    def greet(self, with_rows, with_downs=0):
        barrier = pltpu.get_barrier_semaphore()

        def hello(row, col):
            pl.semaphore_signal(
                barrier, inc=1, device_id=(row, col), device_id_type=pl.DeviceIdType.MESH
            )

        hello(self.row, self.other)

        @pl.when(self.chip > 0)
        def _():
            hello(self.row, self.col - 2)

        @pl.when(self.chip < self.chips - 1)
        def _():
            hello(self.row, self.col + 2)

        count = (
            1
            + (self.chip > 0).astype(jnp.int32)
            + (self.chip < self.chips - 1).astype(jnp.int32)
        )
        if with_rows:
            for step in range(1, self.rows_n):
                hello(self.peer_row(step), self.col)
            count = count + (self.rows_n - 1)
        pl.semaphore_wait(barrier, count)


class LineGather:
    def __init__(self, place, src, dst, core_sems, line_sems, recv_sems, local_sem):
        self.at = place
        self.src, self.dst = src, dst
        self.core_sems, self.line_sems, self.recv_sems = core_sems, line_sems, recv_sems
        self.local = pltpu.make_async_copy(src, dst.at[place.col], local_sem)

    def to_core(self, block, src=None):
        at = self.at
        src = self.dst.at[block] if src is None else src
        return remote(
            src, self.dst.at[block], self.core_sems.at[block], self.recv_sems.at[block],
            (at.row, at.other),
        )

    def to_line(self, block, way, src=None):
        at = self.at
        src = self.dst.at[block] if src is None else src
        return remote(
            src,
            self.dst.at[block],
            self.line_sems.at[block, (way + 1) // 2],
            self.recv_sems.at[block],
            (at.row, at.col + 2 * way),
        )

    def ends(self, way):
        return self.at.chip < self.at.chips - 1 if way > 0 else self.at.chip > 0

    def start(self):
        self.local.start()
        for way in (1, -1):

            @pl.when(self.ends(way))
            def _():
                self.to_line(self.at.col, way, self.src).start()

        self.to_core(self.at.col, self.src).start()

    def arrivals(self, dist, act):
        for way in (1, -1):
            chip = self.at.chip - way * dist
            near = chip >= 0 if way > 0 else chip < self.at.chips

            @pl.when(near)
            def _():
                act(2 * chip + self.at.core, way)

    def step(self, dist, extra=None):
        def act(block, way):
            self.to_core(block).wait_recv()

            @pl.when(self.ends(way))
            def _():
                self.to_line(block, way).start()

            self.to_core(block).start()
            if extra is not None:
                extra(block)

        self.arrivals(dist, act)

    def finish(self):
        self.local.wait()
        self.to_core(self.at.col, self.src).wait_send()
        for way in (1, -1):

            @pl.when(self.ends(way))
            def _():
                self.to_line(self.at.col, way, self.src).wait_send()

        def act(block, way):
            self.to_core(block).wait_send()

            @pl.when(self.ends(way))
            def _():
                self.to_line(block, way).wait_send()

        for dist in range(1, self.at.chips):
            self.arrivals(dist, act)
        for chip in range(self.at.chips):
            self.to_core(2 * chip + 1 - self.at.core).wait_recv()


def gather_sems(cols_n):
    return [
        pltpu.SemaphoreType.DMA((cols_n,)),
        pltpu.SemaphoreType.DMA((cols_n, 2)),
        pltpu.SemaphoreType.DMA((cols_n,)),
        pltpu.SemaphoreType.DMA,
    ]


ANY = pl.BlockSpec(memory_space=pl.ANY)


def line_gather(arrays, collective_id, rows_n, cols_n):
    n = len(arrays)

    def kernel(*refs):
        srcs, dsts, sems = refs[:n], refs[n : 2 * n], refs[2 * n :]
        place = Place(rows_n, cols_n)
        place.greet(False)
        jobs = [
            LineGather(place, srcs[i], dsts[i], *sems[4 * i : 4 * i + 4]) for i in range(n)
        ]
        for job in jobs:
            job.start()
        for dist in range(1, place.chips):
            for job in jobs:
                job.step(dist)
        for job in jobs:
            job.finish()

    return pl.pallas_call(
        kernel,
        in_specs=[ANY] * n,
        out_specs=[ANY] * n,
        out_shape=[jax.ShapeDtypeStruct((cols_n,) + a.shape, a.dtype) for a in arrays],
        scratch_shapes=gather_sems(cols_n) * n,
        compiler_params=pltpu.CompilerParams(collective_id=collective_id, has_side_effects=True),
        name="line_gather",
    )(*arrays)


def first_gather(bundle, cotangent, routes_t, shared, collective_id, rows_n, cols_n):
    def kernel(
        bundle_ref, dy_ref, rt_ref, sh_ref, full_ref, dy_all, rt_all, sh_all, *sems
    ):
        place = Place(rows_n, cols_n)
        b_sems, sems = sems[:4], sems[4:]
        d_sems, sems = sems[:4], sems[4:]
        r_sems, sems = sems[:4], sems[4:]
        row_send, row_core, row_recv, sh_send, sh_recv, sh_local = sems
        place.greet(True)
        row, col = place.row, place.col
        weights = LineGather(place, bundle_ref, full_ref.at[row], *b_sems)
        grads = LineGather(place, dy_ref, dy_all, *d_sems)
        picks = LineGather(place, rt_ref, rt_all, *r_sems)

        def to_row(block, step, src=None):
            home = full_ref.at[row, block]
            return remote(
                home if src is None else src, home, row_send.at[block, step],
                row_recv.at[row, block], (place.peer_row(step), col),
            )

        def push(block, src=None):
            for step in range(1, rows_n):
                to_row(block, step, src).start()

        def from_row(other_row, block):
            home = full_ref.at[other_row, block]
            return remote(
                home, home, row_core.at[other_row, block], row_recv.at[other_row, block],
                (row, place.other),
            )

        def shared_to(step):
            return remote(
                sh_ref, sh_all.at[row], sh_send.at[step], sh_recv.at[row],
                (place.peer_row(step), col),
            )

        weights.start()
        push(col, bundle_ref)
        shared_here = pltpu.make_async_copy(sh_ref, sh_all.at[row], sh_local)
        shared_here.start()
        for step in range(1, rows_n):
            shared_to(step).start()
        for dist in range(1, place.chips):
            weights.step(dist, push)
        grads.start()
        picks.start()
        for dist in range(1, place.chips - 1):
            grads.step(dist)
            picks.step(dist)
        for step in range(1, rows_n):
            other_row = place.peer_row(step)

            @pl.loop(0, place.chips)
            def _(chip):
                copy = from_row(other_row, 2 * chip + place.core)
                copy.wait_recv()
                copy.start()

        grads.step(place.chips - 1)
        picks.step(place.chips - 1)
        weights.finish()
        grads.finish()
        picks.finish()
        shared_here.wait()
        for step in range(1, rows_n):
            other_row = place.peer_row(step)
            shared_to(step).wait_send()
            remote(
                sh_ref, sh_all.at[other_row], sh_send.at[0], sh_recv.at[other_row],
                (other_row, col),
            ).wait_recv()

            @pl.loop(0, place.chips)
            def _(chip):
                to_row(2 * chip + place.core, step).wait_send()
                from_row(other_row, 2 * chip + place.core).wait_send()
                from_row(other_row, 2 * chip + 1 - place.core).wait_recv()

    return pl.pallas_call(
        kernel,
        in_specs=[ANY] * 4,
        out_specs=[ANY] * 4,
        out_shape=[
            jax.ShapeDtypeStruct((rows_n, cols_n) + bundle.shape, bundle.dtype),
            jax.ShapeDtypeStruct((cols_n,) + cotangent.shape, cotangent.dtype),
            jax.ShapeDtypeStruct((cols_n,) + routes_t.shape, routes_t.dtype),
            jax.ShapeDtypeStruct((rows_n,) + shared.shape, shared.dtype),
        ],
        scratch_shapes=gather_sems(cols_n) * 3
        + [
            pltpu.SemaphoreType.DMA((cols_n, rows_n)),
            pltpu.SemaphoreType.DMA((rows_n, cols_n)),
            pltpu.SemaphoreType.DMA((rows_n, cols_n)),
            pltpu.SemaphoreType.DMA((rows_n,)),
            pltpu.SemaphoreType.DMA((rows_n,)),
            pltpu.SemaphoreType.DMA,
        ],
        compiler_params=pltpu.CompilerParams(collective_id=collective_id, has_side_effects=True),
        name="first_gather",
    )(bundle, cotangent, routes_t, shared)


def line_sum_loop(place, mine, recv, send_sems, recv_sems, parts, ready):
    chips, here = place.chips, place.chip
    rows = mine.shape[1] // parts
    items = (chips - 1) * parts

    def copy(chip, part, way):
        span = pl.ds(part * rows, rows)
        goal = here + way
        land = chip if way > 0 else jnp.where(chip == goal, chips, chip)
        return remote(
            mine.at[chip, span],
            recv.at[land, span],
            send_sems.at[chip, part],
            recv_sems.at[land, part],
            (place.row, place.col + 2 * way),
        )

    def incoming(land, part):
        span = pl.ds(part * rows, rows)
        return remote(
            mine.at[0, span], recv.at[land, span], send_sems.at[0, part],
            recv_sems.at[land, part], (place.row, place.other),
        )

    def handle(chip, part, way):
        @pl.when(part == 0)
        def _():
            ready(chip)

        span = pl.ds(part * rows, rows)
        comes = here > 0 if way > 0 else here < chips - 1

        @pl.when(comes)
        def _():
            incoming(chip, part).wait_recv()
            total = mine[chip, span].astype(F32) + recv[chip, span].astype(F32)
            mine[chip, span] = total.astype(mine.dtype)

        copy(chip, part, way).start()

    lag = 2 * (chips - 2 - here)

    @pl.loop(0, items + 2 * (chips - 2))
    def _(at):
        up = jnp.minimum(at, items - 1)
        up_chip = chips - 1 - lax.div(up, parts)

        @pl.when((at < items) & (up_chip > here))
        def _():
            handle(up_chip, lax.rem(up, parts), 1)

        down = at - jnp.maximum(lag, 0)
        safe = jnp.clip(down, 0, items - 1)
        down_chip = lax.div(safe, parts)

        @pl.when((down >= 0) & (down < items) & (down_chip < here))
        def _():
            handle(down_chip, lax.rem(safe, parts), -1)

    ready(here)

    def result(part, store):
        span = pl.ds(part * rows, rows)
        total = mine[here, span].astype(F32)

        @pl.when((here > 0) & (here < chips - 1))
        def _():
            incoming(here, part).wait_recv()
            incoming(chips, part).wait_recv()
            store(span, total + recv[here, span].astype(F32) + recv[chips, span].astype(F32))

        @pl.when((here > 0) & (here == chips - 1))
        def _():
            incoming(here, part).wait_recv()
            store(span, total + recv[here, span].astype(F32))

        @pl.when((here == 0) & (here < chips - 1))
        def _():
            incoming(chips, part).wait_recv()
            store(span, total + recv[chips, span].astype(F32))

    def drain():
        @pl.loop(0, chips)
        def _(chip):
            for part in range(parts):

                @pl.when(chip > here)
                def _():
                    copy(chip, part, 1).wait_send()

                @pl.when(chip < here)
                def _():
                    copy(chip, part, -1).wait_send()

    return result, drain


LINE_PARTS = 4


def line_sum(parts_all, collective_id, rows_n, cols_n):
    chips = cols_n // 2
    block = parts_all.shape[2:]

    def kernel(
        in_ref, out_ref, mine, extra, recv, load_sems, core_send, core_recv, send_sems, recv_sems
    ):
        place = Place(rows_n, cols_n)

        def load(chip):
            return pltpu.make_async_copy(
                in_ref.at[place.core, chip], mine.at[chip], load_sems.at[chip]
            )

        def swap(chip):
            return remote(
                in_ref.at[1 - place.core, chip], extra.at[chip], core_send.at[chip],
                core_recv.at[chip], (place.row, place.other),
            )

        order = []
        for i in range((chips + 1) // 2):
            order += [chips - 1 - i, i] if chips - 1 - i != i else [i]
        for chip in order:
            load(chip).start()
        place.greet(False)
        for chip in order:
            swap(chip).start()

        def ready(chip):
            load(chip).wait()
            swap(chip).wait_recv()
            rows = block[0] // LINE_PARTS
            for part in range(LINE_PARTS):
                span = pl.ds(part * rows, rows)
                mine[chip, span] = (
                    mine[chip, span].astype(F32) + extra[chip, span].astype(F32)
                ).astype(mine.dtype)

        result, drain = line_sum_loop(
            place, mine, recv, send_sems, recv_sems, LINE_PARTS, ready
        )

        def store(span, value):
            out_ref[span] = value

        for part in range(LINE_PARTS):
            result(part, store)
        drain()
        for chip in range(chips):
            swap(chip).wait_send()

    return pl.pallas_call(
        kernel,
        in_specs=[ANY],
        out_specs=pl.BlockSpec(memory_space=pltpu.VMEM),
        out_shape=jax.ShapeDtypeStruct(block, F32),
        scratch_shapes=[
            pltpu.VMEM((chips,) + block, BF),
            pltpu.VMEM((chips,) + block, BF),
            pltpu.VMEM((chips + 1,) + block, BF),
            pltpu.SemaphoreType.DMA((chips,)),
            pltpu.SemaphoreType.DMA((chips,)),
            pltpu.SemaphoreType.DMA((chips,)),
            pltpu.SemaphoreType.DMA((chips, LINE_PARTS)),
            pltpu.SemaphoreType.DMA((chips + 1, LINE_PARTS)),
        ],
        compiler_params=pltpu.CompilerParams(
            collective_id=collective_id, has_side_effects=True,
            vmem_limit_bytes=58 * 1024 * 1024,
        ),
        name="line_sum",
    )(parts_all)


def dense_sum(grads, shared, collective_id, rows_n, cols_n):
    chips = cols_n // 2
    block = grads.shape[3:]

    def kernel(
        in_ref, sh_ref, out_ref, sh_out, mine, extra, rows_in, recv, sh_in,
        load_sem, core_send, core_recv, row_send, row_recv, send_sems, recv_sems,
        sh_send, sh_recv, sh_local,
    ):
        place = Place(rows_n, cols_n)
        row, col = place.row, place.col
        load = pltpu.make_async_copy(in_ref.at[place.core], mine, load_sem)
        load.start()
        shared_here = pltpu.make_async_copy(sh_ref.at[row], sh_in.at[row], sh_local)
        shared_here.start()
        place.greet(True)
        swap = remote(
            in_ref.at[1 - place.core], extra, core_send, core_recv, (row, place.other)
        )
        swap.start()

        def shared_to(step):
            goal = place.peer_row(step)
            return remote(
                sh_ref.at[goal], sh_in.at[row], sh_send.at[step], sh_recv.at[row], (goal, col)
            )

        def shared_from(step):
            source = place.peer_row(step)
            return remote(
                sh_ref.at[source], sh_in.at[source], sh_send.at[0], sh_recv.at[source],
                (source, col),
            )

        def to_row(step, chip):
            goal = place.peer_row(step)
            return remote(
                mine.at[goal, chip], rows_in.at[row, chip], row_send.at[step, chip],
                row_recv.at[row, chip], (goal, col),
            )

        def from_row(step, chip):
            source = place.peer_row(step)
            return remote(
                mine.at[source, chip], rows_in.at[source, chip], row_send.at[0, chip],
                row_recv.at[source, chip], (source, col),
            )

        load.wait()
        swap.wait_recv()
        order = []
        for i in range((chips + 1) // 2):
            order += [chips - 1 - i, i] if chips - 1 - i != i else [i]
        for chip in order:
            for step in range(1, rows_n):
                goal = place.peer_row(step)
                mine[goal, chip] = (
                    mine[goal, chip].astype(F32) + extra[goal, chip].astype(F32)
                ).astype(mine.dtype)
                to_row(step, chip).start()
        for step in range(1, rows_n):
            shared_to(step).start()

        def ready(chip):
            total = mine[row, chip].astype(F32) + extra[row, chip].astype(F32)
            for step in range(1, rows_n):
                from_row(step, chip).wait_recv()
                total = total + rows_in[place.peer_row(step), chip].astype(F32)
            mine[row, chip] = total.astype(mine.dtype)

        result, drain = line_sum_loop(
            place, mine.at[row], recv, send_sems, recv_sems, 1, ready
        )

        def store(span, value):
            out_ref[span] = value

        result(0, store)
        shared_here.wait()
        for step in range(1, rows_n):
            shared_from(step).wait_recv()
        total = sh_in[0].astype(F32)
        for other in range(1, rows_n):
            total = total + sh_in[other].astype(F32)
        sh_out[...] = total
        drain()
        swap.wait_send()
        for step in range(1, rows_n):
            shared_to(step).wait_send()
            for chip in range(chips):
                to_row(step, chip).wait_send()

    vmem = pl.BlockSpec(memory_space=pltpu.VMEM)
    return pl.pallas_call(
        kernel,
        in_specs=[ANY, ANY],
        out_specs=[vmem, vmem],
        out_shape=[
            jax.ShapeDtypeStruct(block, F32),
            jax.ShapeDtypeStruct(shared.shape[1:], F32),
        ],
        scratch_shapes=[
            pltpu.VMEM((rows_n, chips) + block, BF),
            pltpu.VMEM((rows_n, chips) + block, BF),
            pltpu.VMEM((rows_n, chips) + block, BF),
            pltpu.VMEM((chips + 1,) + block, BF),
            pltpu.VMEM(shared.shape, BF),
            pltpu.SemaphoreType.DMA,
            pltpu.SemaphoreType.DMA,
            pltpu.SemaphoreType.DMA,
            pltpu.SemaphoreType.DMA((rows_n, chips)),
            pltpu.SemaphoreType.DMA((rows_n, chips)),
            pltpu.SemaphoreType.DMA((chips, 1)),
            pltpu.SemaphoreType.DMA((chips + 1, 1)),
            pltpu.SemaphoreType.DMA((rows_n,)),
            pltpu.SemaphoreType.DMA((rows_n,)),
            pltpu.SemaphoreType.DMA,
        ],
        compiler_params=pltpu.CompilerParams(
            collective_id=collective_id, has_side_effects=True,
            vmem_limit_bytes=58 * 1024 * 1024,
        ),
        name="dense_sum",
    )(grads, shared)


def routed_kernel(
    x_ref, dy_ref, routes_ref, gates_ref, rank_ref, rank_t_ref, eg_ref, eu_ref, ed_ref,
    sgu_ref, sd_ref,
    out_hbm, gx_hbm, xs_hbm, dys_hbm, hid_ref, gg_ref, gu_ref, ggw_ref, shared_ref,
    xs, dys, pick, wide_out, wide_gx, slot_gate, slot_ggw, stage, slot_sems, stage_sems,
):
    unit = pl.program_id(0)
    units_n = pl.num_programs(0)
    total = x_ref.shape[1]
    cap = xs.shape[1] // 2
    hidden_units = sd_ref.shape[0]
    first = lax.axis_index("col") * EXP_DEV
    slots = pl.ds(unit * 2 * cap, 2 * cap)
    spans = [slice(at, at + 512) for at in range(0, x_ref.shape[2], 512)]

    def slot_copy(which):
        src, dst = ((xs, xs_hbm), (dys, dys_hbm))[which]
        return pltpu.make_async_copy(src, dst.at[:, slots], slot_sems.at[which])

    def stage_copy(which, core):
        dst = (out_hbm, gx_hbm)[which]
        return pltpu.make_async_copy(
            stage.at[which], dst.at[core, unit], stage_sems.at[which]
        )

    @pl.when(unit > 0)
    def _():
        slot_copy(0).wait()
        slot_copy(1).wait()

    for core in range(2):
        gate_rows = gates_ref[core]
        route_rows = routes_ref[core]
        for e in range(EXP_DEV):
            at = lax.broadcasted_iota(jnp.int32, (cap, total), 0)
            here = at == rank_ref[core, e : e + 1, :]
            gate_row = jnp.sum(
                jnp.where(route_rows == first + e, gate_rows, 0.0), axis=0, keepdims=True
            )
            slot_gate[e, core * cap : (core + 1) * cap, :] = jnp.sum(
                jnp.where(here, gate_row, 0.0), axis=1, keepdims=True
            )
            pick[core, e * cap : (e + 1) * cap, :] = jnp.where(here, 1.0, 0.0).astype(BF)
        for src, dst in ((x_ref, xs), (dy_ref, dys)):
            for cols in spans:
                got = mm(pick[core], src[core, :, cols]).astype(BF)
                for e in range(EXP_DEV):
                    dst[e, core * cap : (core + 1) * cap, cols] = got[e * cap : (e + 1) * cap]
    slot_copy(0).start()
    slot_copy(1).start()

    @pl.loop(0, EXP_DEV)
    def _(e):
        rows_x = xs[e]
        gate_part = mm(rows_x, eg_ref[e])
        up_part = mm(rows_x, eu_ref[e])
        act, slope = silu_parts(gate_part)
        grad_hidden = mm_nt(dys[e], ed_ref[e])
        hidden = (act * up_part).astype(BF).astype(F32)
        weight = slot_gate[e]
        gated = (hidden * weight).astype(BF)
        hid_ref[e] = gated
        slot_ggw[e] = jnp.sum(hidden * grad_hidden, axis=1, keepdims=True)
        grad_hidden = grad_hidden * weight
        geg = (grad_hidden * up_part * slope).astype(BF)
        geu = (grad_hidden * act).astype(BF)
        gg_ref[e] = geg
        gu_ref[e] = geu
        rows = pl.ds(pl.multiple_of(e * cap, cap), cap)
        for cols in spans:
            made = mm(gated, ed_ref[e, :, cols]).astype(BF)
            back = (mm_nt(geg, eg_ref[e, cols, :]) + mm_nt(geu, eu_ref[e, cols, :])).astype(BF)
            for core in range(2):
                wide_out[core, rows, cols] = made[core * cap : (core + 1) * cap]
                wide_gx[core, rows, cols] = back[core * cap : (core + 1) * cap]

    ggw_ref[...] = jnp.zeros_like(ggw_ref)
    for core in range(2):
        for e in range(EXP_DEV):
            here = pick[core, e * cap : (e + 1) * cap, :].astype(F32)
            ggw_ref[core, e : e + 1, :] = jnp.sum(
                here * slot_ggw[e, core * cap : (core + 1) * cap, :], axis=0, keepdims=True
            )
        at = lax.broadcasted_iota(jnp.int32, (total, cap), 1)
        back_pick = jnp.concatenate(
            [
                jnp.where(at == rank_t_ref[core, :, e : e + 1], 1.0, 0.0).astype(BF)
                for e in range(EXP_DEV)
            ],
            axis=1,
        )
        both = mm(x_ref[core], sgu_ref[...])
        s_act, s_slope = silu_parts(both[:, :hidden_units])
        s_up = both[:, hidden_units:]
        s_hidden = (s_act * s_up).astype(BF)
        grad_shared = mm_nt(dy_ref[core], sd_ref[...])
        grad_both = jnp.concatenate(
            [(grad_shared * s_up * s_slope).astype(BF), (grad_shared * s_act).astype(BF)],
            axis=1,
        )
        for which in range(2):
            if core == 0:

                @pl.when(unit > 0)
                def _():
                    stage_copy(which, 1).wait()

            else:
                stage_copy(which, 0).wait()
            for cols in spans:
                if which == 0:
                    value = mm(back_pick, wide_out[core, :, cols])
                    value = value + mm(s_hidden, sd_ref[:, cols])
                else:
                    value = mm(back_pick, wide_gx[core, :, cols])
                    value = value + mm_nt(grad_both, sgu_ref[cols, :])
                stage[which, :, cols] = value.astype(BF)
            stage_copy(which, core).start()
        if core == 0:

            @pl.when(unit == 0)
            def _():
                shared_ref[...] = jnp.zeros_like(shared_ref)

        for cols in spans:
            shared_ref[cols, : 2 * hidden_units] += mm_tn(x_ref[core, :, cols], grad_both)
            shared_ref[cols, 2 * hidden_units :] += mm_tn(dy_ref[core, :, cols], s_hidden)

    @pl.when(unit == units_n - 1)
    def _():
        slot_copy(0).wait()
        slot_copy(1).wait()
        stage_copy(0, 1).wait()
        stage_copy(1, 1).wait()


def routed(x_all, dy_all, routes_all, gates_all, rank, egate, eup, edown, sgu, sdown):
    cols_n, total, width = x_all.shape
    chips = cols_n // 2
    cap = 4 * total * TOP // (3 * EXP_DEV * cols_n)
    slots = 2 * cap
    ffn = egate.shape[2]
    hidden_units = sdown.shape[0]
    rank_t = jnp.swapaxes(rank, 1, 2)

    def per_unit(*shape):
        return pl.BlockSpec(shape, lambda q: (q,) + (0,) * (len(shape) - 1))

    def whole(a):
        return pl.BlockSpec(
            a.shape, lambda q: (0,) * a.ndim, pipeline_mode=pl.Buffered(1)
        )

    slot_block = pl.BlockSpec(
        (EXP_DEV, slots, ffn), lambda q: (0, q, 0), pipeline_mode=pl.Buffered(1)
    )
    small = per_unit(2, 8, total)
    return pl.pallas_call(
        routed_kernel,
        grid=(chips,),
        in_specs=[
            per_unit(2, total, width), per_unit(2, total, width), small, small, small,
            per_unit(2, total, 8), whole(egate), whole(eup), whole(edown), whole(sgu),
            whole(sdown),
        ],
        out_specs=[
            ANY, ANY, ANY, ANY, slot_block, slot_block, slot_block, small,
            pl.BlockSpec(
                (width, 3 * hidden_units), lambda q: (0, 0), pipeline_mode=pl.Buffered(1)
            ),
        ],
        out_shape=[
            jax.ShapeDtypeStruct((2, chips, total, width), BF),
            jax.ShapeDtypeStruct((2, chips, total, width), BF),
            jax.ShapeDtypeStruct((EXP_DEV, cols_n * cap, width), BF),
            jax.ShapeDtypeStruct((EXP_DEV, cols_n * cap, width), BF),
            jax.ShapeDtypeStruct((EXP_DEV, cols_n * cap, ffn), BF),
            jax.ShapeDtypeStruct((EXP_DEV, cols_n * cap, ffn), BF),
            jax.ShapeDtypeStruct((EXP_DEV, cols_n * cap, ffn), BF),
            jax.ShapeDtypeStruct((cols_n, 8, total), F32),
            jax.ShapeDtypeStruct((width, 3 * hidden_units), F32),
        ],
        scratch_shapes=[
            pltpu.VMEM((EXP_DEV, slots, width), BF),
            pltpu.VMEM((EXP_DEV, slots, width), BF),
            pltpu.VMEM((2, EXP_DEV * cap, total), BF),
            pltpu.VMEM((2, EXP_DEV * cap, width), BF),
            pltpu.VMEM((2, EXP_DEV * cap, width), BF),
            pltpu.VMEM((EXP_DEV, slots, 1), F32),
            pltpu.VMEM((EXP_DEV, slots, 1), F32),
            pltpu.VMEM((2, total, width), BF),
            pltpu.SemaphoreType.DMA((2,)),
            pltpu.SemaphoreType.DMA((2,)),
        ],
        compiler_params=pltpu.CompilerParams(vmem_limit_bytes=60 * 1024 * 1024),
        name="routed",
    )(x_all, dy_all, routes_all, gates_all, rank, rank_t, egate, eup, edown, sgu, sdown)


def expert_grads_kernel(xs_ref, dys_ref, hid_ref, gg_ref, gu_ref, og_ref, ou_ref, od_ref):
    rows = xs_ref[0]
    og_ref[0] = mm_tn(rows, gg_ref[0]).astype(BF)
    ou_ref[0] = mm_tn(rows, gu_ref[0]).astype(BF)
    od_ref[0] = mm_tn(hid_ref[0], dys_ref[0]).astype(BF)


def expert_grads(xs, dys, hid, gg, gu):
    _, slots, width = xs.shape
    ffn = hid.shape[2]

    def each(rows, cols):
        return pl.BlockSpec((1, rows, cols), lambda e: (e, 0, 0))

    return pl.pallas_call(
        expert_grads_kernel,
        grid=(EXP_DEV,),
        in_specs=[each(slots, width)] * 2 + [each(slots, ffn)] * 3,
        out_specs=[each(width, ffn), each(width, ffn), each(ffn, width)],
        out_shape=[
            jax.ShapeDtypeStruct((EXP_DEV, width, ffn), BF),
            jax.ShapeDtypeStruct((EXP_DEV, width, ffn), BF),
            jax.ShapeDtypeStruct((EXP_DEV, ffn, width), BF),
        ],
        compiler_params=pltpu.CompilerParams(vmem_limit_bytes=60 * 1024 * 1024),
        name="expert_grads",
    )(xs, dys, hid, gg, gu)


def on_device(
    tokens,
    g_attn,
    w_query,
    key_projection,
    value_projection,
    w_out,
    g_moe,
    w_router,
    e_gate,
    e_up,
    e_down,
    s_gate,
    s_up,
    s_down,
    routes,
    deal,
    lengths,
    cotangent,
):
    rows_n = lax.axis_size("row")
    cols_n = lax.axis_size("col")
    row_here = lax.axis_index("row")
    col_here = lax.axis_index("col")
    both = ("row", "col")
    total = tokens.shape[0]
    width = MODEL_WIDTH
    experts = EXP_DEV * cols_n

    q_w, k_w = w_query.shape[1], key_projection.shape[1]
    inner = w_query.shape[0]
    gains = jnp.stack([g_attn, g_moe])
    gains = jnp.pad(gains, ((0, 0), (0, inner - gains.shape[1])))
    tail = jnp.concatenate([w_router.T, gains], axis=0)
    tail = jnp.pad(tail, ((0, 16 - tail.shape[0]), (0, 0)))
    bundle = jnp.concatenate(
        [w_query.T, key_projection.T, value_projection.T, w_out.T, tail], axis=0
    )
    routes_t = jnp.pad(routes.T, ((0, 8 - TOP), (0, 0)), constant_values=-1)
    units = s_gate.shape[1]
    shared = jnp.concatenate([s_gate, s_up], axis=1)
    full, dy_all, routes_all, sgu = first_gather(
        bundle, cotangent, routes_t, shared, 0, rows_n, cols_n
    )
    sgu = sgu.reshape(width, 2 * units)

    def piece(lo, extent):
        part = full[:, :, lo : lo + extent]
        return part.transpose(1, 2, 0, 3).reshape(cols_n * extent, width)

    wq_t = piece(0, q_w)
    wk_t = piece(q_w, k_w)
    wv_t = piece(q_w + k_w, k_w)
    wo_t = piece(q_w + 2 * k_w, q_w)
    t_at = 2 * q_w + 2 * k_w
    router_t = piece(t_at, EXP_DEV)
    n_gain = g_attn.shape[0]
    gain_attn = full[:, :, t_at + EXP_DEV, :n_gain].reshape(width).astype(F32)
    gain_moe = full[:, :, t_at + EXP_DEV + 1, :n_gain].reshape(width).astype(F32)
    egate = lax.all_gather(e_gate, "row", axis=1, tiled=True)
    eup = lax.all_gather(e_up, "row", axis=1, tiled=True)
    edown = lax.all_gather(e_down, "row", axis=2, tiled=True)
    per_row = s_down.shape[0] // units
    sdown_cols = lax.all_gather(s_down, "col", axis=1, tiled=True)
    sdown_mine = lax.dynamic_slice_in_dim(sdown_cols, (col_here % per_row) * units, units, 0)
    sdown = lax.dynamic_index_in_dim(
        lax.all_gather(sdown_mine, "row", axis=0), col_here // per_row, 0, keepdims=False
    )

    mine = col_here * EXP_DEV + jnp.arange(EXP_DEV, dtype=jnp.int32)
    hit = jnp.any(routes_all[:, None, :TOP, :] == mine[None, :, None, None], axis=2)
    rank = jnp.where(hit, jnp.cumsum(hit.astype(jnp.int32), axis=2) - 1, -1)
    rank = jnp.pad(rank, ((0, 0), (0, 8 - EXP_DEV), (0, 0)), constant_values=-1)

    own_lens = lengths[deal.reshape(-1) * cols_n + col_here, row_here]
    seq_ends = jnp.cumsum(own_lens)
    places = jnp.arange(total, dtype=jnp.int32)
    segment = jnp.sum((places[:, None] >= seq_ends[None, :]).astype(jnp.int32), axis=1)

    tokens_f = tokens.astype(F32)
    scale_one = rms_scale(tokens_f)
    unit_one = tokens_f * scale_one
    normed_one = (unit_one * gain_attn).astype(BF)
    queries = mm_nt(normed_one, wq_t).astype(BF)
    keys = mm_nt(normed_one, wk_t).astype(BF)
    values = mm_nt(normed_one, wv_t).astype(BF)
    mixed, log_totals = attend_forward(queries, keys, values, segment)
    after_attn = tokens_f + mm_nt(mixed, wo_t)
    scale_two = rms_scale(after_attn)
    unit_two = after_attn * scale_two
    normed_two = (unit_two * gain_moe).astype(BF)
    logits = mm_nt(normed_two, router_t)
    route_picks = (
        routes[:, :, None] == jnp.arange(experts, dtype=jnp.int32)[None, None, :]
    ).astype(F32)
    chosen = jnp.sum(route_picks * logits[:, None, :], axis=-1)
    gate_raw = jnp.exp(chosen - jnp.max(chosen, axis=-1, keepdims=True))
    gate_weights = gate_raw / jnp.sum(gate_raw, axis=-1, keepdims=True)

    gates_t = jnp.pad(gate_weights.T, ((0, 8 - TOP), (0, 0)))
    x_all, gates_all = line_gather([normed_two, gates_t], 1, rows_n, cols_n)
    out_part, gx_part, xs, dys, hid, gg, gu, ggw, grad_sh = routed(
        x_all, dy_all, routes_all, gates_all, rank, egate, eup, edown, sgu, sdown
    )
    grad_egate, grad_eup, grad_edown = expert_grads(xs, dys, hid, gg, gu)
    ggw = ggw[:, :EXP_DEV]

    gx = line_sum(gx_part, 2, rows_n, cols_n)
    ggw_home = lax.all_to_all(ggw, "col", split_axis=0, concat_axis=0, tiled=True)
    ggw_home = ggw_home.reshape(experts, total).T

    grad_gates = jnp.sum(route_picks * ggw_home[:, None, :], axis=-1)
    grad_chosen = gate_weights * (
        grad_gates - jnp.sum(gate_weights * grad_gates, axis=-1, keepdims=True)
    )
    grad_logits = jnp.sum(route_picks * grad_chosen[:, :, None], axis=1).astype(BF)
    grad_router = mm_tn(grad_logits, normed_two)
    grad_normed_two = gx + mm(grad_logits, router_t)
    grad_two, grad_gain_moe = norm_back(grad_normed_two, unit_two, scale_two, gain_moe)
    grad_after = cotangent.astype(F32) + grad_two
    grad_attn_b = grad_after.astype(BF)
    grad_wout = mm_tn(grad_attn_b, mixed)
    grad_mixed = mm(grad_attn_b, wo_t).astype(BF)
    gq, gk, gv = attend_backward(queries, keys, values, grad_mixed, segment, log_totals)
    grad_wq = mm_tn(gq, normed_one)
    grad_wk = mm_tn(gk, normed_one)
    grad_wv = mm_tn(gv, normed_one)
    grad_normed_one = mm(gq, wq_t) + mm(gk, wk_t) + mm(gv, wv_t)
    grad_one, grad_gain_attn = norm_back(grad_normed_one, unit_one, scale_one, gain_attn)
    grad_tokens = grad_after + grad_one

    moe = line_sum(out_part, 3, rows_n, cols_n)
    output = (after_attn + moe).astype(BF)

    def cut(grad):
        extent = grad.shape[0] // cols_n
        part = grad.astype(BF).reshape(cols_n // 2, 2, extent, rows_n, inner)
        return part.transpose(1, 3, 0, 2, 4)

    def cut_gain(grad):
        part = grad.astype(BF).reshape(rows_n, cols_n // 2, 2, 1, n_gain)
        part = jnp.pad(part, ((0, 0),) * 4 + ((0, inner - n_gain),))
        return part.transpose(2, 0, 1, 3, 4)

    grads = [cut(grad_wq), cut(grad_wk), cut(grad_wv), cut(grad_wout), cut(grad_router)]
    grads += [cut_gain(grad_gain_attn), cut_gain(grad_gain_moe)]
    blank = 16 - EXP_DEV - 2
    grads.append(jnp.zeros((2, rows_n, cols_n // 2, blank, inner), BF))
    grads = jnp.concatenate(grads, axis=3)
    grads_sh = grad_sh.astype(BF).reshape(rows_n, inner, 3 * units)
    dense, dense_sh = dense_sum(grads, grads_sh, 4, rows_n, cols_n)
    out_wq = dense[:q_w].T
    out_wk = dense[q_w : q_w + k_w].T
    out_wv = dense[q_w + k_w : q_w + 2 * k_w].T
    out_wo = dense[q_w + 2 * k_w : t_at].T
    out_router = dense[t_at : t_at + EXP_DEV].T
    out_g_attn = dense[t_at + EXP_DEV, :n_gain]
    out_g_moe = dense[t_at + EXP_DEV + 1, :n_gain]
    out_sg = dense_sh[:, :units]
    out_su = dense_sh[:, units : 2 * units]
    sd_rows = dense_sh[:, 2 * units :].astype(BF).reshape(per_row, inner // per_row, units)
    lands = []
    for turn in range(per_row):
        moves = [
            (rr * cols_n + cc, (cc // per_row) * cols_n + per_row * rr + (cc + turn) % per_row)
            for rr in range(rows_n)
            for cc in range(cols_n)
        ]
        part = lax.dynamic_index_in_dim(sd_rows, (col_here + turn) % per_row, 0, keepdims=False)
        lands.append(lax.ppermute(part, ("row", "col"), moves))
    lands = jnp.stack(lands)
    turns = (col_here - jnp.arange(per_row, dtype=jnp.int32)) % per_row
    out_sd = jnp.take(lands, turns, axis=0).transpose(0, 2, 1)
    out_sd = out_sd.reshape(per_row * units, inner // per_row).astype(F32)

    def row_sum(grad, dim):
        return lax.psum_scatter(
            grad.astype(BF), "row", scatter_dimension=dim, tiled=True
        ).astype(F32)

    out_eg = row_sum(grad_egate, 1)
    out_eu = row_sum(grad_eup, 1)
    out_ed = row_sum(grad_edown, 2)
    return (
        output,
        grad_tokens,
        out_g_attn,
        out_wq,
        out_wk,
        out_wv,
        out_wo,
        out_g_moe,
        out_router,
        out_eg,
        out_eu,
        out_ed,
        out_sg,
        out_su,
        out_sd,
    )


def solution(mesh):
    both = P(("row", "col"), None)
    flat = P(("row", "col"))
    tile = P("row", "col")
    wide = P("col", "row", None)
    down = P("col", None, "row")
    return jax.shard_map(
        on_device,
        mesh=mesh,
        in_specs=(
            both, flat, tile, tile, tile, tile, flat, tile, wide, wide, down,
            tile, tile, tile, both, both, P(), both,
        ),
        out_specs=(
            both, both, flat, tile, tile, tile, tile, flat, tile, wide, wide, down,
            tile, tile, tile,
        ),
        check_vma=False,
    )
```

```python
import functools

import jax
import jax.numpy as jnp
from jax import lax
from jax.experimental import pallas as pl
from jax.experimental.pallas import tpu as pltpu
from jax.sharding import PartitionSpec as P

MODEL_WIDTH = 1536
QUERY_HEADS = 12
KEY_VALUE_HEADS = 4
GROUP = QUERY_HEADS // KEY_VALUE_HEADS
HEAD_SIZE = 128
TOP = 6
EXP_DEV = 4

norm_eps = 1e-05
masked_score = -1e30
BF = jnp.bfloat16
F32 = jnp.float32


def rms_scale(rows):
    return lax.rsqrt(jnp.mean(rows * rows, axis=-1, keepdims=True) + norm_eps)


def silu_parts(values):
    sigmoid_of = jax.nn.sigmoid(values)
    return (values * sigmoid_of, sigmoid_of * (1.0 + values * (1.0 - sigmoid_of)))


def norm_back(grad_normed, unit_rows, scale_rows, gain):
    grad_unit = grad_normed * gain
    grad_rows = scale_rows * (
        grad_unit - unit_rows * jnp.mean(grad_unit * unit_rows, axis=-1, keepdims=True)
    )
    return (grad_rows, jnp.sum(grad_normed * unit_rows, axis=0))


def mm(left, right):
    return jnp.dot(left, right, preferred_element_type=F32)


def mm_nt(left, right):
    return lax.dot_general(left, right, (((1,), (1,)), ((), ())), preferred_element_type=F32)


def mm_tn(left, right):
    return lax.dot_general(left, right, (((0,), (0,)), ((), ())), preferred_element_type=F32)


def ein(spec, a, b):
    return jnp.einsum(spec, a, b, preferred_element_type=F32)


def allowed_mask(seg_col, seg_row):
    total = seg_col.shape[0]
    q_at = lax.broadcasted_iota(jnp.int32, (total, total), 0)
    k_at = lax.broadcasted_iota(jnp.int32, (total, total), 1)
    return (seg_col == seg_row) & (k_at <= q_at)


def attend_forward_kernel(q_ref, k_ref, v_ref, segc_ref, segr_ref, mixed_ref, lse_ref):
    allowed = allowed_mask(segc_ref[...], segr_ref[...])
    keys = k_ref[...]
    values = v_ref[...]
    for g in range(GROUP):
        cols = slice(g * HEAD_SIZE, (g + 1) * HEAD_SIZE)
        scores = mm_nt(q_ref[:, cols], keys) * HEAD_SIZE ** (-0.5)
        scores = jnp.where(allowed, scores, masked_score)
        peak = jnp.max(scores, axis=-1, keepdims=True)
        raw = jnp.exp(scores - peak)
        total = jnp.sum(raw, axis=-1, keepdims=True)
        probs = (raw * (1.0 / total)).astype(BF)
        mixed_ref[:, cols] = mm(probs, values).astype(BF)
        lse_ref[0, :, g : g + 1] = peak + jnp.log(total)


def attend_backward_kernel(
    q_ref, k_ref, v_ref, gm_ref, segc_ref, segr_ref, lse_ref, gq_ref, gk_ref, gv_ref
):
    allowed = allowed_mask(segc_ref[...], segr_ref[...])
    keys = k_ref[...]
    values = v_ref[...]
    scale = HEAD_SIZE ** (-0.5)
    grad_key = None
    for g in range(GROUP):
        cols = slice(g * HEAD_SIZE, (g + 1) * HEAD_SIZE)
        query = q_ref[:, cols]
        grad_mixed = gm_ref[:, cols]
        scores = mm_nt(query, keys) * scale
        probs = jnp.where(allowed, jnp.exp(scores - lse_ref[0, :, g : g + 1]), 0.0)
        grad_probs = mm_nt(grad_mixed, values)
        inner = jnp.sum(probs * grad_probs, axis=-1, keepdims=True)
        grad_scores = (probs * (grad_probs - inner)).astype(BF)
        gq_ref[:, cols] = (mm(grad_scores, keys) * scale).astype(BF)
        part_key = mm_tn(grad_scores, query)
        part_value = mm_tn(probs.astype(BF), grad_mixed)
        if grad_key is None:
            grad_key, grad_value = part_key, part_value
        else:
            grad_key, grad_value = grad_key + part_key, grad_value + part_value
    gk_ref[...] = (grad_key * scale).astype(BF)
    gv_ref[...] = grad_value.astype(BF)


def attention_specs(total):
    wide = pl.BlockSpec((total, GROUP * HEAD_SIZE), lambda h: (0, h))
    narrow = pl.BlockSpec((total, HEAD_SIZE), lambda h: (0, h))
    seg_col = pl.BlockSpec((total, 1), lambda h: (0, 0))
    seg_row = pl.BlockSpec((1, total), lambda h: (0, 0))
    lse = pl.BlockSpec((1, total, GROUP), lambda h: (h, 0, 0))
    return wide, narrow, seg_col, seg_row, lse


def attend_forward(queries, keys, values, segment):
    total = queries.shape[0]
    wide, narrow, seg_col, seg_row, lse = attention_specs(total)
    return pl.pallas_call(
        attend_forward_kernel,
        grid=(KEY_VALUE_HEADS,),
        in_specs=[wide, narrow, narrow, seg_col, seg_row],
        out_specs=[wide, lse],
        out_shape=[
            jax.ShapeDtypeStruct(queries.shape, BF),
            jax.ShapeDtypeStruct((KEY_VALUE_HEADS, total, GROUP), F32),
        ],
        compiler_params=pltpu.CompilerParams(vmem_limit_bytes=48 * 1024 * 1024),
        name="attend_forward",
    )(queries, keys, values, segment[:, None], segment[None, :])


def attend_backward(queries, keys, values, grad_mixed, segment, log_totals):
    total = queries.shape[0]
    wide, narrow, seg_col, seg_row, lse = attention_specs(total)
    return pl.pallas_call(
        attend_backward_kernel,
        grid=(KEY_VALUE_HEADS,),
        in_specs=[wide, narrow, narrow, wide, seg_col, seg_row, lse],
        out_specs=[wide, narrow, narrow],
        out_shape=[
            jax.ShapeDtypeStruct(queries.shape, BF),
            jax.ShapeDtypeStruct(keys.shape, BF),
            jax.ShapeDtypeStruct(keys.shape, BF),
        ],
        compiler_params=pltpu.CompilerParams(vmem_limit_bytes=48 * 1024 * 1024),
        name="attend_backward",
    )(queries, keys, values, grad_mixed, segment[:, None], segment[None, :], log_totals)


def remote(src, dst, send_sem, recv_sem, device):
    return pltpu.make_async_remote_copy(
        src_ref=src,
        dst_ref=dst,
        send_sem=send_sem,
        recv_sem=recv_sem,
        device_id=device,
        device_id_type=pl.DeviceIdType.MESH,
    )


class Place:
    def __init__(self, rows_n, cols_n):
        self.rows_n = rows_n
        self.chips = cols_n // 2
        self.row = lax.axis_index("row")
        self.col = lax.axis_index("col")
        self.chip = lax.div(self.col, 2)
        self.core = lax.rem(self.col, 2)
        self.other = self.col + 1 - 2 * self.core

    def peer_row(self, step):
        return lax.rem(self.row + step, self.rows_n)

    def greet(self, with_rows, per_row=0, downs_back=0):
        barrier = pltpu.get_barrier_semaphore()

        def hello(row, col):
            pl.semaphore_signal(
                barrier, inc=1, device_id=(row, col), device_id_type=pl.DeviceIdType.MESH
            )

        hello(self.row, self.other)

        @pl.when(self.chip > 0)
        def _():
            hello(self.row, self.col - 2)

        @pl.when(self.chip < self.chips - 1)
        def _():
            hello(self.row, self.col + 2)

        count = (
            1
            + (self.chip > 0).astype(jnp.int32)
            + (self.chip < self.chips - 1).astype(jnp.int32)
        )
        if with_rows:
            for step in range(1, self.rows_n):
                hello(self.peer_row(step), self.col)
            count = count + (self.rows_n - 1)
        if per_row:
            source = lax.div(self.col, per_row)
            for col in range(2 * self.chips):

                @pl.when(jnp.logical_not((source == self.row) & (self.col == col)))
                def _():
                    hello(source, jnp.int32(col))

            count = count + self.rows_n * per_row - (source == self.row).astype(jnp.int32)
        if downs_back:
            goal = lax.div(self.col, downs_back)
            for turn in range(downs_back):
                goal_col = downs_back * self.row + turn

                @pl.when(jnp.logical_not((goal == self.row) & (goal_col == self.col)))
                def _():
                    hello(goal, goal_col)

            count = count + downs_back - (goal == self.row).astype(jnp.int32)
        pl.semaphore_wait(barrier, count)


class Moves:
    def __init__(self, place, up, down, from_below, from_above, send_sems, recv_sems):
        self.place = place
        self.copies = [
            remote(
                src, dst, send_sems.at[which], recv_sems.at[which],
                (place.row, place.col + way),
            )
            for which, (src, dst, way) in enumerate(
                ((up, from_below, 2), (down, from_above, -2))
            )
        ]
        self.ends = (place.chip < place.chips - 1, place.chip > 0)

    def start(self):
        for which in range(2):

            @pl.when(self.ends[which])
            def _():
                self.copies[which].start()

    def wait_send(self):
        for which in range(2):

            @pl.when(self.ends[which])
            def _():
                self.copies[which].wait_send()

    def wait_recv(self):
        for which in range(2):

            @pl.when(self.ends[1 - which])
            def _():
                self.copies[which].wait_recv()


class LineGather:
    def __init__(self, place, src, dst, core_sems, line_sems, recv_sems, local_sem):
        self.at = place
        self.src, self.dst = src, dst
        self.core_sems, self.line_sems, self.recv_sems = core_sems, line_sems, recv_sems
        self.local = pltpu.make_async_copy(src, dst.at[place.col], local_sem)

    def to_core(self, block, src=None):
        at = self.at
        src = self.dst.at[block] if src is None else src
        return remote(
            src, self.dst.at[block], self.core_sems.at[block], self.recv_sems.at[block],
            (at.row, at.other),
        )

    def to_line(self, block, way, src=None):
        at = self.at
        src = self.dst.at[block] if src is None else src
        return remote(
            src,
            self.dst.at[block],
            self.line_sems.at[block, (way + 1) // 2],
            self.recv_sems.at[block],
            (at.row, at.col + 2 * way),
        )

    def ends(self, way):
        return self.at.chip < self.at.chips - 1 if way > 0 else self.at.chip > 0

    def start(self):
        self.local.start()
        for way in (1, -1):

            @pl.when(self.ends(way))
            def _():
                self.to_line(self.at.col, way, self.src).start()

        self.to_core(self.at.col, self.src).start()

    def arrivals(self, dist, act):
        for way in (1, -1):
            chip = self.at.chip - way * dist
            near = chip >= 0 if way > 0 else chip < self.at.chips

            @pl.when(near)
            def _():
                act(2 * chip + self.at.core, way)

    def step(self, dist, extra=None):
        def act(block, way):
            self.to_core(block).wait_recv()

            @pl.when(self.ends(way))
            def _():
                self.to_line(block, way).start()

            self.to_core(block).start()
            if extra is not None:
                extra(block)

        self.arrivals(dist, act)

    def finish(self):
        self.local.wait()
        self.to_core(self.at.col, self.src).wait_send()
        for way in (1, -1):

            @pl.when(self.ends(way))
            def _():
                self.to_line(self.at.col, way, self.src).wait_send()

        def act(block, way):
            self.to_core(block).wait_send()

            @pl.when(self.ends(way))
            def _():
                self.to_line(block, way).wait_send()

        for dist in range(1, self.at.chips):
            self.arrivals(dist, act)
        for chip in range(self.at.chips):
            self.to_core(2 * chip + 1 - self.at.core).wait_recv()


def gather_sems(cols_n):
    return [
        pltpu.SemaphoreType.DMA((cols_n,)),
        pltpu.SemaphoreType.DMA((cols_n, 2)),
        pltpu.SemaphoreType.DMA((cols_n,)),
        pltpu.SemaphoreType.DMA,
    ]


ANY = pl.BlockSpec(memory_space=pl.ANY)


def line_gather(arrays, collective_id, rows_n, cols_n):
    n = len(arrays)

    def kernel(*refs):
        srcs, dsts, sems = refs[:n], refs[n : 2 * n], refs[2 * n :]
        place = Place(rows_n, cols_n)
        place.greet(False)
        jobs = [
            LineGather(place, srcs[i], dsts[i], *sems[4 * i : 4 * i + 4]) for i in range(n)
        ]
        for job in jobs:
            job.start()
        for dist in range(1, place.chips):
            for job in jobs:
                job.step(dist)
        for job in jobs:
            job.finish()

    return pl.pallas_call(
        kernel,
        in_specs=[ANY] * n,
        out_specs=[ANY] * n,
        out_shape=[jax.ShapeDtypeStruct((cols_n,) + a.shape, a.dtype) for a in arrays],
        scratch_shapes=gather_sems(cols_n) * n,
        compiler_params=pltpu.CompilerParams(collective_id=collective_id, has_side_effects=True),
        name="line_gather",
    )(*arrays)


def first_gather(bundle, cotangent, routes_t, shared, downs, collective_id, rows_n, cols_n):
    per_row = downs.shape[0]

    def kernel(
        bundle_ref, dy_ref, rt_ref, sh_ref, sd_ref,
        full_ref, dy_all, rt_all, sh_all, sd_all, *sems
    ):
        place = Place(rows_n, cols_n)
        b_sems, sems = sems[:4], sems[4:]
        d_sems, sems = sems[:4], sems[4:]
        r_sems, sems = sems[:4], sems[4:]
        row_send, row_core, row_recv, sh_send, sh_recv, sh_local, sd_send, sd_recv = sems
        place.greet(True, per_row)
        row, col = place.row, place.col
        weights = LineGather(place, bundle_ref, full_ref.at[row], *b_sems)
        grads = LineGather(place, dy_ref, dy_all, *d_sems)
        picks = LineGather(place, rt_ref, rt_all, *r_sems)

        def to_row(block, step, src=None):
            home = full_ref.at[row, block]
            return remote(
                home if src is None else src, home, row_send.at[block, step],
                row_recv.at[row, block], (place.peer_row(step), col),
            )

        def push(block, src=None):
            for step in range(1, rows_n):
                to_row(block, step, src).start()

        def from_row(other_row, block):
            home = full_ref.at[other_row, block]
            return remote(
                home, home, row_core.at[other_row, block], row_recv.at[other_row, block],
                (row, place.other),
            )

        def shared_to(step):
            return remote(
                sh_ref, sh_all.at[row], sh_send.at[step], sh_recv.at[row],
                (place.peer_row(step), col),
            )

        down_row = lax.div(col, per_row)

        def downs_to(act_far, act_here):
            for step in range(rows_n):
                for turn in range(per_row):
                    goal_row, goal_col = place.peer_row(step), per_row * row + turn
                    here = (goal_col == col) if step == 0 else None
                    far = remote(
                        sd_ref.at[turn], sd_all.at[col], sd_send.at[step, turn],
                        sd_recv.at[col], (goal_row, goal_col),
                    )
                    if here is None:
                        act_far(far)
                        continue

                    @pl.when(here)
                    def _():
                        act_here(
                            pltpu.make_async_copy(
                                sd_ref.at[turn], sd_all.at[col], sd_recv.at[col]
                            )
                        )

                    @pl.when(jnp.logical_not(here))
                    def _():
                        act_far(far)

        weights.start()
        push(col, bundle_ref)
        shared_here = pltpu.make_async_copy(sh_ref, sh_all.at[row], sh_local)
        shared_here.start()
        for step in range(1, rows_n):
            shared_to(step).start()
        for dist in range(1, place.chips):
            weights.step(dist, push)
        downs_to(lambda far: far.start(), lambda here: here.start())
        grads.start()
        picks.start()
        for dist in range(1, place.chips - 1):
            grads.step(dist)
            picks.step(dist)
        for step in range(1, rows_n):
            other_row = place.peer_row(step)

            @pl.loop(0, place.chips)
            def _(chip):
                copy = from_row(other_row, 2 * chip + place.core)
                copy.wait_recv()
                copy.start()

        grads.step(place.chips - 1)
        picks.step(place.chips - 1)
        weights.finish()
        grads.finish()
        picks.finish()
        shared_here.wait()
        downs_to(lambda far: far.wait_send(), lambda here: here.wait())

        @pl.loop(0, cols_n)
        def _(source):
            @pl.when(jnp.logical_not((source == col) & (down_row == row)))
            def _():
                remote(
                    sd_ref.at[0], sd_all.at[source], sd_send.at[0, 0], sd_recv.at[source],
                    (row, place.other),
                ).wait_recv()

        for step in range(1, rows_n):
            other_row = place.peer_row(step)
            shared_to(step).wait_send()
            remote(
                sh_ref, sh_all.at[other_row], sh_send.at[0], sh_recv.at[other_row],
                (other_row, col),
            ).wait_recv()

            @pl.loop(0, place.chips)
            def _(chip):
                to_row(2 * chip + place.core, step).wait_send()
                from_row(other_row, 2 * chip + place.core).wait_send()
                from_row(other_row, 2 * chip + 1 - place.core).wait_recv()

    return pl.pallas_call(
        kernel,
        in_specs=[ANY] * 5,
        out_specs=[ANY] * 5,
        out_shape=[
            jax.ShapeDtypeStruct((rows_n, cols_n) + bundle.shape, bundle.dtype),
            jax.ShapeDtypeStruct((cols_n,) + cotangent.shape, cotangent.dtype),
            jax.ShapeDtypeStruct((cols_n,) + routes_t.shape, routes_t.dtype),
            jax.ShapeDtypeStruct((rows_n,) + shared.shape, shared.dtype),
            jax.ShapeDtypeStruct((cols_n,) + downs.shape[1:], downs.dtype),
        ],
        scratch_shapes=gather_sems(cols_n) * 3
        + [
            pltpu.SemaphoreType.DMA((cols_n, rows_n)),
            pltpu.SemaphoreType.DMA((rows_n, cols_n)),
            pltpu.SemaphoreType.DMA((rows_n, cols_n)),
            pltpu.SemaphoreType.DMA((rows_n,)),
            pltpu.SemaphoreType.DMA((rows_n,)),
            pltpu.SemaphoreType.DMA,
            pltpu.SemaphoreType.DMA((rows_n, per_row)),
            pltpu.SemaphoreType.DMA((cols_n,)),
        ],
        compiler_params=pltpu.CompilerParams(collective_id=collective_id, has_side_effects=True),
        name="first_gather",
    )(bundle, cotangent, routes_t, shared, downs)


def line_sum_loop(place, mine, recv, send_sems, recv_sems, parts, ready):
    chips, here = place.chips, place.chip
    rows = mine.shape[1] // parts
    items = (chips - 1) * parts

    def copy(chip, part, way):
        span = pl.ds(part * rows, rows)
        goal = here + way
        land = chip if way > 0 else jnp.where(chip == goal, chips, chip)
        return remote(
            mine.at[chip, span],
            recv.at[land, span],
            send_sems.at[chip, part],
            recv_sems.at[land, part],
            (place.row, place.col + 2 * way),
        )

    def incoming(land, part):
        span = pl.ds(part * rows, rows)
        return remote(
            mine.at[0, span], recv.at[land, span], send_sems.at[0, part],
            recv_sems.at[land, part], (place.row, place.other),
        )

    def handle(chip, part, way):
        @pl.when(part == 0)
        def _():
            ready(chip)

        span = pl.ds(part * rows, rows)
        comes = here > 0 if way > 0 else here < chips - 1

        @pl.when(comes)
        def _():
            incoming(chip, part).wait_recv()
            total = mine[chip, span].astype(F32) + recv[chip, span].astype(F32)
            mine[chip, span] = total.astype(mine.dtype)

        copy(chip, part, way).start()

    lag = 2 * (chips - 2 - here)

    @pl.loop(0, items + 2 * (chips - 2))
    def _(at):
        up = jnp.minimum(at, items - 1)
        up_chip = chips - 1 - lax.div(up, parts)

        @pl.when((at < items) & (up_chip > here))
        def _():
            handle(up_chip, lax.rem(up, parts), 1)

        down = at - jnp.maximum(lag, 0)
        safe = jnp.clip(down, 0, items - 1)
        down_chip = lax.div(safe, parts)

        @pl.when((down >= 0) & (down < items) & (down_chip < here))
        def _():
            handle(down_chip, lax.rem(safe, parts), -1)

    ready(here)

    def result(part, store):
        span = pl.ds(part * rows, rows)
        total = mine[here, span].astype(F32)

        @pl.when((here > 0) & (here < chips - 1))
        def _():
            incoming(here, part).wait_recv()
            incoming(chips, part).wait_recv()
            store(span, total + recv[here, span].astype(F32) + recv[chips, span].astype(F32))

        @pl.when((here > 0) & (here == chips - 1))
        def _():
            incoming(here, part).wait_recv()
            store(span, total + recv[here, span].astype(F32))

        @pl.when((here == 0) & (here < chips - 1))
        def _():
            incoming(chips, part).wait_recv()
            store(span, total + recv[chips, span].astype(F32))

    def drain():
        @pl.loop(0, chips)
        def _(chip):
            for part in range(parts):

                @pl.when(chip > here)
                def _():
                    copy(chip, part, 1).wait_send()

                @pl.when(chip < here)
                def _():
                    copy(chip, part, -1).wait_send()

    return result, drain


def dense_sum(lefts, rights, tails, shared, rounds, collective_id, rows_n, cols_n):
    n_rounds = len(rounds)
    moved = rounds[0][0]
    chips = cols_n // 2
    inner = shared.shape[1]
    units = shared.shape[2] // 3
    per_row = cols_n // rows_n
    extents = [left.shape[1] // cols_n for left in lefts]
    block = (sum(extents), inner)
    n = len(lefts)

    def kernel(*refs):
        left_refs, right_refs = refs[:n], refs[n : 2 * n]
        (
            tail_ref, sh_ref, *round_refs
        ) = refs[2 * n : 2 * n + 2 + 2 * n_rounds]
        (
            out_ref, sh_out, sd_out, arrivals,
            both, extra, rows_in, recv, sh_in, sd_cut, held, came, held_sems, came_sems,
            core_send, core_recv, row_send, row_recv, send_sems, recv_sems,
            sh_send, sh_recv, sh_local, move_send, move_recv, sd_send, sd_recv,
        ) = refs[2 * n + 2 + 2 * n_rounds :]
        place = Place(rows_n, cols_n)
        row, col = place.row, place.col
        mine = both.at[place.core]
        shared_here = pltpu.make_async_copy(sh_ref.at[row], sh_in.at[row], sh_local)
        shared_here.start()
        down_row = lax.div(col, per_row)
        place.greet(True, downs_back=per_row)

        def moves(turn):
            pair = round_refs[:2] if turn == 0 else (held.at[0], held.at[1])
            return Moves(
                place, *pair, arrivals.at[turn, 0], arrivals.at[turn, 1], move_send.at[turn],
                move_recv.at[turn],
            )

        def hold(turn):
            return [
                pltpu.make_async_copy(
                    round_refs[2 * turn + which], held.at[which], held_sems.at[which]
                )
                for which in range(2)
            ]

        def next_round(turn):
            moves(turn - 1).wait_send()
            copies = hold(turn)
            for copy in copies:
                copy.start()
            moves(turn - 1).wait_recv()
            for which, comes in ((0, place.chip > 0), (1, place.chip < chips - 1)):
                bring = pltpu.make_async_copy(
                    arrivals.at[turn - 1, which], came.at[which], came_sems.at[which]
                )

                @pl.when(comes)
                def _():
                    bring.start()

                copies[which].wait()

                @pl.when(comes)
                def _():
                    bring.wait()
                    part = came.shape[1] // 4
                    for at in range(0, came.shape[1], part):
                        span = slice(at, at + part)
                        held[which, span] = (
                            held[which, span].astype(F32) + came[which, span].astype(F32)
                        ).astype(BF)

            moves(turn).start()

        moves(0).start()

        def downs_to(turn, act_far, act_here):
            goal_col = per_row * row + turn
            here = (goal_col == col) & (down_row == row)
            source = lax.rem(col, per_row)

            @pl.when(here)
            def _():
                act_here(
                    pltpu.make_async_copy(
                        sd_cut.at[turn], sd_out.at[source], sd_recv.at[source]
                    )
                )

            @pl.when(jnp.logical_not(here))
            def _():
                act_far(
                    remote(
                        sd_cut.at[turn], sd_out.at[source], sd_send.at[turn],
                        sd_recv.at[source], (down_row, goal_col),
                    )
                )

        def swap(goal):
            return remote(
                both.at[1 - place.core, goal], extra.at[goal], core_send.at[goal],
                core_recv.at[goal], (row, place.other),
            )

        def shared_to(step):
            goal = place.peer_row(step)
            return remote(
                sh_ref.at[goal], sh_in.at[row], sh_send.at[step], sh_recv.at[row], (goal, col)
            )

        def shared_from(step):
            source = place.peer_row(step)
            return remote(
                sh_ref.at[source], sh_in.at[source], sh_send.at[0], sh_recv.at[source],
                (source, col),
            )

        def to_row(goal, chip):
            return remote(
                mine.at[goal, chip], rows_in.at[row, chip], row_send.at[goal, chip],
                row_recv.at[row, chip], (goal, col),
            )

        def from_row(step, chip):
            source = place.peer_row(step)
            return remote(
                mine.at[source, chip], rows_in.at[source, chip], row_send.at[0, chip],
                row_recv.at[source, chip], (source, col),
            )

        order = []
        for i in range((chips + 1) // 2):
            order += [chips - 1 - i, i] if chips - 1 - i != i else [i]

        def push(goal):
            swap(goal).wait_recv()

            @pl.when(goal != row)
            def _():
                for chip in order:
                    mine[goal, chip] = (
                        mine[goal, chip].astype(F32) + extra[goal, chip].astype(F32)
                    ).astype(BF)
                    to_row(goal, chip).start()

        for step in range(1, rows_n):
            shared_to(step).start()
        for goal in range(rows_n):
            cols = slice(goal * inner, (goal + 1) * inner)
            at = 0
            for i in range(n):
                made = mm_tn(left_refs[i][...], right_refs[i][:, cols])
                if i == n - 1:
                    made = made + tail_ref[goal]
                made = made.astype(BF)
                for owner in range(cols_n):
                    both[owner % 2, goal, owner // 2, at : at + extents[i], :] = made[
                        owner * extents[i] : (owner + 1) * extents[i]
                    ]
                at += extents[i]
            swap(goal).start()
            if goal > 0:
                push(goal - 1)
        push(rows_n - 1)
        for turn in range(1, n_rounds):
            next_round(turn)
        shared_here.wait()
        for step in range(1, rows_n):
            shared_from(step).wait_recv()
        total = sh_in[0].astype(F32)
        for other in range(1, rows_n):
            total = total + sh_in[other].astype(F32)
        sh_out[...] = total[:, : 2 * units]
        cut = inner // per_row
        for turn in range(per_row):
            sd_cut[turn] = total[turn * cut : (turn + 1) * cut, 2 * units :]
            downs_to(turn, lambda far: far.start(), lambda here: here.start())

        def ready(chip):
            total = mine[row, chip].astype(F32) + extra[row, chip].astype(F32)
            for step in range(1, rows_n):
                from_row(step, chip).wait_recv()
                total = total + rows_in[place.peer_row(step), chip].astype(F32)
            mine[row, chip] = total.astype(BF)

        result, drain = line_sum_loop(
            place, mine.at[row], recv, send_sems, recv_sems, 1, ready
        )

        def store(span, value):
            out_ref[span] = value

        result(0, store)
        drain()

        moves(n_rounds - 1).wait_send()
        moves(n_rounds - 1).wait_recv()
        for turn in range(per_row):
            downs_to(turn, lambda far: far.wait_send(), lambda here: here.wait())
            at_home = per_row * row + turn
            mine_here = (at_home == col) & (down_row == row)

            @pl.when(jnp.logical_not(mine_here))
            def _():
                remote(
                    sd_cut.at[0], sd_out.at[turn], sd_send.at[turn], sd_recv.at[turn],
                    (down_row, at_home),
                ).wait_recv()

        for step in range(1, rows_n):
            shared_to(step).wait_send()
        for goal in range(rows_n):
            swap(goal).wait_send()

            @pl.when(goal != row)
            def _():
                for chip in range(chips):
                    to_row(goal, chip).wait_send()

    vmem = pl.BlockSpec(memory_space=pltpu.VMEM)
    return pl.pallas_call(
        kernel,
        in_specs=[vmem] * (2 * n + 1) + [ANY] * (1 + 2 * n_rounds),
        out_specs=[vmem, vmem, vmem, ANY],
        out_shape=[
            jax.ShapeDtypeStruct(block, F32),
            jax.ShapeDtypeStruct((inner, 2 * units), F32),
            jax.ShapeDtypeStruct((per_row, inner // per_row, units), F32),
            jax.ShapeDtypeStruct((n_rounds, 2) + moved.shape, moved.dtype),
        ],
        scratch_shapes=[
            pltpu.VMEM((2, rows_n, chips) + block, BF),
            pltpu.VMEM((rows_n, chips) + block, BF),
            pltpu.VMEM((rows_n, chips) + block, BF),
            pltpu.VMEM((chips + 1,) + block, BF),
            pltpu.VMEM(shared.shape, BF),
            pltpu.VMEM((per_row, inner // per_row, units), F32),
            pltpu.VMEM((2,) + moved.shape, BF),
            pltpu.VMEM((2,) + moved.shape, BF),
            pltpu.SemaphoreType.DMA((2,)),
            pltpu.SemaphoreType.DMA((2,)),
            pltpu.SemaphoreType.DMA((rows_n,)),
            pltpu.SemaphoreType.DMA((rows_n,)),
            pltpu.SemaphoreType.DMA((rows_n, chips)),
            pltpu.SemaphoreType.DMA((rows_n, chips)),
            pltpu.SemaphoreType.DMA((chips, 1)),
            pltpu.SemaphoreType.DMA((chips + 1, 1)),
            pltpu.SemaphoreType.DMA((rows_n,)),
            pltpu.SemaphoreType.DMA((rows_n,)),
            pltpu.SemaphoreType.DMA,
            pltpu.SemaphoreType.DMA((n_rounds, 2)),
            pltpu.SemaphoreType.DMA((n_rounds, 2)),
            pltpu.SemaphoreType.DMA((per_row,)),
            pltpu.SemaphoreType.DMA((per_row,)),
        ],
        compiler_params=pltpu.CompilerParams(
            collective_id=collective_id, has_side_effects=True,
            vmem_limit_bytes=60 * 1024 * 1024,
        ),
        cost_estimate=pl.CostEstimate(
            flops=2 * 512 * 1536 * 4096, bytes_accessed=350_000_000, transcendentals=0
        ),
        name="dense_sum",
    )(*lefts, *rights, tails, shared, *[part for pair in rounds for part in pair])


def round_tables(chips):
    order, up, down = [], [], []
    for here in range(chips):
        due = {q: chips - 1 - q + here for q in range(here + 1, chips)}
        due.update({q: q + chips - 1 - here for q in range(here)})
        calls = sorted(due, key=lambda q: (due[q], -q)) + [here]
        order.append(calls)
        at = {q: i for i, q in enumerate(calls)}
        up.append([at.get(chips - 1 - t + here, 0) for t in range(chips - 1)])
        down.append([at.get(t - (chips - 1 - here), 0) for t in range(chips - 1)])
    return order, up, down


class LineRounds:
    def __init__(self, cols_n):
        self.chips = cols_n // 2
        here = lax.axis_index("col") // 2
        _, up, down = round_tables(self.chips)
        self.up_call = jnp.array(up, jnp.int32)[here]
        self.down_call = jnp.array(down, jnp.int32)[here]
        self.not_first, self.not_last = here > 0, here < self.chips - 1
        self.sums = []
        self.below = self.above = None

    def add(self, own, other):
        self.sums.append((own, other))

    def held(self, call):
        total = None
        for i, (own, other) in enumerate(self.sums):
            value = own.astype(F32) + other.astype(F32)
            total = value if i == 0 else jnp.where(call == i, value, total)
        return total

    def kept(self, turn):
        return [self.held(call[turn]).astype(BF) for call in (self.up_call, self.down_call)]

    def outgoing(self, turn):
        ups, downs = self.held(self.up_call[turn]), self.held(self.down_call[turn])
        if turn:
            ups = ups + jnp.where(self.not_first, self.below.astype(F32), 0.0)
            downs = downs + jnp.where(self.not_last, self.above.astype(F32), 0.0)
        return ups.astype(BF), downs.astype(BF)

    def arrived(self, below, above):
        self.below, self.above = below, above

    def result(self):
        own, other = self.sums[-1]
        total = own.astype(F32) + other.astype(F32)
        total = total + jnp.where(self.not_first, self.below.astype(F32), 0.0)
        return total + jnp.where(self.not_last, self.above.astype(F32), 0.0)


def routed_kernel(call, rows_n, cols_n, n_moves, *refs):
    (
        x_hbm, dy_hbm, routes_hbm, routes_t_hbm, gates_hbm, eg_ref, eu_ref, ed_ref, sgu_ref, sd_ref
    ) = refs[:10]
    up_down, refs = refs[10 : 10 + n_moves], refs[10 + n_moves :]
    (
        own_hbm, other_hbm, xs_hbm, dys_hbm, hid_ref, gg_ref, gu_ref, ggw_ref, shared_ref
    ) = refs[:9]
    arrivals, refs = refs[9 : 9 + n_moves], refs[9 + n_moves :]
    (
        x_ref, dy_ref, routes_ref, routes_t_ref, gates_ref,
        xs, dys, pick, back_pick, wide_out, wide_gx, slot_gate, stage,
        load_sems, slot_sems, own_sems, core_send, core_recv, move_send, move_recv,
    ) = refs
    place = Place(rows_n, cols_n)
    my_core = place.core
    unit = jnp.int32(0)
    for chip, calls in enumerate(round_tables(place.chips)[0]):
        unit = unit + jnp.where(place.chip == chip, calls[call], 0)
    pair = pl.ds(2 * unit, 2)
    loads = [
        pltpu.make_async_copy(src.at[pair], dst, load_sems.at[i])
        for i, (src, dst) in enumerate(
            (
                (routes_hbm, routes_ref), (routes_t_hbm, routes_t_ref), (gates_hbm, gates_ref),
                (x_hbm, x_ref), (dy_hbm, dy_ref),
            )
        )
    ]
    moves = None
    if n_moves:
        moves = Moves(place, *up_down, *arrivals, move_send, move_recv)
    e = pl.program_id(0)
    total = x_ref.shape[1]
    cap = xs.shape[1] // 2
    hidden_units = sd_ref.shape[0]
    first = place.col * EXP_DEV
    spans = [slice(at, at + 512) for at in range(0, x_ref.shape[2], 512)]

    def slot_copy(which):
        src, dst = ((xs, xs_hbm), (dys, dys_hbm))[which]
        return pltpu.make_async_copy(src, dst, slot_sems.at[which])

    def own_copy(which):
        return pltpu.make_async_copy(
            stage.at[which, my_core], own_hbm.at[which], own_sems.at[which]
        )

    def core_copy(which):
        return remote(
            stage.at[which, 1 - my_core], other_hbm.at[which], core_send.at[which],
            core_recv.at[which], (place.row, place.other),
        )

    @pl.when(e == 0)
    def _():
        for load in loads:
            load.start()
        place.greet(False)
        if n_moves:
            moves.start()
        ggw_ref[...] = jnp.zeros_like(ggw_ref)
        for load in loads:
            load.wait()
        row_at = lax.broadcasted_iota(jnp.int32, (total, total), 0)
        col_at = lax.broadcasted_iota(jnp.int32, (total, total), 1)
        upto = jnp.where(row_at <= col_at, 1.0, 0.0).astype(BF)
        since = jnp.where(row_at >= col_at, 1.0, 0.0).astype(BF)
        for core in range(2):
            gate_rows = gates_ref[core]
            route_rows = routes_ref[core]
            route_cols = routes_t_ref[core]
            hits = [
                jnp.sum(jnp.where(route_rows == first + i, 1.0, 0.0), axis=0, keepdims=True)
                for i in range(EXP_DEV)
            ]
            hits = jnp.concatenate(hits + [jnp.zeros((8 - EXP_DEV, total), F32)], axis=0)
            rank = jnp.where(hits > 0.0, mm(hits.astype(BF), upto) - 1.0, -1.0)
            hits_t = [
                jnp.sum(jnp.where(route_cols == first + i, 1.0, 0.0), axis=1, keepdims=True)
                for i in range(EXP_DEV)
            ]
            hits_t = jnp.concatenate(hits_t + [jnp.zeros((total, 8 - EXP_DEV), F32)], axis=1)
            rank_t = jnp.where(hits_t > 0.0, mm(since, hits_t.astype(BF)) - 1.0, -1.0)
            at = lax.broadcasted_iota(jnp.int32, (cap, total), 0).astype(F32)
            at_t = lax.broadcasted_iota(jnp.int32, (total, cap), 1).astype(F32)
            backs = []
            for i in range(EXP_DEV):
                here = at == rank[i : i + 1, :]
                gate_row = jnp.sum(
                    jnp.where(route_rows == first + i, gate_rows, 0.0), axis=0, keepdims=True
                )
                slot_gate[i, core * cap : (core + 1) * cap, :] = jnp.sum(
                    jnp.where(here, gate_row, 0.0), axis=1, keepdims=True
                )
                pick[core, i * cap : (i + 1) * cap, :] = jnp.where(here, 1.0, 0.0).astype(BF)
                backs.append(jnp.where(at_t == rank_t[:, i : i + 1], 1.0, 0.0).astype(BF))
            back_pick[core] = jnp.concatenate(backs, axis=1)
            for src, dst in ((x_ref, xs), (dy_ref, dys)):
                for cols in spans:
                    got = mm(pick[core], src[core, :, cols]).astype(BF)
                    for i in range(EXP_DEV):
                        dst[i, core * cap : (core + 1) * cap, cols] = got[
                            i * cap : (i + 1) * cap
                        ]
        slot_copy(0).start()
        slot_copy(1).start()

    rows_x = xs[e]
    gate_part = mm(rows_x, eg_ref[0])
    up_part = mm(rows_x, eu_ref[0])
    act, slope = silu_parts(gate_part)
    grad_hidden = mm_nt(dys[e], ed_ref[0])
    hidden = (act * up_part).astype(BF).astype(F32)
    weight = slot_gate[e]
    gated = (hidden * weight).astype(BF)
    hid_ref[0] = gated
    slot_ggw = jnp.sum(hidden * grad_hidden, axis=1, keepdims=True)
    grad_hidden = grad_hidden * weight
    geg = (grad_hidden * up_part * slope).astype(BF)
    geu = (grad_hidden * act).astype(BF)
    gg_ref[0] = geg
    gu_ref[0] = geu
    rows = pl.ds(pl.multiple_of(e * cap, cap), cap)
    for cols in spans:
        made = mm(gated, ed_ref[0, :, cols]).astype(BF)
        back = (mm_nt(geg, eg_ref[0, cols, :]) + mm_nt(geu, eu_ref[0, cols, :])).astype(BF)
        for core in range(2):
            wide_out[core, rows, cols] = made[core * cap : (core + 1) * cap]
            wide_gx[core, rows, cols] = back[core * cap : (core + 1) * cap]
    sub = lax.broadcasted_iota(jnp.int32, (8, total), 0)
    for core in range(2):
        back = jnp.sum(
            pick[core, rows, :].astype(F32) * slot_ggw[core * cap : (core + 1) * cap],
            axis=0,
            keepdims=True,
        )
        ggw_ref[core] = jnp.where(sub == e, back, ggw_ref[core])

    @pl.when(e == EXP_DEV - 1)
    def _():
        for core in range(2):
            both = mm(x_ref[core], sgu_ref[...])
            s_act, s_slope = silu_parts(both[:, :hidden_units])
            s_up = both[:, hidden_units:]
            s_hidden = (s_act * s_up).astype(BF)
            grad_shared = mm_nt(dy_ref[core], sd_ref[...])
            grad_both = jnp.concatenate(
                [(grad_shared * s_up * s_slope).astype(BF), (grad_shared * s_act).astype(BF)],
                axis=1,
            )
            for cols in spans:
                value = mm(back_pick[core], wide_gx[core, :, cols])
                value = value + mm_nt(grad_both, sgu_ref[cols, :])
                stage[1, core, :, cols] = value.astype(BF)
                value = mm(back_pick[core], wide_out[core, :, cols])
                value = value + mm(s_hidden, sd_ref[:, cols])
                stage[0, core, :, cols] = value.astype(BF)
                made = mm_tn(x_ref[core, :, cols], grad_both)
                made_d = mm_tn(dy_ref[core, :, cols], s_hidden)
                if core == 0:
                    shared_ref[cols, : 2 * hidden_units] = made
                    shared_ref[cols, 2 * hidden_units :] = made_d
                else:
                    shared_ref[cols, : 2 * hidden_units] += made
                    shared_ref[cols, 2 * hidden_units :] += made_d
        for which in (1, 0):
            core_copy(which).start()
            own_copy(which).start()
        slot_copy(0).wait()
        slot_copy(1).wait()
        if n_moves:
            moves.wait_send()
            moves.wait_recv()
        for which in (1, 0):
            own_copy(which).wait()
            core_copy(which).wait_send()
            core_copy(which).wait_recv()


def routed(call, rows_n, x_all, dy_all, routes, routes_t, gates, egate, eup, edown, sgu, sdown, moves):
    cols_n, total, width = x_all.shape
    cap = 4 * total * TOP // (3 * EXP_DEV * cols_n)
    slots = 2 * cap
    ffn = egate.shape[2]
    hidden_units = sdown.shape[0]

    def each(*shape):
        return pl.BlockSpec((1,) + shape, lambda e: (e,) + (0,) * len(shape))

    def whole(*shape):
        return pl.BlockSpec(
            shape, lambda e: (0,) * len(shape), pipeline_mode=pl.Buffered(1)
        )

    slot_block = each(slots, ffn)
    return pl.pallas_call(
        functools.partial(routed_kernel, call, rows_n, cols_n, len(moves)),
        grid=(EXP_DEV,),
        in_specs=[ANY] * 5
        + [
            each(width, ffn), each(width, ffn), each(ffn, width), whole(*sgu.shape),
            whole(*sdown.shape),
        ]
        + [ANY] * len(moves),
        out_specs=[
            ANY, ANY, ANY, ANY, slot_block, slot_block, slot_block,
            whole(2, 8, total), whole(width, 3 * hidden_units),
        ]
        + [ANY] * len(moves),
        out_shape=[
            jax.ShapeDtypeStruct((2, total, width), BF),
            jax.ShapeDtypeStruct((2, total, width), BF),
            jax.ShapeDtypeStruct((EXP_DEV, slots, width), BF),
            jax.ShapeDtypeStruct((EXP_DEV, slots, width), BF),
            jax.ShapeDtypeStruct((EXP_DEV, slots, ffn), BF),
            jax.ShapeDtypeStruct((EXP_DEV, slots, ffn), BF),
            jax.ShapeDtypeStruct((EXP_DEV, slots, ffn), BF),
            jax.ShapeDtypeStruct((2, 8, total), F32),
            jax.ShapeDtypeStruct((width, 3 * hidden_units), F32),
        ]
        + [jax.ShapeDtypeStruct(a.shape, a.dtype) for a in moves],
        scratch_shapes=[
            pltpu.VMEM((2, total, width), BF),
            pltpu.VMEM((2, total, width), BF),
            pltpu.VMEM((2, 8, total), jnp.int32),
            pltpu.VMEM((2, total, 8), jnp.int32),
            pltpu.VMEM((2, 8, total), F32),
            pltpu.VMEM((EXP_DEV, slots, width), BF),
            pltpu.VMEM((EXP_DEV, slots, width), BF),
            pltpu.VMEM((2, EXP_DEV * cap, total), BF),
            pltpu.VMEM((2, total, EXP_DEV * cap), BF),
            pltpu.VMEM((2, EXP_DEV * cap, width), BF),
            pltpu.VMEM((2, EXP_DEV * cap, width), BF),
            pltpu.VMEM((EXP_DEV, slots, 1), F32),
            pltpu.VMEM((2, 2, total, width), BF),
            pltpu.SemaphoreType.DMA((5,)),
            pltpu.SemaphoreType.DMA((2,)),
            pltpu.SemaphoreType.DMA((2,)),
            pltpu.SemaphoreType.DMA((2,)),
            pltpu.SemaphoreType.DMA((2,)),
            pltpu.SemaphoreType.DMA((2,)),
            pltpu.SemaphoreType.DMA((2,)),
        ],
        compiler_params=pltpu.CompilerParams(
            collective_id=4 + call, has_side_effects=True, vmem_limit_bytes=60 * 1024 * 1024
        ),
        cost_estimate=pl.CostEstimate(
            flops=24_000_000_000, bytes_accessed=100_000_000, transcendentals=0
        ),
        name="routed",
    )(
        x_all, dy_all, routes, routes_t, gates, egate, eup, edown, sgu, sdown, *moves
    )


def expert_grads_kernel(units_n, place_of, *refs):
    xs, dys, hid, gg, gu = (refs[i * units_n : (i + 1) * units_n] for i in range(5))
    up, down, og_ref, ou_ref, od_ref, from_below, from_above, send_sems, recv_sems = refs[
        5 * units_n :
    ]
    place = place_of()
    moves = Moves(place, up, down, from_below, from_above, send_sems, recv_sems)

    @pl.when(pl.program_id(0) == 0)
    def _():
        place.greet(False)
        moves.start()

    rows_n = og_ref.shape[0]
    inner = og_ref.shape[2]

    def joined(parts, cols=slice(None)):
        return jnp.concatenate([part[0, :, cols] for part in parts], axis=0)

    all_gg, all_gu, all_hid = joined(gg), joined(gu), joined(hid)
    for row in range(rows_n):
        cols = slice(row * inner, (row + 1) * inner)
        rows = joined(xs, cols)
        og_ref[row, 0] = mm_tn(rows, all_gg).astype(BF)
        ou_ref[row, 0] = mm_tn(rows, all_gu).astype(BF)
        od_ref[row, 0] = mm_tn(all_hid, joined(dys, cols)).astype(BF)

    @pl.when(pl.program_id(0) == EXP_DEV - 1)
    def _():
        moves.wait_send()
        moves.wait_recv()


def expert_grads(xs, dys, hid, gg, gu, rows_n, cols_n, moves, collective_id):
    _, slots, width = xs[0].shape
    ffn = hid[0].shape[2]
    inner = width // rows_n
    units_n = len(xs)

    def each(cols):
        return pl.BlockSpec((1, slots, cols), lambda e: (e, 0, 0))

    return pl.pallas_call(
        functools.partial(expert_grads_kernel, units_n, lambda: Place(rows_n, cols_n)),
        grid=(EXP_DEV,),
        in_specs=[each(width)] * (2 * units_n)
        + [each(ffn)] * (3 * units_n)
        + [ANY] * 2,
        out_specs=[
            pl.BlockSpec((rows_n, 1, inner, ffn), lambda e: (0, e, 0, 0)),
            pl.BlockSpec((rows_n, 1, inner, ffn), lambda e: (0, e, 0, 0)),
            pl.BlockSpec((rows_n, 1, ffn, inner), lambda e: (0, e, 0, 0)),
            ANY,
            ANY,
        ],
        out_shape=[
            jax.ShapeDtypeStruct((rows_n, EXP_DEV, inner, ffn), BF),
            jax.ShapeDtypeStruct((rows_n, EXP_DEV, inner, ffn), BF),
            jax.ShapeDtypeStruct((rows_n, EXP_DEV, ffn, inner), BF),
            jax.ShapeDtypeStruct(moves[0].shape, moves[0].dtype),
            jax.ShapeDtypeStruct(moves[1].shape, moves[1].dtype),
        ],
        scratch_shapes=[pltpu.SemaphoreType.DMA((2,)), pltpu.SemaphoreType.DMA((2,))],
        compiler_params=pltpu.CompilerParams(
            collective_id=collective_id, has_side_effects=True, vmem_limit_bytes=60 * 1024 * 1024
        ),
        cost_estimate=pl.CostEstimate(
            flops=20_000_000_000, bytes_accessed=100_000_000, transcendentals=0
        ),
        name="expert_grads",
    )(*xs, *dys, *hid, *gg, *gu, *moves)


def on_device(
    tokens,
    g_attn,
    w_query,
    key_projection,
    value_projection,
    w_out,
    g_moe,
    w_router,
    e_gate,
    e_up,
    e_down,
    s_gate,
    s_up,
    s_down,
    routes,
    deal,
    lengths,
    cotangent,
):
    rows_n = lax.axis_size("row")
    cols_n = lax.axis_size("col")
    row_here = lax.axis_index("row")
    col_here = lax.axis_index("col")
    both = ("row", "col")
    total = tokens.shape[0]
    width = MODEL_WIDTH
    experts = EXP_DEV * cols_n

    q_w, k_w = w_query.shape[1], key_projection.shape[1]
    inner = w_query.shape[0]
    gains = jnp.stack([g_attn, g_moe])
    gains = jnp.pad(gains, ((0, 0), (0, inner - gains.shape[1])))
    tail = jnp.concatenate([w_router.T, gains], axis=0)
    tail = jnp.pad(tail, ((0, 16 - tail.shape[0]), (0, 0)))
    bundle = jnp.concatenate(
        [w_query.T, key_projection.T, value_projection.T, w_out.T, tail], axis=0
    )
    routes_t = jnp.pad(routes.T, ((0, 8 - TOP), (0, 0)), constant_values=-1)
    units = s_gate.shape[1]
    shared = jnp.concatenate([s_gate, s_up], axis=1)
    per_row = s_down.shape[0] // units
    downs = s_down.reshape(per_row, units, s_down.shape[1])
    full, dy_all, routes_all, sgu, sdown = first_gather(
        bundle, cotangent, routes_t, shared, downs, 0, rows_n, cols_n
    )
    sdown = jnp.swapaxes(sdown, 0, 1).reshape(units, width)
    sgu = sgu.reshape(width, 2 * units)

    def piece(lo, extent):
        part = full[:, :, lo : lo + extent]
        return part.transpose(1, 2, 0, 3).reshape(cols_n * extent, width)

    wq_t = piece(0, q_w)
    wk_t = piece(q_w, k_w)
    wv_t = piece(q_w + k_w, k_w)
    wo_t = piece(q_w + 2 * k_w, q_w)
    t_at = 2 * q_w + 2 * k_w
    router_t = piece(t_at, EXP_DEV)
    n_gain = g_attn.shape[0]
    gain_attn = full[:, :, t_at + EXP_DEV, :n_gain].reshape(width).astype(F32)
    gain_moe = full[:, :, t_at + EXP_DEV + 1, :n_gain].reshape(width).astype(F32)
    egate = lax.all_gather(e_gate, "row", axis=1, tiled=True)
    eup = lax.all_gather(e_up, "row", axis=1, tiled=True)
    edown = lax.all_gather(e_down, "row", axis=2, tiled=True)
    own_lens = lengths[deal.reshape(-1) * cols_n + col_here, row_here]
    seq_ends = jnp.cumsum(own_lens)
    places = jnp.arange(total, dtype=jnp.int32)
    segment = jnp.sum((places[:, None] >= seq_ends[None, :]).astype(jnp.int32), axis=1)

    tokens_f = tokens.astype(F32)
    scale_one = rms_scale(tokens_f)
    unit_one = tokens_f * scale_one
    normed_one = (unit_one * gain_attn).astype(BF)
    queries = mm_nt(normed_one, wq_t).astype(BF)
    keys = mm_nt(normed_one, wk_t).astype(BF)
    values = mm_nt(normed_one, wv_t).astype(BF)
    mixed, log_totals = attend_forward(queries, keys, values, segment)
    after_attn = tokens_f + mm_nt(mixed, wo_t)
    scale_two = rms_scale(after_attn)
    unit_two = after_attn * scale_two
    normed_two = (unit_two * gain_moe).astype(BF)
    logits = mm_nt(normed_two, router_t)
    route_picks = (
        routes[:, :, None] == jnp.arange(experts, dtype=jnp.int32)[None, None, :]
    ).astype(F32)
    chosen = jnp.sum(route_picks * logits[:, None, :], axis=-1)
    gate_raw = jnp.exp(chosen - jnp.max(chosen, axis=-1, keepdims=True))
    gate_weights = gate_raw / jnp.sum(gate_raw, axis=-1, keepdims=True)

    gates_t = jnp.pad(gate_weights.T, ((0, 8 - TOP), (0, 0)))
    x_all, gates_all = line_gather([normed_two, gates_t], 1, rows_n, cols_n)
    chips = cols_n // 2
    my_order = jnp.array(round_tables(chips)[0], jnp.int32)[col_here // 2]
    routes_rows = jnp.swapaxes(routes_all, 1, 2)
    gx_sum, moe_sum = LineRounds(cols_n), LineRounds(cols_n)
    saved, ggw, grad_sh = [], 0.0, 0.0
    for call in range(chips):
        moves = gx_sum.outgoing(call - 1) if call else ()
        own, other, *keep = routed(
            call, rows_n, x_all, dy_all, routes_all, routes_rows, gates_all, egate, eup, edown,
            sgu, sdown, moves,
        )
        saved.append(keep[:5])
        ggw_part, sh_part, *arrivals = keep[5:]
        if call:
            gx_sum.arrived(*arrivals)
        grad_sh = grad_sh + sh_part
        is_unit = jnp.arange(chips, dtype=jnp.int32)[:, None, None, None] == my_order[call]
        ggw = ggw + jnp.where(is_unit, ggw_part[None], 0.0)
        gx_sum.add(own[1], other[1])
        moe_sum.add(own[0], other[0])
    gx = gx_sum.result()
    grad_egate, grad_eup, grad_edown, below, above = expert_grads(
        *zip(*saved), rows_n, cols_n, moe_sum.outgoing(0), 3
    )
    moe_sum.arrived(below, above)
    ggw = ggw.reshape(cols_n, 8, total)[:, :EXP_DEV]

    ggw_home = lax.all_to_all(ggw, "col", split_axis=0, concat_axis=0, tiled=True)
    ggw_home = ggw_home.reshape(experts, total).T

    grad_gates = jnp.sum(route_picks * ggw_home[:, None, :], axis=-1)
    grad_chosen = gate_weights * (
        grad_gates - jnp.sum(gate_weights * grad_gates, axis=-1, keepdims=True)
    )
    grad_logits = jnp.sum(route_picks * grad_chosen[:, :, None], axis=1).astype(BF)
    grad_normed_two = gx + mm(grad_logits, router_t)
    grad_two, grad_gain_moe = norm_back(grad_normed_two, unit_two, scale_two, gain_moe)
    grad_after = cotangent.astype(F32) + grad_two
    grad_attn_b = grad_after.astype(BF)
    grad_mixed = mm(grad_attn_b, wo_t).astype(BF)
    gq, gk, gv = attend_backward(queries, keys, values, grad_mixed, segment, log_totals)
    grad_normed_one = mm(gq, wq_t) + mm(gk, wk_t) + mm(gv, wv_t)
    grad_one, grad_gain_attn = norm_back(grad_normed_one, unit_one, scale_one, gain_attn)
    grad_tokens = grad_after + grad_one

    rounds = [moe_sum.outgoing(1)] + [moe_sum.kept(turn) for turn in range(2, chips - 1)]

    def gain_rows(grad):
        part = grad.reshape(rows_n, cols_n, 1, n_gain)
        return jnp.pad(part, ((0, 0),) * 3 + ((0, inner - n_gain),))

    tails = jnp.concatenate([gain_rows(grad_gain_attn), gain_rows(grad_gain_moe)], axis=2)
    tails = jnp.pad(tails, ((0, 0), (0, 0), (EXP_DEV, 16 - EXP_DEV - 2), (0, 0)))
    tails = tails.reshape(rows_n, cols_n * 16, inner)
    logits_left = grad_logits.reshape(total, cols_n, EXP_DEV)
    logits_left = jnp.pad(logits_left, ((0, 0), (0, 0), (0, 16 - EXP_DEV)))
    grads_sh = grad_sh.astype(BF).reshape(rows_n, inner, 3 * units)
    dense, dense_sh, sd_parts, arrivals = dense_sum(
        [gq, gk, gv, grad_attn_b, logits_left.reshape(total, cols_n * 16)],
        [normed_one, normed_one, normed_one, mixed, normed_two],
        tails, grads_sh, rounds, 2, rows_n, cols_n,
    )
    moe_sum.arrived(arrivals[-1, 0], arrivals[-1, 1])
    output = (after_attn + moe_sum.result()).astype(BF)
    out_wq = dense[:q_w].T
    out_wk = dense[q_w : q_w + k_w].T
    out_wv = dense[q_w + k_w : q_w + 2 * k_w].T
    out_wo = dense[q_w + 2 * k_w : t_at].T
    out_router = dense[t_at : t_at + EXP_DEV].T
    out_g_attn = dense[t_at + EXP_DEV, :n_gain]
    out_g_moe = dense[t_at + EXP_DEV + 1, :n_gain]
    out_sg = dense_sh[:, :units]
    out_su = dense_sh[:, units:]
    out_sd = sd_parts.transpose(0, 2, 1).reshape(per_row * units, inner // per_row)

    def row_sum(grad):
        return lax.psum_scatter(grad, "row", scatter_dimension=0).astype(F32)

    out_eg = row_sum(grad_egate)
    out_eu = row_sum(grad_eup)
    out_ed = row_sum(grad_edown)
    return (
        output,
        grad_tokens,
        out_g_attn,
        out_wq,
        out_wk,
        out_wv,
        out_wo,
        out_g_moe,
        out_router,
        out_eg,
        out_eu,
        out_ed,
        out_sg,
        out_su,
        out_sd,
    )


def solution(mesh):
    both = P(("row", "col"), None)
    flat = P(("row", "col"))
    tile = P("row", "col")
    wide = P("col", "row", None)
    down = P("col", None, "row")
    return jax.shard_map(
        on_device,
        mesh=mesh,
        in_specs=(
            both, flat, tile, tile, tile, tile, flat, tile, wide, wide, down,
            tile, tile, tile, both, both, P(), both,
        ),
        out_specs=(
            both, both, flat, tile, tile, tile, tile, flat, tile, wide, wide, down,
            tile, tile, tile,
        ),
        check_vma=False,
    )
```

```python
import functools

import jax
import jax.numpy as jnp
from jax import lax
from jax.experimental import pallas as pl
from jax.experimental.pallas import tpu as pltpu
from jax.sharding import PartitionSpec as P

MODEL_WIDTH = 1536
QUERY_HEADS = 12
KEY_VALUE_HEADS = 4
GROUP = QUERY_HEADS // KEY_VALUE_HEADS
HEAD_SIZE = 128
TOP = 6
EXP_DEV = 4

norm_eps = 1e-05
masked_score = -1e30
BF = jnp.bfloat16
F32 = jnp.float32


def rms_scale(rows):
    return lax.rsqrt(jnp.mean(rows * rows, axis=-1, keepdims=True) + norm_eps)


def silu_parts(values):
    sigmoid_of = jax.nn.sigmoid(values)
    return (values * sigmoid_of, sigmoid_of * (1.0 + values * (1.0 - sigmoid_of)))


def norm_back(grad_normed, unit_rows, scale_rows, gain):
    grad_unit = grad_normed * gain
    grad_rows = scale_rows * (
        grad_unit - unit_rows * jnp.mean(grad_unit * unit_rows, axis=-1, keepdims=True)
    )
    return (grad_rows, jnp.sum(grad_normed * unit_rows, axis=0))


def mm(left, right):
    return jnp.dot(left, right, preferred_element_type=F32)


def mm_nt(left, right):
    return lax.dot_general(left, right, (((1,), (1,)), ((), ())), preferred_element_type=F32)


def mm_tn(left, right):
    return lax.dot_general(left, right, (((0,), (0,)), ((), ())), preferred_element_type=F32)


def ein(spec, a, b):
    return jnp.einsum(spec, a, b, preferred_element_type=F32)


def allowed_mask(seg_col, seg_row):
    total = seg_col.shape[0]
    q_at = lax.broadcasted_iota(jnp.int32, (total, total), 0)
    k_at = lax.broadcasted_iota(jnp.int32, (total, total), 1)
    return (seg_col == seg_row) & (k_at <= q_at)


def attend_forward_group(h, q_ref, k_ref, v_ref, allowed, mixed_ref, lse_ref):
    here = pl.ds(pl.multiple_of(h * HEAD_SIZE, HEAD_SIZE), HEAD_SIZE)
    keys = k_ref[:, here]
    values = v_ref[:, here]
    for g in range(GROUP):
        at = pl.multiple_of((h * GROUP + g) * HEAD_SIZE, HEAD_SIZE)
        cols = pl.ds(at, HEAD_SIZE)
        scores = mm_nt(q_ref[:, cols], keys) * HEAD_SIZE ** (-0.5)
        scores = jnp.where(allowed, scores, masked_score)
        peak = jnp.max(scores, axis=-1, keepdims=True)
        raw = jnp.exp(scores - peak)
        total = jnp.sum(raw, axis=-1, keepdims=True)
        probs = (raw * (1.0 / total)).astype(BF)
        mixed_ref[:, cols] = mm(probs, values).astype(BF)
        lse_ref[h, :, g : g + 1] = peak + jnp.log(total)


def attend_backward_group(h, q_ref, k_ref, v_ref, gm_ref, allowed, lse_ref, gq_ref, gk_ref, gv_ref):
    here = pl.ds(pl.multiple_of(h * HEAD_SIZE, HEAD_SIZE), HEAD_SIZE)
    keys = k_ref[:, here]
    values = v_ref[:, here]
    scale = HEAD_SIZE ** (-0.5)
    grad_key = grad_value = None
    for g in range(GROUP):
        at = pl.multiple_of((h * GROUP + g) * HEAD_SIZE, HEAD_SIZE)
        cols = pl.ds(at, HEAD_SIZE)
        query = q_ref[:, cols]
        grad_mixed = gm_ref[:, cols]
        scores = mm_nt(query, keys) * scale
        probs = jnp.where(allowed, jnp.exp(scores - lse_ref[h, :, g : g + 1]), 0.0)
        grad_probs = mm_nt(grad_mixed, values)
        inner = jnp.sum(probs * grad_probs, axis=-1, keepdims=True)
        grad_scores = (probs * (grad_probs - inner)).astype(BF)
        gq_ref[:, cols] = (mm(grad_scores, keys) * scale).astype(BF)
        part_key = mm_tn(grad_scores, query)
        part_value = mm_tn(probs.astype(BF), grad_mixed)
        grad_key = part_key if g == 0 else grad_key + part_key
        grad_value = part_value if g == 0 else grad_value + part_value
    gk_ref[:, here] = (grad_key * scale).astype(BF)
    gv_ref[:, here] = grad_value.astype(BF)


class DenseWeights:
    def __init__(self, full, extents):
        self.rows_n, self.cols_n, _, self.inner = full.shape
        self.extents = extents
        self.width = self.rows_n * self.inner
        self.cut = self.inner % 128 == 0
        self.operands = [full]
        if not self.cut:
            self.operands = []
            at = 0
            for extent in extents:
                part = full[:, :, at : at + extent].transpose(1, 2, 0, 3)
                self.operands.append(part.reshape(self.cols_n, extent, self.width))
                at += extent
        self.count = len(self.operands)
        self.scratch = [
            pltpu.VMEM((self.cols_n, extent, self.width), BF) for extent in extents
        ] + [pltpu.SemaphoreType.DMA((len(extents), self.rows_n))]

    def copies(self, sources, held, sems):
        made = []
        at = 0
        for part, extent in enumerate(self.extents):
            if self.cut:
                made.append(
                    [
                        pltpu.make_async_copy(
                            sources[0].at[r, :, pl.ds(at, extent), :],
                            held[part].at[:, :, pl.ds(r * self.inner, self.inner)],
                            sems.at[part, r],
                        )
                        for r in range(self.rows_n)
                    ]
                )
            else:
                made.append(
                    [pltpu.make_async_copy(sources[part], held[part], sems.at[part, 0])]
                )
            at += extent
        return made


ROW_STEP = 64


def flat(value):
    return value.reshape(value.shape[0] * value.shape[1], value.shape[2])


def route_columns(routes):
    return lax.div(routes, EXP_DEV) * 16 + lax.rem(routes, EXP_DEV)


def column_spans(width, count=KEY_VALUE_HEADS):
    step = width // count
    return [slice(at, at + step) for at in range(0, width, step)]


def block_start(tokens, full, extents, gains, segment, routes):
    total, width = tokens.shape
    weights = DenseWeights(full, extents)
    n = weights.count
    per_group = weights.cols_n // KEY_VALUE_HEADS

    def kernel(*refs):
        sources = refs[:n]
        (
            tok_ref, gain_ref, segc_ref, segr_ref, routes_ref,
            n1_ref, q_ref, k_ref, v_ref, mixed_ref, lse_ref, after_ref, n2_ref, s1_ref, s2_ref,
            gates_ref, gates_t_ref, *held, sems,
        ) = refs[n:]
        copies = weights.copies(sources, held, sems)
        for part in copies:
            for copy in part:
                copy.start()

        @pl.loop(0, total // ROW_STEP)
        def _(step):
            rows = pl.ds(pl.multiple_of(step * ROW_STEP, ROW_STEP), ROW_STEP)
            x = tok_ref[rows].astype(F32)
            scale = rms_scale(x)
            n1_ref[rows] = (x * scale * gain_ref[0:1]).astype(BF)
            s1_ref[rows] = scale

        for part in copies:
            for copy in part:
                copy.wait()
        normed = n1_ref[...]
        for h, cols in enumerate(column_spans(width)):
            mine = slice(h * per_group, (h + 1) * per_group)
            q_ref[:, cols] = mm_nt(normed, flat(held[0][mine])).astype(BF)
        k_ref[...] = mm_nt(normed, flat(held[1][...])).astype(BF)
        v_ref[...] = mm_nt(normed, flat(held[2][...])).astype(BF)
        allowed = allowed_mask(segc_ref[...], segr_ref[...])

        @pl.loop(0, KEY_VALUE_HEADS)
        def _(h):
            attend_forward_group(h, q_ref, k_ref, v_ref, allowed, mixed_ref, lse_ref)

        mixed = mixed_ref[...]
        for h, cols in enumerate(column_spans(width)):
            mine = slice(h * per_group, (h + 1) * per_group)
            after_ref[:, cols] = tok_ref[:, cols].astype(F32) + mm_nt(mixed, flat(held[3][mine]))

        @pl.loop(0, total // ROW_STEP)
        def _(step):
            rows = pl.ds(pl.multiple_of(step * ROW_STEP, ROW_STEP), ROW_STEP)
            after = after_ref[rows]
            scale = rms_scale(after)
            n2_ref[rows] = (after * scale * gain_ref[1:2]).astype(BF)
            s2_ref[rows] = scale

        logits = mm_nt(n2_ref[...], flat(held[4][...]))
        lane = lax.broadcasted_iota(jnp.int32, logits.shape, 1)
        goal = route_columns(routes_ref[...])
        chosen = [
            jnp.sum(jnp.where(lane == goal[:, i : i + 1], logits, 0.0), axis=1, keepdims=True)
            for i in range(TOP)
        ]
        peak = functools.reduce(jnp.maximum, chosen)
        raw = [jnp.exp(value - peak) for value in chosen]
        whole = functools.reduce(jnp.add, raw)
        lane = lax.broadcasted_iota(jnp.int32, (total, 128), 1)
        wide = jnp.zeros((total, 128), F32)
        for i in range(TOP):
            wide = jnp.where(lane == i, raw[i] / whole, wide)
        gates_ref[...] = wide[:, :8]
        gates_t_ref[...] = wide.T[:8]

    vmem = pl.BlockSpec(memory_space=pltpu.VMEM)
    kv = KEY_VALUE_HEADS * HEAD_SIZE
    shapes = [
        ((total, width), BF), ((total, width), BF), ((total, kv), BF), ((total, kv), BF),
        ((total, width), BF), ((KEY_VALUE_HEADS, total, GROUP), F32), ((total, width), F32),
        ((total, width), BF), ((total, 1), F32), ((total, 1), F32), ((total, 8), F32),
        ((8, total), F32),
    ]
    return pl.pallas_call(
        kernel,
        in_specs=[pl.BlockSpec(memory_space=pl.ANY)] * n + [vmem] * 5,
        out_specs=[vmem] * len(shapes),
        out_shape=[jax.ShapeDtypeStruct(shape, kind) for shape, kind in shapes],
        scratch_shapes=weights.scratch,
        compiler_params=pltpu.CompilerParams(vmem_limit_bytes=60 * 1024 * 1024),
        cost_estimate=pl.CostEstimate(
            flops=10_000_000_000, bytes_accessed=30_000_000, transcendentals=0
        ),
        name="block_start",
    )(*weights.operands, tokens, gains, segment[:, None], segment[None, :], routes)


def block_end(
    tokens, cotangent, full, extents, gains, segment, routes, gates, ggw, sums,
    queries, keys, values, log_totals, after, scale_one, scale_two,
):
    total, width = tokens.shape
    weights = DenseWeights(full, extents)
    n = weights.count
    chips = weights.cols_n // 2
    experts = ggw.shape[0]

    def kernel(*refs):
        sources = refs[:n]
        (
            tok_ref, dy_ref, gain_ref, segc_ref, segr_ref, routes_ref, gates_ref, ggw_ref,
            own_ref, other_ref, below_ref, above_ref, q_ref, k_ref, v_ref, lse_ref, after_ref,
            s1_ref, s2_ref,
            gtok_ref, gq_ref, gk_ref, gv_ref, gab_ref, glog_ref, ggain_ref,
            acc, grad_mixed, *held, sems,
        ) = refs[n:]
        copies = weights.copies(sources, held, sems)
        for part in (4, 3, 0, 1, 2):
            for copy in copies[part]:
                copy.start()
        chip = lax.div(lax.axis_index("col"), 2)
        not_first, not_last = chip > 0, chip < chips - 1

        per_expert = jnp.pad(ggw_ref[...], ((0, 128 - experts), (0, 0))).T
        lane = lax.broadcasted_iota(jnp.int32, (total, 128), 1)
        goals = routes_ref[...]
        weight = [gates_ref[:, i : i + 1] for i in range(TOP)]
        grads = [
            jnp.sum(jnp.where(lane == goals[:, i : i + 1], per_expert, 0.0), axis=1, keepdims=True)
            for i in range(TOP)
        ]
        mean = functools.reduce(jnp.add, [w * g for w, g in zip(weight, grads)])
        goals = route_columns(goals)
        lane = lax.broadcasted_iota(jnp.int32, glog_ref.shape, 1)
        spread = jnp.zeros(glog_ref.shape, F32)
        for i in range(TOP):
            spread = jnp.where(lane == goals[:, i : i + 1], weight[i] * (grads[i] - mean), spread)
        glog = spread.astype(BF)
        glog_ref[...] = glog
        for copy in copies[4]:
            copy.wait()
        for cols in column_spans(width):
            acc[:, cols] = mm(glog, flat(held[4][:, :, cols]))
        ggain_ref[...] = jnp.zeros_like(ggain_ref)

        @pl.loop(0, total // ROW_STEP)
        def _(step):
            rows = pl.ds(pl.multiple_of(step * ROW_STEP, ROW_STEP), ROW_STEP)
            grad = acc[rows] + own_ref[rows].astype(F32) + other_ref[rows].astype(F32)
            grad = grad + jnp.where(not_first, below_ref[rows].astype(F32), 0.0)
            grad = grad + jnp.where(not_last, above_ref[rows].astype(F32), 0.0)
            scale = s2_ref[rows]
            unit = after_ref[rows] * scale
            back, gain = norm_back(grad, unit, scale, gain_ref[1:2])
            ggain_ref[1:2] += gain[None]
            value = dy_ref[rows].astype(F32) + back
            acc[rows] = value
            gab_ref[rows] = value.astype(BF)

        for copy in copies[3]:
            copy.wait()
        rounded = gab_ref[...]
        for cols in column_spans(width):
            grad_mixed[:, cols] = mm(rounded, flat(held[3][:, :, cols])).astype(BF)
        allowed = allowed_mask(segc_ref[...], segr_ref[...])

        @pl.loop(0, KEY_VALUE_HEADS)
        def _(h):
            attend_backward_group(
                h, q_ref, k_ref, v_ref, grad_mixed, allowed, lse_ref, gq_ref, gk_ref, gv_ref
            )

        for part in range(3):
            for copy in copies[part]:
                copy.wait()
        for cols in column_spans(width):
            gtok_ref[:, cols] = (
                mm(gq_ref[...], flat(held[0][:, :, cols]))
                + mm(gk_ref[...], flat(held[1][:, :, cols]))
                + mm(gv_ref[...], flat(held[2][:, :, cols]))
            )

        @pl.loop(0, total // ROW_STEP)
        def _(step):
            rows = pl.ds(pl.multiple_of(step * ROW_STEP, ROW_STEP), ROW_STEP)
            scale = s1_ref[rows]
            unit = tok_ref[rows].astype(F32) * scale
            back, gain = norm_back(gtok_ref[rows], unit, scale, gain_ref[0:1])
            ggain_ref[0:1] += gain[None]
            gtok_ref[rows] = acc[rows] + back

    vmem = pl.BlockSpec(memory_space=pltpu.VMEM)
    kv = KEY_VALUE_HEADS * HEAD_SIZE
    shapes = [
        ((total, width), F32), ((total, width), BF), ((total, kv), BF), ((total, kv), BF),
        ((total, width), BF), ((total, weights.cols_n * 16), BF), ((2, width), F32),
    ]
    args = (
        tokens, cotangent, gains, segment[:, None], segment[None, :], routes, gates, ggw, *sums,
        queries, keys, values, log_totals, after, scale_one, scale_two,
    )
    return pl.pallas_call(
        kernel,
        in_specs=[pl.BlockSpec(memory_space=pl.ANY)] * n + [vmem] * len(args),
        out_specs=[vmem] * len(shapes),
        out_shape=[jax.ShapeDtypeStruct(shape, kind) for shape, kind in shapes],
        scratch_shapes=[pltpu.VMEM((total, width), F32), pltpu.VMEM((total, width), BF)]
        + weights.scratch,
        compiler_params=pltpu.CompilerParams(vmem_limit_bytes=60 * 1024 * 1024),
        cost_estimate=pl.CostEstimate(
            flops=20_000_000_000, bytes_accessed=40_000_000, transcendentals=0
        ),
        name="block_end",
    )(*weights.operands, *args)


def remote(src, dst, send_sem, recv_sem, device):
    return pltpu.make_async_remote_copy(
        src_ref=src,
        dst_ref=dst,
        send_sem=send_sem,
        recv_sem=recv_sem,
        device_id=device,
        device_id_type=pl.DeviceIdType.MESH,
    )


class Place:
    def __init__(self, rows_n, cols_n):
        self.rows_n = rows_n
        self.chips = cols_n // 2
        self.row = lax.axis_index("row")
        self.col = lax.axis_index("col")
        self.chip = lax.div(self.col, 2)
        self.core = lax.rem(self.col, 2)
        self.other = self.col + 1 - 2 * self.core

    def peer_row(self, step):
        return lax.rem(self.row + step, self.rows_n)

    def greet(self, with_rows, per_row=0, downs_back=0):
        barrier = pltpu.get_barrier_semaphore()

        def hello(row, col):
            pl.semaphore_signal(
                barrier, inc=1, device_id=(row, col), device_id_type=pl.DeviceIdType.MESH
            )

        hello(self.row, self.other)

        @pl.when(self.chip > 0)
        def _():
            hello(self.row, self.col - 2)

        @pl.when(self.chip < self.chips - 1)
        def _():
            hello(self.row, self.col + 2)

        count = (
            1
            + (self.chip > 0).astype(jnp.int32)
            + (self.chip < self.chips - 1).astype(jnp.int32)
        )
        if with_rows:
            for step in range(1, self.rows_n):
                hello(self.peer_row(step), self.col)
            count = count + (self.rows_n - 1)
        if per_row:
            source = lax.div(self.col, per_row)
            for col in range(2 * self.chips):

                @pl.when(jnp.logical_not((source == self.row) & (self.col == col)))
                def _():
                    hello(source, jnp.int32(col))

            count = count + self.rows_n * per_row - (source == self.row).astype(jnp.int32)
        if downs_back:
            goal = lax.div(self.col, downs_back)
            for turn in range(downs_back):
                goal_col = downs_back * self.row + turn

                @pl.when(jnp.logical_not((goal == self.row) & (goal_col == self.col)))
                def _():
                    hello(goal, goal_col)

            count = count + downs_back - (goal == self.row).astype(jnp.int32)
        pl.semaphore_wait(barrier, count)


class Moves:
    def __init__(self, place, up, down, from_below, from_above, send_sems, recv_sems):
        self.place = place
        self.copies = [
            remote(
                src, dst, send_sems.at[which], recv_sems.at[which],
                (place.row, place.col + way),
            )
            for which, (src, dst, way) in enumerate(
                ((up, from_below, 2), (down, from_above, -2))
            )
        ]
        self.ends = (place.chip < place.chips - 1, place.chip > 0)

    def start(self):
        for which in range(2):

            @pl.when(self.ends[which])
            def _():
                self.copies[which].start()

    def wait_send(self):
        for which in range(2):

            @pl.when(self.ends[which])
            def _():
                self.copies[which].wait_send()

    def wait_recv(self):
        for which in range(2):

            @pl.when(self.ends[1 - which])
            def _():
                self.copies[which].wait_recv()


class LineGather:
    def __init__(self, place, src, dst, core_sems, line_sems, recv_sems, local_sem):
        self.at = place
        self.src, self.dst = src, dst
        self.core_sems, self.line_sems, self.recv_sems = core_sems, line_sems, recv_sems
        self.local = pltpu.make_async_copy(src, dst.at[place.col], local_sem)

    def to_core(self, block, src=None):
        at = self.at
        src = self.dst.at[block] if src is None else src
        return remote(
            src, self.dst.at[block], self.core_sems.at[block], self.recv_sems.at[block],
            (at.row, at.other),
        )

    def to_line(self, block, way, src=None):
        at = self.at
        src = self.dst.at[block] if src is None else src
        return remote(
            src,
            self.dst.at[block],
            self.line_sems.at[block, (way + 1) // 2],
            self.recv_sems.at[block],
            (at.row, at.col + 2 * way),
        )

    def ends(self, way):
        return self.at.chip < self.at.chips - 1 if way > 0 else self.at.chip > 0

    def start(self):
        self.local.start()
        for way in (1, -1):

            @pl.when(self.ends(way))
            def _():
                self.to_line(self.at.col, way, self.src).start()

        self.to_core(self.at.col, self.src).start()

    def arrivals(self, dist, act):
        for way in (1, -1):
            chip = self.at.chip - way * dist
            near = chip >= 0 if way > 0 else chip < self.at.chips

            @pl.when(near)
            def _():
                act(2 * chip + self.at.core, way)

    def step(self, dist, extra=None):
        def act(block, way):
            self.to_core(block).wait_recv()

            @pl.when(self.ends(way))
            def _():
                self.to_line(block, way).start()

            self.to_core(block).start()
            if extra is not None:
                extra(block)

        self.arrivals(dist, act)

    def finish(self):
        self.local.wait()
        self.to_core(self.at.col, self.src).wait_send()
        for way in (1, -1):

            @pl.when(self.ends(way))
            def _():
                self.to_line(self.at.col, way, self.src).wait_send()

        def act(block, way):
            self.to_core(block).wait_send()

            @pl.when(self.ends(way))
            def _():
                self.to_line(block, way).wait_send()

        for dist in range(1, self.at.chips):
            self.arrivals(dist, act)
        for chip in range(self.at.chips):
            self.to_core(2 * chip + 1 - self.at.core).wait_recv()


def gather_sems(cols_n):
    return [
        pltpu.SemaphoreType.DMA((cols_n,)),
        pltpu.SemaphoreType.DMA((cols_n, 2)),
        pltpu.SemaphoreType.DMA((cols_n,)),
        pltpu.SemaphoreType.DMA,
    ]


ANY = pl.BlockSpec(memory_space=pl.ANY)


def line_gather(arrays, collective_id, rows_n, cols_n):
    n = len(arrays)

    def kernel(*refs):
        srcs, dsts, sems = refs[:n], refs[n : 2 * n], refs[2 * n :]
        place = Place(rows_n, cols_n)
        place.greet(False)
        jobs = [
            LineGather(place, srcs[i], dsts[i], *sems[4 * i : 4 * i + 4]) for i in range(n)
        ]
        for job in jobs:
            job.start()
        for dist in range(1, place.chips):
            for job in jobs:
                job.step(dist)
        for job in jobs:
            job.finish()

    return pl.pallas_call(
        kernel,
        in_specs=[ANY] * n,
        out_specs=[ANY] * n,
        out_shape=[jax.ShapeDtypeStruct((cols_n,) + a.shape, a.dtype) for a in arrays],
        scratch_shapes=gather_sems(cols_n) * n,
        compiler_params=pltpu.CompilerParams(collective_id=collective_id, has_side_effects=True),
        name="line_gather",
    )(*arrays)


def first_gather(bundle, cotangent, routes_t, shared, downs, collective_id, rows_n, cols_n):
    per_row = downs.shape[0]

    def kernel(
        bundle_ref, dy_ref, rt_ref, sh_ref, sd_ref,
        full_ref, dy_all, rt_all, sh_all, sd_all, *sems
    ):
        place = Place(rows_n, cols_n)
        b_sems, sems = sems[:4], sems[4:]
        d_sems, sems = sems[:4], sems[4:]
        r_sems, sems = sems[:4], sems[4:]
        row_send, row_core, row_recv, sh_send, sh_recv, sh_local, sd_send, sd_recv = sems
        place.greet(True, per_row)
        row, col = place.row, place.col
        weights = LineGather(place, bundle_ref, full_ref.at[row], *b_sems)
        grads = LineGather(place, dy_ref, dy_all, *d_sems)
        picks = LineGather(place, rt_ref, rt_all, *r_sems)

        def to_row(block, step, src=None):
            home = full_ref.at[row, block]
            return remote(
                home if src is None else src, home, row_send.at[block, step],
                row_recv.at[row, block], (place.peer_row(step), col),
            )

        def push(block, src=None):
            for step in range(1, rows_n):
                to_row(block, step, src).start()

        def from_row(other_row, block):
            home = full_ref.at[other_row, block]
            return remote(
                home, home, row_core.at[other_row, block], row_recv.at[other_row, block],
                (row, place.other),
            )

        def shared_to(step):
            return remote(
                sh_ref, sh_all.at[row], sh_send.at[step], sh_recv.at[row],
                (place.peer_row(step), col),
            )

        down_row = lax.div(col, per_row)

        def downs_to(act_far, act_here):
            for step in range(rows_n):
                for turn in range(per_row):
                    goal_row, goal_col = place.peer_row(step), per_row * row + turn
                    here = (goal_col == col) if step == 0 else None
                    far = remote(
                        sd_ref.at[turn], sd_all.at[col], sd_send.at[step, turn],
                        sd_recv.at[col], (goal_row, goal_col),
                    )
                    if here is None:
                        act_far(far)
                        continue

                    @pl.when(here)
                    def _():
                        act_here(
                            pltpu.make_async_copy(
                                sd_ref.at[turn], sd_all.at[col], sd_recv.at[col]
                            )
                        )

                    @pl.when(jnp.logical_not(here))
                    def _():
                        act_far(far)

        weights.start()
        push(col, bundle_ref)
        shared_here = pltpu.make_async_copy(sh_ref, sh_all.at[row], sh_local)
        shared_here.start()
        for step in range(1, rows_n):
            shared_to(step).start()
        for dist in range(1, place.chips):
            weights.step(dist, push)
        downs_to(lambda far: far.start(), lambda here: here.start())
        grads.start()
        picks.start()
        for dist in range(1, place.chips - 1):
            grads.step(dist)
            picks.step(dist)
        for step in range(1, rows_n):
            other_row = place.peer_row(step)

            @pl.loop(0, place.chips)
            def _(chip):
                copy = from_row(other_row, 2 * chip + place.core)
                copy.wait_recv()
                copy.start()

        grads.step(place.chips - 1)
        picks.step(place.chips - 1)
        weights.finish()
        grads.finish()
        picks.finish()
        shared_here.wait()
        downs_to(lambda far: far.wait_send(), lambda here: here.wait())

        @pl.loop(0, cols_n)
        def _(source):
            @pl.when(jnp.logical_not((source == col) & (down_row == row)))
            def _():
                remote(
                    sd_ref.at[0], sd_all.at[source], sd_send.at[0, 0], sd_recv.at[source],
                    (row, place.other),
                ).wait_recv()

        for step in range(1, rows_n):
            other_row = place.peer_row(step)
            shared_to(step).wait_send()
            remote(
                sh_ref, sh_all.at[other_row], sh_send.at[0], sh_recv.at[other_row],
                (other_row, col),
            ).wait_recv()

            @pl.loop(0, place.chips)
            def _(chip):
                to_row(2 * chip + place.core, step).wait_send()
                from_row(other_row, 2 * chip + place.core).wait_send()
                from_row(other_row, 2 * chip + 1 - place.core).wait_recv()

    return pl.pallas_call(
        kernel,
        in_specs=[ANY] * 5,
        out_specs=[ANY] * 5,
        out_shape=[
            jax.ShapeDtypeStruct((rows_n, cols_n) + bundle.shape, bundle.dtype),
            jax.ShapeDtypeStruct((cols_n,) + cotangent.shape, cotangent.dtype),
            jax.ShapeDtypeStruct((cols_n,) + routes_t.shape, routes_t.dtype),
            jax.ShapeDtypeStruct((rows_n,) + shared.shape, shared.dtype),
            jax.ShapeDtypeStruct((cols_n,) + downs.shape[1:], downs.dtype),
        ],
        scratch_shapes=gather_sems(cols_n) * 3
        + [
            pltpu.SemaphoreType.DMA((cols_n, rows_n)),
            pltpu.SemaphoreType.DMA((rows_n, cols_n)),
            pltpu.SemaphoreType.DMA((rows_n, cols_n)),
            pltpu.SemaphoreType.DMA((rows_n,)),
            pltpu.SemaphoreType.DMA((rows_n,)),
            pltpu.SemaphoreType.DMA,
            pltpu.SemaphoreType.DMA((rows_n, per_row)),
            pltpu.SemaphoreType.DMA((cols_n,)),
        ],
        compiler_params=pltpu.CompilerParams(collective_id=collective_id, has_side_effects=True),
        name="first_gather",
    )(bundle, cotangent, routes_t, shared, downs)


def line_sum_loop(place, mine, recv, send_sems, recv_sems, parts, ready):
    chips, here = place.chips, place.chip
    rows = mine.shape[1] // parts
    items = (chips - 1) * parts

    def copy(chip, part, way):
        span = pl.ds(part * rows, rows)
        goal = here + way
        land = chip if way > 0 else jnp.where(chip == goal, chips, chip)
        return remote(
            mine.at[chip, span],
            recv.at[land, span],
            send_sems.at[chip, part],
            recv_sems.at[land, part],
            (place.row, place.col + 2 * way),
        )

    def incoming(land, part):
        span = pl.ds(part * rows, rows)
        return remote(
            mine.at[0, span], recv.at[land, span], send_sems.at[0, part],
            recv_sems.at[land, part], (place.row, place.other),
        )

    def handle(chip, part, way):
        @pl.when(part == 0)
        def _():
            ready(chip)

        span = pl.ds(part * rows, rows)
        comes = here > 0 if way > 0 else here < chips - 1

        @pl.when(comes)
        def _():
            incoming(chip, part).wait_recv()
            total = mine[chip, span].astype(F32) + recv[chip, span].astype(F32)
            mine[chip, span] = total.astype(mine.dtype)

        copy(chip, part, way).start()

    lag = 2 * (chips - 2 - here)

    @pl.loop(0, items + 2 * (chips - 2))
    def _(at):
        up = jnp.minimum(at, items - 1)
        up_chip = chips - 1 - lax.div(up, parts)

        @pl.when((at < items) & (up_chip > here))
        def _():
            handle(up_chip, lax.rem(up, parts), 1)

        down = at - jnp.maximum(lag, 0)
        safe = jnp.clip(down, 0, items - 1)
        down_chip = lax.div(safe, parts)

        @pl.when((down >= 0) & (down < items) & (down_chip < here))
        def _():
            handle(down_chip, lax.rem(safe, parts), -1)

    ready(here)

    def result(part, store):
        span = pl.ds(part * rows, rows)
        total = mine[here, span].astype(F32)

        @pl.when((here > 0) & (here < chips - 1))
        def _():
            incoming(here, part).wait_recv()
            incoming(chips, part).wait_recv()
            store(span, total + recv[here, span].astype(F32) + recv[chips, span].astype(F32))

        @pl.when((here > 0) & (here == chips - 1))
        def _():
            incoming(here, part).wait_recv()
            store(span, total + recv[here, span].astype(F32))

        @pl.when((here == 0) & (here < chips - 1))
        def _():
            incoming(chips, part).wait_recv()
            store(span, total + recv[chips, span].astype(F32))

    def drain():
        @pl.loop(0, chips)
        def _(chip):
            for part in range(parts):

                @pl.when(chip > here)
                def _():
                    copy(chip, part, 1).wait_send()

                @pl.when(chip < here)
                def _():
                    copy(chip, part, -1).wait_send()

    return result, drain


def dense_sum(lefts, rights, tails, shared, rounds, collective_id, rows_n, cols_n):
    n_rounds = len(rounds)
    moved = rounds[0][0]
    chips = cols_n // 2
    inner = shared.shape[1]
    units = shared.shape[2] // 3
    per_row = cols_n // rows_n
    extents = [left.shape[1] // cols_n for left in lefts]
    block = (sum(extents), inner)
    n = len(lefts)

    def kernel(*refs):
        left_refs, right_refs = refs[:n], refs[n : 2 * n]
        (
            tail_ref, sh_ref, *round_refs
        ) = refs[2 * n : 2 * n + 2 + 2 * n_rounds]
        (
            out_ref, sh_out, sd_out, arrivals,
            both, extra, rows_in, recv, sh_in, sd_cut, held, came, held_sems, came_sems,
            core_send, core_recv, row_send, row_recv, send_sems, recv_sems,
            sh_send, sh_recv, sh_local, move_send, move_recv, sd_send, sd_recv,
        ) = refs[2 * n + 2 + 2 * n_rounds :]
        place = Place(rows_n, cols_n)
        row, col = place.row, place.col
        mine = both.at[place.core]
        shared_here = pltpu.make_async_copy(sh_ref.at[row], sh_in.at[row], sh_local)
        shared_here.start()
        down_row = lax.div(col, per_row)
        place.greet(True, downs_back=per_row)

        def moves(turn):
            pair = round_refs[:2] if turn == 0 else (held.at[0], held.at[1])
            return Moves(
                place, *pair, arrivals.at[turn, 0], arrivals.at[turn, 1], move_send.at[turn],
                move_recv.at[turn],
            )

        def hold(turn):
            return [
                pltpu.make_async_copy(
                    round_refs[2 * turn + which], held.at[which], held_sems.at[which]
                )
                for which in range(2)
            ]

        def next_round(turn):
            moves(turn - 1).wait_send()
            copies = hold(turn)
            for copy in copies:
                copy.start()
            moves(turn - 1).wait_recv()
            for which, comes in ((0, place.chip > 0), (1, place.chip < chips - 1)):
                bring = pltpu.make_async_copy(
                    arrivals.at[turn - 1, which], came.at[which], came_sems.at[which]
                )

                @pl.when(comes)
                def _():
                    bring.start()

                copies[which].wait()

                @pl.when(comes)
                def _():
                    bring.wait()
                    part = came.shape[1] // 4
                    for at in range(0, came.shape[1], part):
                        span = slice(at, at + part)
                        held[which, span] = (
                            held[which, span].astype(F32) + came[which, span].astype(F32)
                        ).astype(BF)

            moves(turn).start()

        moves(0).start()

        def downs_to(turn, act_far, act_here):
            goal_col = per_row * row + turn
            here = (goal_col == col) & (down_row == row)
            source = lax.rem(col, per_row)

            @pl.when(here)
            def _():
                act_here(
                    pltpu.make_async_copy(
                        sd_cut.at[turn], sd_out.at[source], sd_recv.at[source]
                    )
                )

            @pl.when(jnp.logical_not(here))
            def _():
                act_far(
                    remote(
                        sd_cut.at[turn], sd_out.at[source], sd_send.at[turn],
                        sd_recv.at[source], (down_row, goal_col),
                    )
                )

        def swap(goal):
            return remote(
                both.at[1 - place.core, goal], extra.at[goal], core_send.at[goal],
                core_recv.at[goal], (row, place.other),
            )

        def shared_to(step):
            goal = place.peer_row(step)
            return remote(
                sh_ref.at[goal], sh_in.at[row], sh_send.at[step], sh_recv.at[row], (goal, col)
            )

        def shared_from(step):
            source = place.peer_row(step)
            return remote(
                sh_ref.at[source], sh_in.at[source], sh_send.at[0], sh_recv.at[source],
                (source, col),
            )

        def to_row(goal, chip):
            return remote(
                mine.at[goal, chip], rows_in.at[row, chip], row_send.at[goal, chip],
                row_recv.at[row, chip], (goal, col),
            )

        def from_row(step, chip):
            source = place.peer_row(step)
            return remote(
                mine.at[source, chip], rows_in.at[source, chip], row_send.at[0, chip],
                row_recv.at[source, chip], (source, col),
            )

        order = []
        for i in range((chips + 1) // 2):
            order += [chips - 1 - i, i] if chips - 1 - i != i else [i]

        def push(goal):
            swap(goal).wait_recv()

            @pl.when(goal != row)
            def _():
                for chip in order:
                    mine[goal, chip] = (
                        mine[goal, chip].astype(F32) + extra[goal, chip].astype(F32)
                    ).astype(BF)
                    to_row(goal, chip).start()

        for step in range(1, rows_n):
            shared_to(step).start()
        for goal in range(rows_n):
            cols = slice(goal * inner, (goal + 1) * inner)
            at = 0
            for i in range(n):
                made = mm_tn(left_refs[i][...], right_refs[i][:, cols])
                if i == n - 1:
                    made = made + tail_ref[goal]
                made = made.astype(BF)
                for owner in range(cols_n):
                    both[owner % 2, goal, owner // 2, at : at + extents[i], :] = made[
                        owner * extents[i] : (owner + 1) * extents[i]
                    ]
                at += extents[i]
            swap(goal).start()
            if goal > 0:
                push(goal - 1)
        push(rows_n - 1)
        for turn in range(1, n_rounds):
            next_round(turn)
        shared_here.wait()
        for step in range(1, rows_n):
            shared_from(step).wait_recv()
        total = sh_in[0].astype(F32)
        for other in range(1, rows_n):
            total = total + sh_in[other].astype(F32)
        sh_out[...] = total[:, : 2 * units]
        cut = inner // per_row
        for turn in range(per_row):
            sd_cut[turn] = total[turn * cut : (turn + 1) * cut, 2 * units :]
            downs_to(turn, lambda far: far.start(), lambda here: here.start())

        def ready(chip):
            total = mine[row, chip].astype(F32) + extra[row, chip].astype(F32)
            for step in range(1, rows_n):
                from_row(step, chip).wait_recv()
                total = total + rows_in[place.peer_row(step), chip].astype(F32)
            mine[row, chip] = total.astype(BF)

        result, drain = line_sum_loop(
            place, mine.at[row], recv, send_sems, recv_sems, 1, ready
        )

        def store(span, value):
            out_ref[span] = value

        result(0, store)
        drain()

        moves(n_rounds - 1).wait_send()
        moves(n_rounds - 1).wait_recv()
        for turn in range(per_row):
            downs_to(turn, lambda far: far.wait_send(), lambda here: here.wait())
            at_home = per_row * row + turn
            mine_here = (at_home == col) & (down_row == row)

            @pl.when(jnp.logical_not(mine_here))
            def _():
                remote(
                    sd_cut.at[0], sd_out.at[turn], sd_send.at[turn], sd_recv.at[turn],
                    (down_row, at_home),
                ).wait_recv()

        for step in range(1, rows_n):
            shared_to(step).wait_send()
        for goal in range(rows_n):
            swap(goal).wait_send()

            @pl.when(goal != row)
            def _():
                for chip in range(chips):
                    to_row(goal, chip).wait_send()

    vmem = pl.BlockSpec(memory_space=pltpu.VMEM)
    return pl.pallas_call(
        kernel,
        in_specs=[vmem] * (2 * n + 1) + [ANY] * (1 + 2 * n_rounds),
        out_specs=[vmem, vmem, vmem, ANY],
        out_shape=[
            jax.ShapeDtypeStruct(block, F32),
            jax.ShapeDtypeStruct((inner, 2 * units), F32),
            jax.ShapeDtypeStruct((per_row, inner // per_row, units), F32),
            jax.ShapeDtypeStruct((n_rounds, 2) + moved.shape, moved.dtype),
        ],
        scratch_shapes=[
            pltpu.VMEM((2, rows_n, chips) + block, BF),
            pltpu.VMEM((rows_n, chips) + block, BF),
            pltpu.VMEM((rows_n, chips) + block, BF),
            pltpu.VMEM((chips + 1,) + block, BF),
            pltpu.VMEM(shared.shape, BF),
            pltpu.VMEM((per_row, inner // per_row, units), F32),
            pltpu.VMEM((2,) + moved.shape, BF),
            pltpu.VMEM((2,) + moved.shape, BF),
            pltpu.SemaphoreType.DMA((2,)),
            pltpu.SemaphoreType.DMA((2,)),
            pltpu.SemaphoreType.DMA((rows_n,)),
            pltpu.SemaphoreType.DMA((rows_n,)),
            pltpu.SemaphoreType.DMA((rows_n, chips)),
            pltpu.SemaphoreType.DMA((rows_n, chips)),
            pltpu.SemaphoreType.DMA((chips, 1)),
            pltpu.SemaphoreType.DMA((chips + 1, 1)),
            pltpu.SemaphoreType.DMA((rows_n,)),
            pltpu.SemaphoreType.DMA((rows_n,)),
            pltpu.SemaphoreType.DMA,
            pltpu.SemaphoreType.DMA((n_rounds, 2)),
            pltpu.SemaphoreType.DMA((n_rounds, 2)),
            pltpu.SemaphoreType.DMA((per_row,)),
            pltpu.SemaphoreType.DMA((per_row,)),
        ],
        compiler_params=pltpu.CompilerParams(
            collective_id=collective_id, has_side_effects=True,
            vmem_limit_bytes=60 * 1024 * 1024,
        ),
        cost_estimate=pl.CostEstimate(
            flops=2 * 512 * 1536 * 4096, bytes_accessed=350_000_000, transcendentals=0
        ),
        name="dense_sum",
    )(*lefts, *rights, tails, shared, *[part for pair in rounds for part in pair])


def round_tables(chips):
    order, up, down = [], [], []
    for here in range(chips):
        due = {q: chips - 1 - q + here for q in range(here + 1, chips)}
        due.update({q: q + chips - 1 - here for q in range(here)})
        calls = sorted(due, key=lambda q: (due[q], -q)) + [here]
        order.append(calls)
        at = {q: i for i, q in enumerate(calls)}
        up.append([at.get(chips - 1 - t + here, 0) for t in range(chips - 1)])
        down.append([at.get(t - (chips - 1 - here), 0) for t in range(chips - 1)])
    return order, up, down


class LineRounds:
    def __init__(self, cols_n):
        self.chips = cols_n // 2
        here = lax.axis_index("col") // 2
        _, up, down = round_tables(self.chips)
        self.up_call = jnp.array(up, jnp.int32)[here]
        self.down_call = jnp.array(down, jnp.int32)[here]
        self.not_first, self.not_last = here > 0, here < self.chips - 1
        self.sums = []
        self.below = self.above = None

    def add(self, own, other):
        self.sums.append((own, other))

    def held(self, call):
        total = None
        for i, (own, other) in enumerate(self.sums):
            value = own.astype(F32) + other.astype(F32)
            total = value if i == 0 else jnp.where(call == i, value, total)
        return total

    def kept(self, turn):
        return [self.held(call[turn]).astype(BF) for call in (self.up_call, self.down_call)]

    def outgoing(self, turn):
        ups, downs = self.held(self.up_call[turn]), self.held(self.down_call[turn])
        if turn:
            ups = ups + jnp.where(self.not_first, self.below.astype(F32), 0.0)
            downs = downs + jnp.where(self.not_last, self.above.astype(F32), 0.0)
        return ups.astype(BF), downs.astype(BF)

    def arrived(self, below, above):
        self.below, self.above = below, above

    def result(self):
        own, other = self.sums[-1]
        total = own.astype(F32) + other.astype(F32)
        total = total + jnp.where(self.not_first, self.below.astype(F32), 0.0)
        return total + jnp.where(self.not_last, self.above.astype(F32), 0.0)


def routed_kernel(call, rows_n, cols_n, n_moves, *refs):
    (
        x_hbm, dy_hbm, routes_hbm, routes_t_hbm, gates_hbm, eg_ref, eu_ref, ed_ref, sgu_ref, sd_ref
    ) = refs[:10]
    up_down, refs = refs[10 : 10 + n_moves], refs[10 + n_moves :]
    (
        own_hbm, other_hbm, xs_hbm, dys_hbm, hid_ref, gg_ref, gu_ref, ggw_ref, shared_ref
    ) = refs[:9]
    arrivals, refs = refs[9 : 9 + n_moves], refs[9 + n_moves :]
    (
        x_ref, dy_ref, routes_ref, routes_t_ref, gates_ref,
        xs, dys, pick, back_pick, wide_out, wide_gx, slot_gate, stage,
        load_sems, slot_sems, own_sems, core_send, core_recv, move_send, move_recv,
    ) = refs
    place = Place(rows_n, cols_n)
    my_core = place.core
    unit = jnp.int32(0)
    for chip, calls in enumerate(round_tables(place.chips)[0]):
        unit = unit + jnp.where(place.chip == chip, calls[call], 0)
    pair = pl.ds(2 * unit, 2)
    loads = [
        pltpu.make_async_copy(src.at[pair], dst, load_sems.at[i])
        for i, (src, dst) in enumerate(
            (
                (routes_hbm, routes_ref), (routes_t_hbm, routes_t_ref), (gates_hbm, gates_ref),
                (x_hbm, x_ref), (dy_hbm, dy_ref),
            )
        )
    ]
    moves = None
    if n_moves:
        moves = Moves(place, *up_down, *arrivals, move_send, move_recv)
    e = pl.program_id(0)
    total = x_ref.shape[1]
    cap = xs.shape[1] // 2
    hidden_units = sd_ref.shape[0]
    first = place.col * EXP_DEV
    spans = [slice(at, at + 512) for at in range(0, x_ref.shape[2], 512)]

    def slot_copy(which):
        src, dst = ((xs, xs_hbm), (dys, dys_hbm))[which]
        return pltpu.make_async_copy(src, dst, slot_sems.at[which])

    def own_copy(which):
        return pltpu.make_async_copy(
            stage.at[which, my_core], own_hbm.at[which], own_sems.at[which]
        )

    def core_copy(which):
        return remote(
            stage.at[which, 1 - my_core], other_hbm.at[which], core_send.at[which],
            core_recv.at[which], (place.row, place.other),
        )

    @pl.when(e == 0)
    def _():
        for load in loads:
            load.start()
        place.greet(False)
        if n_moves:
            moves.start()
        ggw_ref[...] = jnp.zeros_like(ggw_ref)
        for load in loads:
            load.wait()
        row_at = lax.broadcasted_iota(jnp.int32, (total, total), 0)
        col_at = lax.broadcasted_iota(jnp.int32, (total, total), 1)
        upto = jnp.where(row_at <= col_at, 1.0, 0.0).astype(BF)
        since = jnp.where(row_at >= col_at, 1.0, 0.0).astype(BF)
        for core in range(2):
            gate_rows = gates_ref[core]
            route_rows = routes_ref[core]
            route_cols = routes_t_ref[core]
            hits = [
                jnp.sum(jnp.where(route_rows == first + i, 1.0, 0.0), axis=0, keepdims=True)
                for i in range(EXP_DEV)
            ]
            hits = jnp.concatenate(hits + [jnp.zeros((8 - EXP_DEV, total), F32)], axis=0)
            rank = jnp.where(hits > 0.0, mm(hits.astype(BF), upto) - 1.0, -1.0)
            hits_t = [
                jnp.sum(jnp.where(route_cols == first + i, 1.0, 0.0), axis=1, keepdims=True)
                for i in range(EXP_DEV)
            ]
            hits_t = jnp.concatenate(hits_t + [jnp.zeros((total, 8 - EXP_DEV), F32)], axis=1)
            rank_t = jnp.where(hits_t > 0.0, mm(since, hits_t.astype(BF)) - 1.0, -1.0)
            at = lax.broadcasted_iota(jnp.int32, (cap, total), 0).astype(F32)
            at_t = lax.broadcasted_iota(jnp.int32, (total, cap), 1).astype(F32)
            backs = []
            for i in range(EXP_DEV):
                here = at == rank[i : i + 1, :]
                gate_row = jnp.sum(
                    jnp.where(route_rows == first + i, gate_rows, 0.0), axis=0, keepdims=True
                )
                slot_gate[i, core * cap : (core + 1) * cap, :] = jnp.sum(
                    jnp.where(here, gate_row, 0.0), axis=1, keepdims=True
                )
                pick[core, i * cap : (i + 1) * cap, :] = jnp.where(here, 1.0, 0.0).astype(BF)
                backs.append(jnp.where(at_t == rank_t[:, i : i + 1], 1.0, 0.0).astype(BF))
            back_pick[core] = jnp.concatenate(backs, axis=1)
            for src, dst in ((x_ref, xs), (dy_ref, dys)):
                for cols in spans:
                    got = mm(pick[core], src[core, :, cols]).astype(BF)
                    for i in range(EXP_DEV):
                        dst[i, core * cap : (core + 1) * cap, cols] = got[
                            i * cap : (i + 1) * cap
                        ]
        slot_copy(0).start()
        slot_copy(1).start()

    rows_x = xs[e]
    gate_part = mm(rows_x, eg_ref[0])
    up_part = mm(rows_x, eu_ref[0])
    act, slope = silu_parts(gate_part)
    grad_hidden = mm_nt(dys[e], ed_ref[0])
    hidden = (act * up_part).astype(BF).astype(F32)
    weight = slot_gate[e]
    gated = (hidden * weight).astype(BF)
    hid_ref[0] = gated
    slot_ggw = jnp.sum(hidden * grad_hidden, axis=1, keepdims=True)
    grad_hidden = grad_hidden * weight
    geg = (grad_hidden * up_part * slope).astype(BF)
    geu = (grad_hidden * act).astype(BF)
    gg_ref[0] = geg
    gu_ref[0] = geu
    rows = pl.ds(pl.multiple_of(e * cap, cap), cap)
    for cols in spans:
        made = mm(gated, ed_ref[0, :, cols]).astype(BF)
        back = (mm_nt(geg, eg_ref[0, cols, :]) + mm_nt(geu, eu_ref[0, cols, :])).astype(BF)
        for core in range(2):
            wide_out[core, rows, cols] = made[core * cap : (core + 1) * cap]
            wide_gx[core, rows, cols] = back[core * cap : (core + 1) * cap]
    sub = lax.broadcasted_iota(jnp.int32, (8, total), 0)
    for core in range(2):
        back = jnp.sum(
            pick[core, rows, :].astype(F32) * slot_ggw[core * cap : (core + 1) * cap],
            axis=0,
            keepdims=True,
        )
        ggw_ref[core] = jnp.where(sub == e, back, ggw_ref[core])

    @pl.when(e == EXP_DEV - 1)
    def _():
        for core in range(2):
            both = mm(x_ref[core], sgu_ref[...])
            s_act, s_slope = silu_parts(both[:, :hidden_units])
            s_up = both[:, hidden_units:]
            s_hidden = (s_act * s_up).astype(BF)
            grad_shared = mm_nt(dy_ref[core], sd_ref[...])
            grad_both = jnp.concatenate(
                [(grad_shared * s_up * s_slope).astype(BF), (grad_shared * s_act).astype(BF)],
                axis=1,
            )
            for cols in spans:
                value = mm(back_pick[core], wide_gx[core, :, cols])
                value = value + mm_nt(grad_both, sgu_ref[cols, :])
                stage[1, core, :, cols] = value.astype(BF)
                value = mm(back_pick[core], wide_out[core, :, cols])
                value = value + mm(s_hidden, sd_ref[:, cols])
                stage[0, core, :, cols] = value.astype(BF)
                made = mm_tn(x_ref[core, :, cols], grad_both)
                made_d = mm_tn(dy_ref[core, :, cols], s_hidden)
                if core == 0:
                    shared_ref[cols, : 2 * hidden_units] = made
                    shared_ref[cols, 2 * hidden_units :] = made_d
                else:
                    shared_ref[cols, : 2 * hidden_units] += made
                    shared_ref[cols, 2 * hidden_units :] += made_d
        for which in (1, 0):
            core_copy(which).start()
            own_copy(which).start()
        slot_copy(0).wait()
        slot_copy(1).wait()
        if n_moves:
            moves.wait_send()
            moves.wait_recv()
        for which in (1, 0):
            own_copy(which).wait()
            core_copy(which).wait_send()
            core_copy(which).wait_recv()


def routed(call, rows_n, x_all, dy_all, routes, routes_t, gates, egate, eup, edown, sgu, sdown, moves):
    cols_n, total, width = x_all.shape
    cap = 4 * total * TOP // (3 * EXP_DEV * cols_n)
    slots = 2 * cap
    ffn = egate.shape[2]
    hidden_units = sdown.shape[0]

    def each(*shape):
        return pl.BlockSpec((1,) + shape, lambda e: (e,) + (0,) * len(shape))

    def whole(*shape):
        return pl.BlockSpec(
            shape, lambda e: (0,) * len(shape), pipeline_mode=pl.Buffered(1)
        )

    slot_block = each(slots, ffn)
    return pl.pallas_call(
        functools.partial(routed_kernel, call, rows_n, cols_n, len(moves)),
        grid=(EXP_DEV,),
        in_specs=[ANY] * 5
        + [
            each(width, ffn), each(width, ffn), each(ffn, width), whole(*sgu.shape),
            whole(*sdown.shape),
        ]
        + [ANY] * len(moves),
        out_specs=[
            ANY, ANY, ANY, ANY, slot_block, slot_block, slot_block,
            whole(2, 8, total), whole(width, 3 * hidden_units),
        ]
        + [ANY] * len(moves),
        out_shape=[
            jax.ShapeDtypeStruct((2, total, width), BF),
            jax.ShapeDtypeStruct((2, total, width), BF),
            jax.ShapeDtypeStruct((EXP_DEV, slots, width), BF),
            jax.ShapeDtypeStruct((EXP_DEV, slots, width), BF),
            jax.ShapeDtypeStruct((EXP_DEV, slots, ffn), BF),
            jax.ShapeDtypeStruct((EXP_DEV, slots, ffn), BF),
            jax.ShapeDtypeStruct((EXP_DEV, slots, ffn), BF),
            jax.ShapeDtypeStruct((2, 8, total), F32),
            jax.ShapeDtypeStruct((width, 3 * hidden_units), F32),
        ]
        + [jax.ShapeDtypeStruct(a.shape, a.dtype) for a in moves],
        scratch_shapes=[
            pltpu.VMEM((2, total, width), BF),
            pltpu.VMEM((2, total, width), BF),
            pltpu.VMEM((2, 8, total), jnp.int32),
            pltpu.VMEM((2, total, 8), jnp.int32),
            pltpu.VMEM((2, 8, total), F32),
            pltpu.VMEM((EXP_DEV, slots, width), BF),
            pltpu.VMEM((EXP_DEV, slots, width), BF),
            pltpu.VMEM((2, EXP_DEV * cap, total), BF),
            pltpu.VMEM((2, total, EXP_DEV * cap), BF),
            pltpu.VMEM((2, EXP_DEV * cap, width), BF),
            pltpu.VMEM((2, EXP_DEV * cap, width), BF),
            pltpu.VMEM((EXP_DEV, slots, 1), F32),
            pltpu.VMEM((2, 2, total, width), BF),
            pltpu.SemaphoreType.DMA((5,)),
            pltpu.SemaphoreType.DMA((2,)),
            pltpu.SemaphoreType.DMA((2,)),
            pltpu.SemaphoreType.DMA((2,)),
            pltpu.SemaphoreType.DMA((2,)),
            pltpu.SemaphoreType.DMA((2,)),
            pltpu.SemaphoreType.DMA((2,)),
        ],
        compiler_params=pltpu.CompilerParams(
            collective_id=4 + call, has_side_effects=True, vmem_limit_bytes=60 * 1024 * 1024
        ),
        cost_estimate=pl.CostEstimate(
            flops=24_000_000_000, bytes_accessed=100_000_000, transcendentals=0
        ),
        name="routed",
    )(
        x_all, dy_all, routes, routes_t, gates, egate, eup, edown, sgu, sdown, *moves
    )


def expert_grads_kernel(units_n, rows_n, cut_left, *refs):
    left, right, out_ref = refs[:units_n], refs[units_n : 2 * units_n], refs[-1]
    inner = (left if cut_left else right)[0].shape[2] // rows_n

    def joined(parts, cols=slice(None)):
        return jnp.concatenate([part[0, :, cols] for part in parts], axis=0)

    other = joined(right if cut_left else left)
    for row in range(rows_n):
        cut = joined(left if cut_left else right, slice(row * inner, (row + 1) * inner))
        pair = (cut, other) if cut_left else (other, cut)
        out_ref[row, 0] = mm_tn(*pair).astype(BF)


def expert_grads(left, right, rows_n, cut_left):
    slots = left[0].shape[1]
    units_n = len(left)
    sizes = [left[0].shape[2], right[0].shape[2]]
    specs = [
        pl.BlockSpec((1, slots, size), lambda e: (e, 0, 0)) for size in sizes for _ in left
    ]
    sizes[0 if cut_left else 1] //= rows_n
    return pl.pallas_call(
        functools.partial(expert_grads_kernel, units_n, rows_n, cut_left),
        grid=(EXP_DEV,),
        in_specs=specs,
        out_specs=pl.BlockSpec((rows_n, 1) + tuple(sizes), lambda e: (0, e, 0, 0)),
        out_shape=jax.ShapeDtypeStruct((rows_n, EXP_DEV) + tuple(sizes), BF),
        compiler_params=pltpu.CompilerParams(vmem_limit_bytes=60 * 1024 * 1024),
        cost_estimate=pl.CostEstimate(
            flops=7_000_000_000, bytes_accessed=30_000_000, transcendentals=0
        ),
        name="expert_grads",
    )(*left, *right)


def on_device(
    tokens,
    g_attn,
    w_query,
    key_projection,
    value_projection,
    w_out,
    g_moe,
    w_router,
    e_gate,
    e_up,
    e_down,
    s_gate,
    s_up,
    s_down,
    routes,
    deal,
    lengths,
    cotangent,
):
    rows_n = lax.axis_size("row")
    cols_n = lax.axis_size("col")
    row_here = lax.axis_index("row")
    col_here = lax.axis_index("col")
    both = ("row", "col")
    total = tokens.shape[0]
    width = MODEL_WIDTH
    experts = EXP_DEV * cols_n

    q_w, k_w = w_query.shape[1], key_projection.shape[1]
    inner = w_query.shape[0]
    gains = jnp.stack([g_attn, g_moe])
    gains = jnp.pad(gains, ((0, 0), (0, inner - gains.shape[1])))
    tail = jnp.concatenate([w_router.T, gains], axis=0)
    tail = jnp.pad(tail, ((0, 16 - tail.shape[0]), (0, 0)))
    bundle = jnp.concatenate(
        [w_query.T, key_projection.T, value_projection.T, w_out.T, tail], axis=0
    )
    routes_t = jnp.pad(routes.T, ((0, 8 - TOP), (0, 0)), constant_values=-1)
    units = s_gate.shape[1]
    shared = jnp.concatenate([s_gate, s_up], axis=1)
    per_row = s_down.shape[0] // units
    downs = s_down.reshape(per_row, units, s_down.shape[1])
    full, dy_all, routes_all, sgu, sdown = first_gather(
        bundle, cotangent, routes_t, shared, downs, 0, rows_n, cols_n
    )
    sdown = jnp.swapaxes(sdown, 0, 1).reshape(units, width)
    sgu = sgu.reshape(width, 2 * units)

    t_at = 2 * q_w + 2 * k_w
    extents = [q_w, k_w, k_w, q_w, 16]
    n_gain = g_attn.shape[0]
    gains = full[:, :, t_at + EXP_DEV : t_at + EXP_DEV + 2, :n_gain].transpose(2, 0, 1, 3)
    gains = gains.reshape(2, width).astype(F32)
    egate = lax.all_gather(e_gate, "row", axis=1, tiled=True)
    eup = lax.all_gather(e_up, "row", axis=1, tiled=True)
    edown = lax.all_gather(e_down, "row", axis=2, tiled=True)
    own_lens = lengths[deal.reshape(-1) * cols_n + col_here, row_here]
    seq_ends = jnp.cumsum(own_lens)
    places = jnp.arange(total, dtype=jnp.int32)
    segment = jnp.sum((places[:, None] >= seq_ends[None, :]).astype(jnp.int32), axis=1)

    (
        normed_one, queries, keys, values, mixed, log_totals, after_attn, normed_two, scale_one,
        scale_two, gates, gates_t,
    ) = block_start(tokens, full, extents, gains, segment, routes)

    x_all, gates_all = line_gather([normed_two, gates_t], 1, rows_n, cols_n)
    chips = cols_n // 2
    my_order = jnp.array(round_tables(chips)[0], jnp.int32)[col_here // 2]
    routes_rows = jnp.swapaxes(routes_all, 1, 2)
    gx_sum, moe_sum = LineRounds(cols_n), LineRounds(cols_n)
    saved, ggw, grad_sh = [], 0.0, 0.0
    for call in range(chips):
        moves = gx_sum.outgoing(call - 1) if call else ()
        own, other, *keep = routed(
            call, rows_n, x_all, dy_all, routes_all, routes_rows, gates_all, egate, eup, edown,
            sgu, sdown, moves,
        )
        saved.append(keep[:5])
        ggw_part, sh_part, *arrivals = keep[5:]
        if call:
            gx_sum.arrived(*arrivals)
        grad_sh = grad_sh + sh_part
        is_unit = jnp.arange(chips, dtype=jnp.int32)[:, None, None, None] == my_order[call]
        ggw = ggw + jnp.where(is_unit, ggw_part[None], 0.0)
        gx_sum.add(own[1], other[1])
        moe_sum.add(own[0], other[0])
    xs, dys, hid, gg, gu = zip(*saved)
    grad_edown = expert_grads(hid, dys, rows_n, False)
    grad_egate = expert_grads(xs, gg, rows_n, True)
    grad_eup = expert_grads(xs, gu, rows_n, True)
    ggw = ggw.reshape(cols_n, 8, total)[:, :EXP_DEV]

    ggw_home = lax.all_to_all(ggw, "col", split_axis=0, concat_axis=0, tiled=True)
    grad_tokens, gq, gk, gv, grad_attn_b, logits_left, gain_grads = block_end(
        tokens, cotangent, full, extents, gains, segment, routes, gates,
        ggw_home.reshape(experts, total),
        (gx_sum.sums[-1][0], gx_sum.sums[-1][1], gx_sum.below, gx_sum.above),
        queries, keys, values, log_totals, after_attn, scale_one, scale_two,
    )

    rounds = [moe_sum.outgoing(0)] + [moe_sum.kept(turn) for turn in range(1, chips - 1)]

    def gain_rows(grad):
        part = grad.reshape(rows_n, cols_n, 1, n_gain)
        return jnp.pad(part, ((0, 0),) * 3 + ((0, inner - n_gain),))

    tails = jnp.concatenate([gain_rows(gain_grads[0]), gain_rows(gain_grads[1])], axis=2)
    tails = jnp.pad(tails, ((0, 0), (0, 0), (EXP_DEV, 16 - EXP_DEV - 2), (0, 0)))
    tails = tails.reshape(rows_n, cols_n * 16, inner)
    grads_sh = grad_sh.astype(BF).reshape(rows_n, inner, 3 * units)
    dense, dense_sh, sd_parts, arrivals = dense_sum(
        [gq, gk, gv, grad_attn_b, logits_left],
        [normed_one, normed_one, normed_one, mixed, normed_two],
        tails, grads_sh, rounds, 2, rows_n, cols_n,
    )
    moe_sum.arrived(arrivals[-1, 0], arrivals[-1, 1])
    output = (after_attn + moe_sum.result()).astype(BF)
    out_wq = dense[:q_w].T
    out_wk = dense[q_w : q_w + k_w].T
    out_wv = dense[q_w + k_w : q_w + 2 * k_w].T
    out_wo = dense[q_w + 2 * k_w : t_at].T
    out_router = dense[t_at : t_at + EXP_DEV].T
    out_g_attn = dense[t_at + EXP_DEV, :n_gain]
    out_g_moe = dense[t_at + EXP_DEV + 1, :n_gain]
    out_sg = dense_sh[:, :units]
    out_su = dense_sh[:, units:]
    out_sd = sd_parts.transpose(0, 2, 1).reshape(per_row * units, inner // per_row)

    def row_sum(grad):
        return lax.psum_scatter(grad, "row", scatter_dimension=0).astype(F32)

    out_eg = row_sum(grad_egate)
    out_eu = row_sum(grad_eup)
    out_ed = row_sum(grad_edown)
    return (
        output,
        grad_tokens,
        out_g_attn,
        out_wq,
        out_wk,
        out_wv,
        out_wo,
        out_g_moe,
        out_router,
        out_eg,
        out_eu,
        out_ed,
        out_sg,
        out_su,
        out_sd,
    )


def solution(mesh):
    both = P(("row", "col"), None)
    flat = P(("row", "col"))
    tile = P("row", "col")
    wide = P("col", "row", None)
    down = P("col", None, "row")
    return jax.shard_map(
        on_device,
        mesh=mesh,
        in_specs=(
            both, flat, tile, tile, tile, tile, flat, tile, wide, wide, down,
            tile, tile, tile, both, both, P(), both,
        ),
        out_specs=(
            both, both, flat, tile, tile, tile, tile, flat, tile, wide, wide, down,
            tile, tile, tile,
        ),
        check_vma=False,
    )
```

```python
import functools

import jax
import jax.numpy as jnp
from jax import lax
from jax.experimental import pallas as pl
from jax.experimental.pallas import tpu as pltpu
from jax.sharding import PartitionSpec as P

MODEL_WIDTH = 1536
QUERY_HEADS = 12
KEY_VALUE_HEADS = 4
GROUP = QUERY_HEADS // KEY_VALUE_HEADS
HEAD_SIZE = 128
TOP = 6
EXP_DEV = 4

norm_eps = 1e-05
masked_score = -1e30
BF = jnp.bfloat16
F32 = jnp.float32


def rms_scale(rows):
    return lax.rsqrt(jnp.mean(rows * rows, axis=-1, keepdims=True) + norm_eps)


def silu_parts(values):
    sigmoid_of = jax.nn.sigmoid(values)
    return (values * sigmoid_of, sigmoid_of * (1.0 + values * (1.0 - sigmoid_of)))


def norm_back(grad_normed, unit_rows, scale_rows, gain):
    grad_unit = grad_normed * gain
    grad_rows = scale_rows * (
        grad_unit - unit_rows * jnp.mean(grad_unit * unit_rows, axis=-1, keepdims=True)
    )
    return (grad_rows, jnp.sum(grad_normed * unit_rows, axis=0))


def mm(left, right):
    return jnp.dot(left, right, preferred_element_type=F32)


def mm_nt(left, right):
    return lax.dot_general(left, right, (((1,), (1,)), ((), ())), preferred_element_type=F32)


def mm_tn(left, right):
    return lax.dot_general(left, right, (((0,), (0,)), ((), ())), preferred_element_type=F32)


def ein(spec, a, b):
    return jnp.einsum(spec, a, b, preferred_element_type=F32)


def allowed_mask(seg_col, seg_row):
    total = seg_col.shape[0]
    q_at = lax.broadcasted_iota(jnp.int32, (total, total), 0)
    k_at = lax.broadcasted_iota(jnp.int32, (total, total), 1)
    return (seg_col == seg_row) & (k_at <= q_at)


def attend_forward_group(h, q_ref, k_ref, v_ref, allowed, mixed_ref, lse_ref):
    here = pl.ds(pl.multiple_of(h * HEAD_SIZE, HEAD_SIZE), HEAD_SIZE)
    keys = k_ref[:, here]
    values = v_ref[:, here]
    for g in range(GROUP):
        at = pl.multiple_of((h * GROUP + g) * HEAD_SIZE, HEAD_SIZE)
        cols = pl.ds(at, HEAD_SIZE)
        scores = mm_nt(q_ref[:, cols], keys) * HEAD_SIZE ** (-0.5)
        scores = jnp.where(allowed, scores, masked_score)
        peak = jnp.max(scores, axis=-1, keepdims=True)
        raw = jnp.exp(scores - peak)
        total = jnp.sum(raw, axis=-1, keepdims=True)
        probs = (raw * (1.0 / total)).astype(BF)
        mixed_ref[:, cols] = mm(probs, values).astype(BF)
        lse_ref[h, :, g : g + 1] = peak + jnp.log(total)


def attend_backward_group(h, q_ref, k_ref, v_ref, gm_ref, allowed, lse_ref, gq_ref, gk_ref, gv_ref):
    here = pl.ds(pl.multiple_of(h * HEAD_SIZE, HEAD_SIZE), HEAD_SIZE)
    keys = k_ref[:, here]
    values = v_ref[:, here]
    scale = HEAD_SIZE ** (-0.5)
    grad_key = grad_value = None
    for g in range(GROUP):
        at = pl.multiple_of((h * GROUP + g) * HEAD_SIZE, HEAD_SIZE)
        cols = pl.ds(at, HEAD_SIZE)
        query = q_ref[:, cols]
        grad_mixed = gm_ref[:, cols]
        scores = mm_nt(query, keys) * scale
        probs = jnp.where(allowed, jnp.exp(scores - lse_ref[h, :, g : g + 1]), 0.0)
        grad_probs = mm_nt(grad_mixed, values)
        inner = jnp.sum(probs * grad_probs, axis=-1, keepdims=True)
        grad_scores = (probs * (grad_probs - inner)).astype(BF)
        gq_ref[:, cols] = (mm(grad_scores, keys) * scale).astype(BF)
        part_key = mm_tn(grad_scores, query)
        part_value = mm_tn(probs.astype(BF), grad_mixed)
        grad_key = part_key if g == 0 else grad_key + part_key
        grad_value = part_value if g == 0 else grad_value + part_value
    gk_ref[:, here] = (grad_key * scale).astype(BF)
    gv_ref[:, here] = grad_value.astype(BF)


class DenseWeights:
    def __init__(self, full, extents):
        self.rows_n, self.cols_n, _, self.inner = full.shape
        self.extents = extents
        self.width = self.rows_n * self.inner
        self.cut = self.inner % 128 == 0
        self.operands = [full]
        if not self.cut:
            self.operands = []
            at = 0
            for extent in extents:
                part = full[:, :, at : at + extent].transpose(1, 2, 0, 3)
                self.operands.append(part.reshape(self.cols_n, extent, self.width))
                at += extent
        self.count = len(self.operands)
        self.scratch = [
            pltpu.VMEM((self.cols_n, extent, self.width), BF) for extent in extents
        ] + [pltpu.SemaphoreType.DMA((len(extents), self.rows_n))]

    def copies(self, sources, held, sems):
        made = []
        at = 0
        for part, extent in enumerate(self.extents):
            if self.cut:
                made.append(
                    [
                        pltpu.make_async_copy(
                            sources[0].at[r, :, pl.ds(at, extent), :],
                            held[part].at[:, :, pl.ds(r * self.inner, self.inner)],
                            sems.at[part, r],
                        )
                        for r in range(self.rows_n)
                    ]
                )
            else:
                made.append(
                    [pltpu.make_async_copy(sources[part], held[part], sems.at[part, 0])]
                )
            at += extent
        return made


ROW_STEP = 64


def flat(value):
    return value.reshape(value.shape[0] * value.shape[1], value.shape[2])


def route_columns(routes):
    return lax.div(routes, EXP_DEV) * 16 + lax.rem(routes, EXP_DEV)


def column_spans(width, count=KEY_VALUE_HEADS):
    step = width // count
    return [slice(at, at + step) for at in range(0, width, step)]


def block_start(tokens, full, extents, gains, segment, routes):
    total, width = tokens.shape
    weights = DenseWeights(full, extents)
    n = weights.count
    per_group = weights.cols_n // KEY_VALUE_HEADS

    def kernel(*refs):
        sources = refs[:n]
        (
            tok_ref, gain_ref, segc_ref, segr_ref, routes_ref,
            n1_ref, q_ref, k_ref, v_ref, mixed_ref, lse_ref, after_ref, n2_ref, s1_ref, s2_ref,
            gates_ref, gates_t_ref, *held, sems,
        ) = refs[n:]
        copies = weights.copies(sources, held, sems)
        for part in copies:
            for copy in part:
                copy.start()

        @pl.loop(0, total // ROW_STEP)
        def _(step):
            rows = pl.ds(pl.multiple_of(step * ROW_STEP, ROW_STEP), ROW_STEP)
            x = tok_ref[rows].astype(F32)
            scale = rms_scale(x)
            n1_ref[rows] = (x * scale * gain_ref[0:1]).astype(BF)
            s1_ref[rows] = scale

        for part in copies:
            for copy in part:
                copy.wait()
        normed = n1_ref[...]
        for h, cols in enumerate(column_spans(width)):
            mine = slice(h * per_group, (h + 1) * per_group)
            q_ref[:, cols] = mm_nt(normed, flat(held[0][mine])).astype(BF)
        k_ref[...] = mm_nt(normed, flat(held[1][...])).astype(BF)
        v_ref[...] = mm_nt(normed, flat(held[2][...])).astype(BF)
        allowed = allowed_mask(segc_ref[...], segr_ref[...])

        @pl.loop(0, KEY_VALUE_HEADS)
        def _(h):
            attend_forward_group(h, q_ref, k_ref, v_ref, allowed, mixed_ref, lse_ref)

        mixed = mixed_ref[...]
        for h, cols in enumerate(column_spans(width)):
            mine = slice(h * per_group, (h + 1) * per_group)
            after_ref[:, cols] = tok_ref[:, cols].astype(F32) + mm_nt(mixed, flat(held[3][mine]))

        @pl.loop(0, total // ROW_STEP)
        def _(step):
            rows = pl.ds(pl.multiple_of(step * ROW_STEP, ROW_STEP), ROW_STEP)
            after = after_ref[rows]
            scale = rms_scale(after)
            n2_ref[rows] = (after * scale * gain_ref[1:2]).astype(BF)
            s2_ref[rows] = scale

        logits = mm_nt(n2_ref[...], flat(held[4][...]))
        lane = lax.broadcasted_iota(jnp.int32, logits.shape, 1)
        goal = route_columns(routes_ref[...])
        chosen = [
            jnp.sum(jnp.where(lane == goal[:, i : i + 1], logits, 0.0), axis=1, keepdims=True)
            for i in range(TOP)
        ]
        peak = functools.reduce(jnp.maximum, chosen)
        raw = [jnp.exp(value - peak) for value in chosen]
        whole = functools.reduce(jnp.add, raw)
        lane = lax.broadcasted_iota(jnp.int32, (total, 128), 1)
        wide = jnp.zeros((total, 128), F32)
        for i in range(TOP):
            wide = jnp.where(lane == i, raw[i] / whole, wide)
        gates_ref[...] = wide[:, :8]
        gates_t_ref[...] = wide.T[:8]

    vmem = pl.BlockSpec(memory_space=pltpu.VMEM)
    kv = KEY_VALUE_HEADS * HEAD_SIZE
    shapes = [
        ((total, width), BF), ((total, width), BF), ((total, kv), BF), ((total, kv), BF),
        ((total, width), BF), ((KEY_VALUE_HEADS, total, GROUP), F32), ((total, width), F32),
        ((total, width), BF), ((total, 1), F32), ((total, 1), F32), ((total, 8), F32),
        ((8, total), F32),
    ]
    return pl.pallas_call(
        kernel,
        in_specs=[pl.BlockSpec(memory_space=pl.ANY)] * n + [vmem] * 5,
        out_specs=[vmem] * len(shapes),
        out_shape=[jax.ShapeDtypeStruct(shape, kind) for shape, kind in shapes],
        scratch_shapes=weights.scratch,
        compiler_params=pltpu.CompilerParams(vmem_limit_bytes=60 * 1024 * 1024),
        cost_estimate=pl.CostEstimate(
            flops=10_000_000_000, bytes_accessed=30_000_000, transcendentals=0
        ),
        name="block_start",
    )(*weights.operands, tokens, gains, segment[:, None], segment[None, :], routes)


def block_end(
    tokens, cotangent, full, extents, gains, segment, routes, gates, ggw, sums,
    queries, keys, values, log_totals, after, scale_one, scale_two,
):
    total, width = tokens.shape
    weights = DenseWeights(full, extents)
    n = weights.count
    chips = weights.cols_n // 2
    experts = ggw.shape[0]

    def kernel(*refs):
        sources = refs[:n]
        (
            tok_ref, dy_ref, gain_ref, segc_ref, segr_ref, routes_ref, gates_ref, ggw_ref,
            own_ref, other_ref, below_ref, above_ref, q_ref, k_ref, v_ref, lse_ref, after_ref,
            s1_ref, s2_ref,
            gtok_ref, gq_ref, gk_ref, gv_ref, gab_ref, glog_ref, ggain_ref,
            acc, grad_mixed, *held, sems,
        ) = refs[n:]
        copies = weights.copies(sources, held, sems)
        for part in (4, 3, 0, 1, 2):
            for copy in copies[part]:
                copy.start()
        chip = lax.div(lax.axis_index("col"), 2)
        not_first, not_last = chip > 0, chip < chips - 1

        per_expert = jnp.pad(ggw_ref[...], ((0, 128 - experts), (0, 0))).T
        lane = lax.broadcasted_iota(jnp.int32, (total, 128), 1)
        goals = routes_ref[...]
        weight = [gates_ref[:, i : i + 1] for i in range(TOP)]
        grads = [
            jnp.sum(jnp.where(lane == goals[:, i : i + 1], per_expert, 0.0), axis=1, keepdims=True)
            for i in range(TOP)
        ]
        mean = functools.reduce(jnp.add, [w * g for w, g in zip(weight, grads)])
        goals = route_columns(goals)
        lane = lax.broadcasted_iota(jnp.int32, glog_ref.shape, 1)
        spread = jnp.zeros(glog_ref.shape, F32)
        for i in range(TOP):
            spread = jnp.where(lane == goals[:, i : i + 1], weight[i] * (grads[i] - mean), spread)
        glog = spread.astype(BF)
        glog_ref[...] = glog
        for copy in copies[4]:
            copy.wait()
        for cols in column_spans(width):
            acc[:, cols] = mm(glog, flat(held[4][:, :, cols]))
        ggain_ref[...] = jnp.zeros_like(ggain_ref)

        @pl.loop(0, total // ROW_STEP)
        def _(step):
            rows = pl.ds(pl.multiple_of(step * ROW_STEP, ROW_STEP), ROW_STEP)
            grad = acc[rows] + own_ref[rows].astype(F32) + other_ref[rows].astype(F32)
            grad = grad + jnp.where(not_first, below_ref[rows].astype(F32), 0.0)
            grad = grad + jnp.where(not_last, above_ref[rows].astype(F32), 0.0)
            scale = s2_ref[rows]
            unit = after_ref[rows] * scale
            back, gain = norm_back(grad, unit, scale, gain_ref[1:2])
            ggain_ref[1:2] += gain[None]
            value = dy_ref[rows].astype(F32) + back
            acc[rows] = value
            gab_ref[rows] = value.astype(BF)

        for copy in copies[3]:
            copy.wait()
        rounded = gab_ref[...]
        for cols in column_spans(width):
            grad_mixed[:, cols] = mm(rounded, flat(held[3][:, :, cols])).astype(BF)
        allowed = allowed_mask(segc_ref[...], segr_ref[...])

        @pl.loop(0, KEY_VALUE_HEADS)
        def _(h):
            attend_backward_group(
                h, q_ref, k_ref, v_ref, grad_mixed, allowed, lse_ref, gq_ref, gk_ref, gv_ref
            )

        for part in range(3):
            for copy in copies[part]:
                copy.wait()
        for cols in column_spans(width):
            gtok_ref[:, cols] = (
                mm(gq_ref[...], flat(held[0][:, :, cols]))
                + mm(gk_ref[...], flat(held[1][:, :, cols]))
                + mm(gv_ref[...], flat(held[2][:, :, cols]))
            )

        @pl.loop(0, total // ROW_STEP)
        def _(step):
            rows = pl.ds(pl.multiple_of(step * ROW_STEP, ROW_STEP), ROW_STEP)
            scale = s1_ref[rows]
            unit = tok_ref[rows].astype(F32) * scale
            back, gain = norm_back(gtok_ref[rows], unit, scale, gain_ref[0:1])
            ggain_ref[0:1] += gain[None]
            gtok_ref[rows] = acc[rows] + back

    vmem = pl.BlockSpec(memory_space=pltpu.VMEM)
    kv = KEY_VALUE_HEADS * HEAD_SIZE
    shapes = [
        ((total, width), F32), ((total, width), BF), ((total, kv), BF), ((total, kv), BF),
        ((total, width), BF), ((total, weights.cols_n * 16), BF), ((2, width), F32),
    ]
    args = (
        tokens, cotangent, gains, segment[:, None], segment[None, :], routes, gates, ggw, *sums,
        queries, keys, values, log_totals, after, scale_one, scale_two,
    )
    return pl.pallas_call(
        kernel,
        in_specs=[pl.BlockSpec(memory_space=pl.ANY)] * n + [vmem] * len(args),
        out_specs=[vmem] * len(shapes),
        out_shape=[jax.ShapeDtypeStruct(shape, kind) for shape, kind in shapes],
        scratch_shapes=[pltpu.VMEM((total, width), F32), pltpu.VMEM((total, width), BF)]
        + weights.scratch,
        compiler_params=pltpu.CompilerParams(vmem_limit_bytes=60 * 1024 * 1024),
        cost_estimate=pl.CostEstimate(
            flops=20_000_000_000, bytes_accessed=40_000_000, transcendentals=0
        ),
        name="block_end",
    )(*weights.operands, *args)


def remote(src, dst, send_sem, recv_sem, device):
    return pltpu.make_async_remote_copy(
        src_ref=src,
        dst_ref=dst,
        send_sem=send_sem,
        recv_sem=recv_sem,
        device_id=device,
        device_id_type=pl.DeviceIdType.MESH,
    )


class Place:
    def __init__(self, rows_n, cols_n):
        self.rows_n = rows_n
        self.chips = cols_n // 2
        self.row = lax.axis_index("row")
        self.col = lax.axis_index("col")
        self.chip = lax.div(self.col, 2)
        self.core = lax.rem(self.col, 2)
        self.other = self.col + 1 - 2 * self.core

    def peer_row(self, step):
        return lax.rem(self.row + step, self.rows_n)

    def square(self):
        across = self.row + 1 - 2 * lax.rem(self.row, 2)
        along = lax.rem(self.row + 2, 4)
        return across, along, along + 1 - 2 * lax.rem(along, 2)

    def greet(self, with_rows, downs_back=0):
        barrier = pltpu.get_barrier_semaphore()

        def hello(row, col):
            pl.semaphore_signal(
                barrier, inc=1, device_id=(row, col), device_id_type=pl.DeviceIdType.MESH
            )

        hello(self.row, self.other)

        @pl.when(self.chip > 0)
        def _():
            hello(self.row, self.col - 2)

        @pl.when(self.chip < self.chips - 1)
        def _():
            hello(self.row, self.col + 2)

        count = (
            1
            + (self.chip > 0).astype(jnp.int32)
            + (self.chip < self.chips - 1).astype(jnp.int32)
        )
        if with_rows:
            for step in range(1, self.rows_n):
                hello(self.peer_row(step), self.col)
            count = count + (self.rows_n - 1)
        if downs_back:
            goal = lax.div(self.col, downs_back)
            for turn in range(downs_back):
                goal_col = downs_back * self.row + turn

                @pl.when(jnp.logical_not((goal == self.row) & (goal_col == self.col)))
                def _():
                    hello(goal, goal_col)

            count = count + downs_back - (goal == self.row).astype(jnp.int32)
        pl.semaphore_wait(barrier, count)


class Moves:
    def __init__(self, place, up, down, from_below, from_above, send_sems, recv_sems):
        self.place = place
        self.copies = [
            remote(
                src, dst, send_sems.at[which], recv_sems.at[which],
                (place.row, place.col + way),
            )
            for which, (src, dst, way) in enumerate(
                ((up, from_below, 2), (down, from_above, -2))
            )
        ]
        self.ends = (place.chip < place.chips - 1, place.chip > 0)

    def start(self):
        for which in range(2):

            @pl.when(self.ends[which])
            def _():
                self.copies[which].start()

    def wait_send(self):
        for which in range(2):

            @pl.when(self.ends[which])
            def _():
                self.copies[which].wait_send()

    def wait_recv(self):
        for which in range(2):

            @pl.when(self.ends[1 - which])
            def _():
                self.copies[which].wait_recv()


class RoundStart:
    def __init__(self, place, call_refs, held, came, held_sems, came_sems):
        self.place, self.call_refs = place, call_refs
        self.held, self.came = held, came
        self.held_sems, self.came_sems = held_sems, came_sems
        self.tables = round_tables(place.chips)[1:]

    def bring(self, which, call):
        own, other = self.call_refs[2 * call], self.call_refs[2 * call + 1]
        return (
            pltpu.make_async_copy(own.at[1], self.held.at[which], self.held_sems.at[which]),
            pltpu.make_async_copy(other.at[1], self.came.at[which], self.came_sems.at[which]),
        )

    def add_came(self, which):
        part = self.came.shape[1] // 4
        for at in range(0, self.came.shape[1], part):
            span = slice(at, at + part)
            self.held[which, span] = (
                self.held[which, span].astype(F32) + self.came[which, span].astype(F32)
            ).astype(BF)

    def prepare(self, turn):
        for which in range(2):
            call = jnp.int32(0)
            for chip in range(self.place.chips):
                number = self.tables[which][chip][turn]
                call = call + jnp.where(self.place.chip == chip, number, 0)
            for i in range(turn + 1):

                @pl.when(call == i)
                def _():
                    for copy in self.bring(which, i):
                        copy.start()

        for which in range(2):
            for copy in self.bring(which, 0):
                copy.wait()
            self.add_came(which)

    def add(self, before):
        comes = (self.place.chip > 0, self.place.chip < self.place.chips - 1)

        def copy(which):
            return pltpu.make_async_copy(
                before[which], self.came.at[which], self.came_sems.at[which]
            )

        for which in range(2):

            @pl.when(comes[which])
            def _():
                copy(which).start()

        for which in range(2):

            @pl.when(comes[which])
            def _():
                copy(which).wait()
                self.add_came(which)

    def moves(self, after, send_sems, recv_sems):
        return Moves(
            self.place, self.held.at[0], self.held.at[1], *after, send_sems, recv_sems
        )

    @staticmethod
    def scratch(block):
        return [
            pltpu.VMEM((2,) + block, BF),
            pltpu.VMEM((2,) + block, BF),
            pltpu.SemaphoreType.DMA((2,)),
            pltpu.SemaphoreType.DMA((2,)),
        ]


class LineGather:
    def __init__(self, place, src, dst, core_sems, line_sems, recv_sems, local_sem):
        self.at = place
        self.src, self.dst = src, dst
        self.core_sems, self.line_sems, self.recv_sems = core_sems, line_sems, recv_sems
        self.local = pltpu.make_async_copy(src, dst.at[place.col], local_sem)

    def to_core(self, block, src=None):
        at = self.at
        src = self.dst.at[block] if src is None else src
        return remote(
            src, self.dst.at[block], self.core_sems.at[block], self.recv_sems.at[block],
            (at.row, at.other),
        )

    def to_line(self, block, way, src=None):
        at = self.at
        src = self.dst.at[block] if src is None else src
        return remote(
            src,
            self.dst.at[block],
            self.line_sems.at[block, (way + 1) // 2],
            self.recv_sems.at[block],
            (at.row, at.col + 2 * way),
        )

    def ends(self, way):
        return self.at.chip < self.at.chips - 1 if way > 0 else self.at.chip > 0

    def start(self):
        self.local.start()
        for way in (1, -1):

            @pl.when(self.ends(way))
            def _():
                self.to_line(self.at.col, way, self.src).start()

        self.to_core(self.at.col, self.src).start()

    def arrivals(self, dist, act):
        for way in (1, -1):
            chip = self.at.chip - way * dist
            near = chip >= 0 if way > 0 else chip < self.at.chips

            @pl.when(near)
            def _():
                act(2 * chip + self.at.core, way)

    def step(self, dist, extra=None):
        def act(block, way):
            self.to_core(block).wait_recv()

            @pl.when(self.ends(way))
            def _():
                self.to_line(block, way).start()

            self.to_core(block).start()
            if extra is not None:
                extra(block)

        self.arrivals(dist, act)

    def finish(self):
        self.local.wait()
        self.to_core(self.at.col, self.src).wait_send()
        for way in (1, -1):

            @pl.when(self.ends(way))
            def _():
                self.to_line(self.at.col, way, self.src).wait_send()

        def act(block, way):
            self.to_core(block).wait_send()

            @pl.when(self.ends(way))
            def _():
                self.to_line(block, way).wait_send()

        for dist in range(1, self.at.chips):
            self.arrivals(dist, act)
        for chip in range(self.at.chips):
            self.to_core(2 * chip + 1 - self.at.core).wait_recv()


def gather_sems(cols_n):
    return [
        pltpu.SemaphoreType.DMA((cols_n,)),
        pltpu.SemaphoreType.DMA((cols_n, 2)),
        pltpu.SemaphoreType.DMA((cols_n,)),
        pltpu.SemaphoreType.DMA,
    ]


ANY = pl.BlockSpec(memory_space=pl.ANY)


def line_gather(arrays, collective_id, rows_n, cols_n):
    n = len(arrays)

    def kernel(*refs):
        srcs, dsts, sems = refs[:n], refs[n : 2 * n], refs[2 * n :]
        place = Place(rows_n, cols_n)
        place.greet(False)
        jobs = [
            LineGather(place, srcs[i], dsts[i], *sems[4 * i : 4 * i + 4]) for i in range(n)
        ]
        for job in jobs:
            job.start()
        for dist in range(1, place.chips):
            for job in jobs:
                job.step(dist)
        for job in jobs:
            job.finish()

    return pl.pallas_call(
        kernel,
        in_specs=[ANY] * n,
        out_specs=[ANY] * n,
        out_shape=[jax.ShapeDtypeStruct((cols_n,) + a.shape, a.dtype) for a in arrays],
        scratch_shapes=gather_sems(cols_n) * n,
        compiler_params=pltpu.CompilerParams(collective_id=collective_id, has_side_effects=True),
        name="line_gather",
    )(*arrays)


def first_gather(
    bundle, cotangent, routes_t, shared, downs, expert, later, collective_id, rows_n, cols_n
):
    per_row = downs.shape[0]
    square = rows_n == 4
    n_goals = 2 if square else rows_n - 1
    n_later = len(later)
    inner = expert.shape[1]
    half_experts = expert.shape[0] // 2

    def kernel(*refs):
        bundle_ref, dy_ref, rt_ref, sh_ref, sd_ref, ex_ref = refs[:6]
        refs = refs[6 + n_later :]
        full_ref, dy_all, rt_all, sh_all, sd_all, ex_all = refs[:6]
        down_line, *sems = refs[6 + n_later :]
        place = Place(rows_n, cols_n)
        b_sems, sems = sems[:4], sems[4:]
        d_sems, sems = sems[:4], sems[4:]
        r_sems, sems = sems[:4], sems[4:]
        l_sems, sems = sems[:4], sems[4:]
        (
            row_send, row_core, row_recv, sh_send, sh_recv, sh_local, sd_send, sd_recv,
            sd_local, ex_send, ex_recv, ex_local,
        ) = sems
        place.greet(True)
        row, col = place.row, place.col
        across = along = corner = None
        goals = [place.peer_row(step) for step in range(1, rows_n)]
        sources = goals
        if square:
            across, along, corner = place.square()
            goals, sources = [across, along], [across, along, corner]
        weights = LineGather(place, bundle_ref, full_ref.at[row], *b_sems)
        grads = LineGather(place, dy_ref, dy_all, *d_sems)
        picks = LineGather(place, rt_ref, rt_all, *r_sems)

        def to_row(block, n, src=None):
            home = full_ref.at[row, block]
            return remote(
                home if src is None else src, home, row_send.at[block, n],
                row_recv.at[row, block], (goals[n], col),
            )

        def push(block, src=None):
            for n in range(n_goals):
                to_row(block, n, src).start()

        def from_row(source, block):
            home = full_ref.at[source, block]
            return remote(
                home, home, row_core.at[source, block], row_recv.at[source, block],
                (row, place.other),
            )

        def onward(source, block, goal):
            home = full_ref.at[source, block]
            return remote(
                home, home, row_send.at[block, 2], row_recv.at[source, block], (goal, col)
            )

        def take(source, block):
            copy = from_row(source, block)
            copy.wait_recv()
            copy.start()

        def expert_rows(source, half):
            return ex_all.at[
                pl.ds(half * half_experts, half_experts),
                pl.ds(pl.multiple_of(source * inner, inner), inner),
            ]

        def expert_to(n, half):
            return remote(
                ex_ref.at[pl.ds(half * half_experts, half_experts)], expert_rows(row, half),
                ex_send.at[n, half], ex_recv.at[row, half], (goals[n], col),
            )

        def expert_onward(source, half, goal):
            home = expert_rows(source, half)
            return remote(
                home, home, ex_send.at[2, half], ex_recv.at[source, half], (goal, col)
            )

        def shared_to(step):
            return remote(
                sh_ref, sh_all.at[row], sh_send.at[step], sh_recv.at[row],
                (place.peer_row(step), col),
            )

        lines = LineGather(place, sd_ref, down_line, *l_sems)
        holder = lax.div(col, per_row) == row
        pieces = down_line.at[:, lax.rem(col, per_row)]
        pieces_here = pltpu.make_async_copy(pieces, sd_all, sd_local)

        def downs_to(step):
            return remote(
                pieces, sd_all, sd_send.at[step], sd_recv, (place.peer_row(step), col)
            )

        weights.start()
        push(col, bundle_ref)
        if square:
            for n, half in ((0, 0), (1, 1)):
                expert_to(n, half).start()
        lines.start()
        for dist in range(1, place.chips):
            weights.step(dist, push)
            lines.step(dist)
        grads.start()
        picks.start()
        lines.finish()

        @pl.when(holder)
        def _():
            pieces_here.start()
            for step in range(1, rows_n):
                downs_to(step).start()

        if square:
            for n, half in ((0, 1), (1, 0)):
                expert_to(n, half).start()
        else:
            for n in range(n_goals):
                for half in range(2):
                    expert_to(n, half).start()
        shared_here = pltpu.make_async_copy(sh_ref, sh_all.at[row], sh_local)
        shared_here.start()
        expert_here = [
            pltpu.make_async_copy(
                ex_ref.at[pl.ds(half * half_experts, half_experts)], expert_rows(row, half),
                ex_local.at[half],
            )
            for half in range(2)
        ]
        for copy in expert_here:
            copy.start()
        for step in range(1, rows_n):
            shared_to(step).start()
        for dist in range(1, place.chips - 1):
            grads.step(dist)
            picks.step(dist)
            if square and dist == 1:

                @pl.loop(0, place.chips)
                def _(i):
                    chip = lax.rem(place.chip + i, place.chips)
                    block = 2 * chip + place.core
                    even = lax.rem(chip, 2) == 0
                    take(across, block)

                    @pl.when(even)
                    def _():
                        onward(across, block, along).start()

                    take(along, block)

                    @pl.when(jnp.logical_not(even))
                    def _():
                        onward(along, block, across).start()

                expert_onward(across, 0, along).wait_recv()
                expert_onward(across, 0, along).start()
                expert_onward(along, 1, across).wait_recv()
                expert_onward(along, 1, across).start()
        for source in [corner] if square else sources:

            @pl.loop(0, place.chips)
            def _(chip):
                take(source, 2 * chip + place.core)

        grads.step(place.chips - 1)
        picks.step(place.chips - 1)
        weights.finish()
        grads.finish()
        picks.finish()
        shared_here.wait()
        for copy in expert_here:
            copy.wait()

        @pl.when(holder)
        def _():
            pieces_here.wait()
            for step in range(1, rows_n):
                downs_to(step).wait_send()

        @pl.when(jnp.logical_not(holder))
        def _():
            downs_to(1).wait_recv()

        for n in range(n_goals):
            for half in range(2):
                expert_to(n, half).wait_send()
        if square:
            expert_onward(across, 0, along).wait_send()
            expert_onward(along, 1, across).wait_send()
            expert_onward(across, 1, along).wait_recv()
            expert_onward(along, 0, across).wait_recv()
            expert_onward(corner, 0, along).wait_recv()
            expert_onward(corner, 1, along).wait_recv()
        else:
            for source in sources:
                for half in range(2):
                    expert_onward(source, half, source).wait_recv()
        for step in range(1, rows_n):
            other_row = place.peer_row(step)
            shared_to(step).wait_send()
            remote(
                sh_ref, sh_all.at[other_row], sh_send.at[0], sh_recv.at[other_row],
                (other_row, col),
            ).wait_recv()

        @pl.loop(0, place.chips)
        def _(chip):
            block = 2 * chip + place.core
            for n in range(n_goals):
                to_row(block, n).wait_send()
            if square:
                onward(across, block, along).wait_send()
            for source in sources:
                from_row(source, block).wait_send()
                from_row(source, 2 * chip + 1 - place.core).wait_recv()

    outs = [
        jax.ShapeDtypeStruct((rows_n, cols_n) + bundle.shape, bundle.dtype),
        jax.ShapeDtypeStruct((cols_n,) + cotangent.shape, cotangent.dtype),
        jax.ShapeDtypeStruct((cols_n,) + routes_t.shape, routes_t.dtype),
        jax.ShapeDtypeStruct((rows_n,) + shared.shape, shared.dtype),
        jax.ShapeDtypeStruct((cols_n,) + downs.shape[1:], downs.dtype),
        jax.ShapeDtypeStruct(
            (expert.shape[0], rows_n * inner, expert.shape[2]), expert.dtype
        ),
    ] + [jax.ShapeDtypeStruct(a.shape, a.dtype) for a in later]
    outs.append(jax.ShapeDtypeStruct((cols_n,) + downs.shape, downs.dtype))
    return pl.pallas_call(
        kernel,
        in_specs=[ANY] * (6 + n_later),
        out_specs=[ANY] * (7 + n_later),
        out_shape=outs,
        input_output_aliases={6 + i: 6 + i for i in range(n_later)},
        scratch_shapes=gather_sems(cols_n) * 4
        + [
            pltpu.SemaphoreType.DMA((cols_n, max(rows_n, 3))),
            pltpu.SemaphoreType.DMA((rows_n, cols_n)),
            pltpu.SemaphoreType.DMA((rows_n, cols_n)),
            pltpu.SemaphoreType.DMA((rows_n,)),
            pltpu.SemaphoreType.DMA((rows_n,)),
            pltpu.SemaphoreType.DMA,
            pltpu.SemaphoreType.DMA((rows_n,)),
            pltpu.SemaphoreType.DMA,
            pltpu.SemaphoreType.DMA,
            pltpu.SemaphoreType.DMA((max(rows_n, 3), 2)),
            pltpu.SemaphoreType.DMA((rows_n, 2)),
            pltpu.SemaphoreType.DMA((2,)),
        ],
        compiler_params=pltpu.CompilerParams(collective_id=collective_id, has_side_effects=True),
        name="first_gather",
    )(bundle, cotangent, routes_t, shared, downs, expert, *later)


def line_sum_loop(place, mine, recv, send_sems, recv_sems, parts, ready):
    chips, here = place.chips, place.chip
    rows = mine.shape[1] // parts
    items = (chips - 1) * parts

    def copy(chip, part, way):
        span = pl.ds(part * rows, rows)
        goal = here + way
        land = chip if way > 0 else jnp.where(chip == goal, chips, chip)
        return remote(
            mine.at[chip, span],
            recv.at[land, span],
            send_sems.at[chip, part],
            recv_sems.at[land, part],
            (place.row, place.col + 2 * way),
        )

    def incoming(land, part):
        span = pl.ds(part * rows, rows)
        return remote(
            mine.at[0, span], recv.at[land, span], send_sems.at[0, part],
            recv_sems.at[land, part], (place.row, place.other),
        )

    def handle(chip, part, way):
        @pl.when(part == 0)
        def _():
            ready(chip)

        span = pl.ds(part * rows, rows)
        comes = here > 0 if way > 0 else here < chips - 1

        @pl.when(comes)
        def _():
            incoming(chip, part).wait_recv()
            total = mine[chip, span].astype(F32) + recv[chip, span].astype(F32)
            mine[chip, span] = total.astype(mine.dtype)

        copy(chip, part, way).start()

    lag = 2 * (chips - 2 - here)

    @pl.loop(0, items + 2 * (chips - 2))
    def _(at):
        up = jnp.minimum(at, items - 1)
        up_chip = chips - 1 - lax.div(up, parts)

        @pl.when((at < items) & (up_chip > here))
        def _():
            handle(up_chip, lax.rem(up, parts), 1)

        down = at - jnp.maximum(lag, 0)
        safe = jnp.clip(down, 0, items - 1)
        down_chip = lax.div(safe, parts)

        @pl.when((down >= 0) & (down < items) & (down_chip < here))
        def _():
            handle(down_chip, lax.rem(safe, parts), -1)

    ready(here)

    def result(part, store):
        span = pl.ds(part * rows, rows)
        total = mine[here, span].astype(F32)

        @pl.when((here > 0) & (here < chips - 1))
        def _():
            incoming(here, part).wait_recv()
            incoming(chips, part).wait_recv()
            store(span, total + recv[here, span].astype(F32) + recv[chips, span].astype(F32))

        @pl.when((here > 0) & (here == chips - 1))
        def _():
            incoming(here, part).wait_recv()
            store(span, total + recv[here, span].astype(F32))

        @pl.when((here == 0) & (here < chips - 1))
        def _():
            incoming(chips, part).wait_recv()
            store(span, total + recv[chips, span].astype(F32))

    def drain():
        @pl.loop(0, chips)
        def _(chip):
            for part in range(parts):

                @pl.when(chip > here)
                def _():
                    copy(chip, part, 1).wait_send()

                @pl.when(chip < here)
                def _():
                    copy(chip, part, -1).wait_send()

    return result, drain


def dense_sum(lefts, rights, tails, shared, calls, collective_id, rows_n, cols_n):
    chips = cols_n // 2
    n_rounds = chips - 1
    moved = jax.ShapeDtypeStruct(calls[0][0].shape[1:], BF)
    square = rows_n == 4
    inner = shared.shape[1]
    units = shared.shape[2] // 3
    per_row = cols_n // rows_n
    extents = [left.shape[1] // cols_n for left in lefts]
    block = (sum(extents), inner)
    n = len(lefts)

    def kernel(*refs):
        left_refs, right_refs = refs[:n], refs[n : 2 * n]
        (
            tail_ref, sh_ref, *call_refs
        ) = refs[2 * n : 2 * n + 2 + 2 * chips]
        (
            out_ref, sh_out, sd_out, arrivals,
            both, extra, rows_in, recv, sh_in, sd_cut, held, came, held_sems, came_sems,
            core_send, core_recv, row_send, row_recv, send_sems, recv_sems,
            sh_send, sh_recv, sh_local, move_send, move_recv, sd_send, sd_recv,
        ) = refs[2 * n + 2 + 2 * chips :]
        place = Place(rows_n, cols_n)
        row, col = place.row, place.col
        mine = both.at[place.core]
        shared_here = pltpu.make_async_copy(sh_ref.at[row], sh_in.at[row], sh_local)
        shared_here.start()
        down_row = lax.div(col, per_row)
        place.greet(True, downs_back=per_row)

        tables = round_tables(chips)[1:]

        def moves(turn):
            return Moves(
                place, held.at[0], held.at[1], arrivals.at[turn, 0], arrivals.at[turn, 1],
                move_send.at[turn], move_recv.at[turn],
            )

        def add_came(which):
            part = came.shape[1] // 4
            for at in range(0, came.shape[1], part):
                span = slice(at, at + part)
                held[which, span] = (
                    held[which, span].astype(F32) + came[which, span].astype(F32)
                ).astype(BF)

        def bring(which, own, other):
            return (
                pltpu.make_async_copy(own, held.at[which], held_sems.at[which]),
                pltpu.make_async_copy(other, came.at[which], came_sems.at[which]),
            )

        def next_round(turn):
            if turn:
                moves(turn - 1).wait_send()
            for which in range(2):
                call = jnp.int32(0)
                for chip in range(chips):
                    call = call + jnp.where(place.chip == chip, tables[which][chip][turn], 0)
                for i in range(turn + 1):

                    @pl.when(call == i)
                    def _():
                        for copy in bring(which, call_refs[2 * i].at[0], call_refs[2 * i + 1].at[0]):
                            copy.start()

            for which in range(2):
                for copy in bring(which, call_refs[0].at[0], call_refs[1].at[0]):
                    copy.wait()
                add_came(which)
            if turn:
                moves(turn - 1).wait_recv()
                comes = (place.chip > 0, place.chip < chips - 1)
                for which in range(2):

                    @pl.when(comes[which])
                    def _():
                        pltpu.make_async_copy(
                            arrivals.at[turn - 1, which], came.at[which], came_sems.at[which]
                        ).start()

                for which in range(2):

                    @pl.when(comes[which])
                    def _():
                        pltpu.make_async_copy(
                            arrivals.at[turn - 1, which], came.at[which], came_sems.at[which]
                        ).wait()
                        add_came(which)

            moves(turn).start()

        next_round(0)

        def downs_to(turn, act_far, act_here):
            goal_col = per_row * row + turn
            here = (goal_col == col) & (down_row == row)
            source = lax.rem(col, per_row)

            @pl.when(here)
            def _():
                act_here(
                    pltpu.make_async_copy(
                        sd_cut.at[turn], sd_out.at[source], sd_recv.at[source]
                    )
                )

            @pl.when(jnp.logical_not(here))
            def _():
                act_far(
                    remote(
                        sd_cut.at[turn], sd_out.at[source], sd_send.at[turn],
                        sd_recv.at[source], (down_row, goal_col),
                    )
                )

        def swap(goal):
            return remote(
                both.at[1 - place.core, goal], extra.at[goal], core_send.at[goal],
                core_recv.at[goal], (row, place.other),
            )

        def shared_to(step):
            goal = place.peer_row(step)
            return remote(
                sh_ref.at[goal], sh_in.at[row], sh_send.at[step], sh_recv.at[row], (goal, col)
            )

        def shared_from(step):
            source = place.peer_row(step)
            return remote(
                sh_ref.at[source], sh_in.at[source], sh_send.at[0], sh_recv.at[source],
                (source, col),
            )

        across = along = corner = None
        if square:
            across, along, corner = place.square()

        def ways(chip):
            return (across, along) if chip % 2 == 0 else (along, across)

        def to_near(goal, slot, chip):
            near = ways(chip)[1 if slot == 2 else 0]
            return remote(
                mine.at[goal, chip], rows_in.at[slot, chip], row_send.at[slot, chip],
                row_recv.at[slot, chip], (near, col),
            )

        def to_row(goal, chip):
            return remote(
                mine.at[goal, chip], rows_in.at[row, chip], row_send.at[goal, chip],
                row_recv.at[row, chip], (goal, col),
            )

        def from_row(step, chip):
            source = place.peer_row(step)
            return remote(
                mine.at[source, chip], rows_in.at[source, chip], row_send.at[0, chip],
                row_recv.at[source, chip], (source, col),
            )

        order = []
        for i in range((chips + 1) // 2):
            order += [chips - 1 - i, i] if chips - 1 - i != i else [i]

        def push(goal):
            swap(goal).wait_recv()

            @pl.when(goal != row)
            def _():
                for chip in order:
                    mine[goal, chip] = (
                        mine[goal, chip].astype(F32) + extra[goal, chip].astype(F32)
                    ).astype(BF)
                    if not square:
                        to_row(goal, chip).start()
                        continue

                    @pl.when(goal == ways(chip)[0])
                    def _():
                        to_near(goal, 0, chip).start()

                    @pl.when(goal == corner)
                    def _():
                        to_near(goal, 1, chip).start()

        def hand_on():
            for chip in order:
                goal = ways(chip)[1]
                to_near(goal, 1, chip).wait_recv()
                mine[goal, chip] = (
                    mine[goal, chip].astype(F32) + rows_in[1, chip].astype(F32)
                ).astype(BF)
                to_near(goal, 2, chip).start()

        for step in range(1, rows_n):
            shared_to(step).start()
        for goal in range(rows_n):
            cols = slice(goal * inner, (goal + 1) * inner)
            at = 0
            for i in range(n):
                made = mm_tn(left_refs[i][...], right_refs[i][:, cols])
                if i == n - 1:
                    made = made + tail_ref[goal]
                made = made.astype(BF)
                for owner in range(cols_n):
                    both[owner % 2, goal, owner // 2, at : at + extents[i], :] = made[
                        owner * extents[i] : (owner + 1) * extents[i]
                    ]
                at += extents[i]
            swap(goal).start()
            if goal > 0:
                push(goal - 1)
        push(rows_n - 1)
        for turn in range(1, n_rounds):
            next_round(turn)
            if square and turn == 1:
                hand_on()
        shared_here.wait()
        for step in range(1, rows_n):
            shared_from(step).wait_recv()
        total = sh_in[0].astype(F32)
        for other in range(1, rows_n):
            total = total + sh_in[other].astype(F32)
        sh_out[...] = total[:, : 2 * units]
        cut = inner // per_row
        for turn in range(per_row):
            sd_cut[turn] = total[turn * cut : (turn + 1) * cut, 2 * units :]
            downs_to(turn, lambda far: far.start(), lambda here: here.start())

        def ready(chip):
            total = mine[row, chip].astype(F32) + extra[row, chip].astype(F32)
            if square:
                for slot in (0, 2):
                    remote(
                        mine.at[row, chip], rows_in.at[slot, chip], row_send.at[slot, chip],
                        row_recv.at[slot, chip], (across, col),
                    ).wait_recv()
                    total = total + rows_in[slot, chip].astype(F32)
            else:
                for step in range(1, rows_n):
                    from_row(step, chip).wait_recv()
                    total = total + rows_in[place.peer_row(step), chip].astype(F32)
            mine[row, chip] = total.astype(BF)

        result, drain = line_sum_loop(
            place, mine.at[row], recv, send_sems, recv_sems, 1, ready
        )

        def store(span, value):
            out_ref[span] = value

        result(0, store)
        drain()

        moves(n_rounds - 1).wait_send()
        moves(n_rounds - 1).wait_recv()
        for turn in range(per_row):
            downs_to(turn, lambda far: far.wait_send(), lambda here: here.wait())
            at_home = per_row * row + turn
            mine_here = (at_home == col) & (down_row == row)

            @pl.when(jnp.logical_not(mine_here))
            def _():
                remote(
                    sd_cut.at[0], sd_out.at[turn], sd_send.at[turn], sd_recv.at[turn],
                    (down_row, at_home),
                ).wait_recv()

        for step in range(1, rows_n):
            shared_to(step).wait_send()
        for goal in range(rows_n):
            swap(goal).wait_send()

            if not square:

                @pl.when(goal != row)
                def _():
                    for chip in range(chips):
                        to_row(goal, chip).wait_send()

        if square:
            for chip in range(chips):
                for slot in range(3):
                    to_near(row, slot, chip).wait_send()

    vmem = pl.BlockSpec(memory_space=pltpu.VMEM)
    return pl.pallas_call(
        kernel,
        in_specs=[vmem] * (2 * n + 1) + [ANY] * (1 + 2 * chips),
        out_specs=[vmem, vmem, vmem, ANY],
        out_shape=[
            jax.ShapeDtypeStruct(block, F32),
            jax.ShapeDtypeStruct((inner, 2 * units), F32),
            jax.ShapeDtypeStruct((per_row, inner // per_row, units), F32),
            jax.ShapeDtypeStruct((n_rounds, 2) + moved.shape, moved.dtype),
        ],
        scratch_shapes=[
            pltpu.VMEM((2, rows_n, chips) + block, BF),
            pltpu.VMEM((rows_n, chips) + block, BF),
            pltpu.VMEM((rows_n, chips) + block, BF),
            pltpu.VMEM((chips + 1,) + block, BF),
            pltpu.VMEM(shared.shape, BF),
            pltpu.VMEM((per_row, inner // per_row, units), F32),
            pltpu.VMEM((2,) + moved.shape, BF),
            pltpu.VMEM((2,) + moved.shape, BF),
            pltpu.SemaphoreType.DMA((2,)),
            pltpu.SemaphoreType.DMA((2,)),
            pltpu.SemaphoreType.DMA((rows_n,)),
            pltpu.SemaphoreType.DMA((rows_n,)),
            pltpu.SemaphoreType.DMA((rows_n, chips)),
            pltpu.SemaphoreType.DMA((rows_n, chips)),
            pltpu.SemaphoreType.DMA((chips, 1)),
            pltpu.SemaphoreType.DMA((chips + 1, 1)),
            pltpu.SemaphoreType.DMA((rows_n,)),
            pltpu.SemaphoreType.DMA((rows_n,)),
            pltpu.SemaphoreType.DMA,
            pltpu.SemaphoreType.DMA((n_rounds, 2)),
            pltpu.SemaphoreType.DMA((n_rounds, 2)),
            pltpu.SemaphoreType.DMA((per_row,)),
            pltpu.SemaphoreType.DMA((per_row,)),
        ],
        compiler_params=pltpu.CompilerParams(
            collective_id=collective_id, has_side_effects=True,
            vmem_limit_bytes=60 * 1024 * 1024,
        ),
        cost_estimate=pl.CostEstimate(
            flops=2 * 512 * 1536 * 4096, bytes_accessed=350_000_000, transcendentals=0
        ),
        name="dense_sum",
    )(*lefts, *rights, tails, shared, *[part for pair in calls for part in pair])


def round_tables(chips):
    order, up, down = [], [], []
    for here in range(chips):
        due = {q: chips - 1 - q + here for q in range(here + 1, chips)}
        due.update({q: q + chips - 1 - here for q in range(here)})
        calls = sorted(due, key=lambda q: (due[q], -q)) + [here]
        order.append(calls)
        at = {q: i for i, q in enumerate(calls)}
        up.append([at.get(chips - 1 - t + here, 0) for t in range(chips - 1)])
        down.append([at.get(t - (chips - 1 - here), 0) for t in range(chips - 1)])
    return order, up, down


class LineRounds:
    def __init__(self, cols_n):
        self.chips = cols_n // 2
        here = lax.axis_index("col") // 2
        self.not_first, self.not_last = here > 0, here < self.chips - 1
        self.sums = []
        self.below = self.above = None

    def add(self, own, other):
        self.sums.append((own, other))

    def arrived(self, below, above):
        self.below, self.above = below, above

    def result(self):
        own, other = self.sums[-1]
        total = own.astype(F32) + other.astype(F32)
        total = total + jnp.where(self.not_first, self.below.astype(F32), 0.0)
        return total + jnp.where(self.not_last, self.above.astype(F32), 0.0)


def routed_kernel(call, rows_n, cols_n, *refs):
    (
        x_hbm, dy_hbm, routes_hbm, routes_t_hbm, gates_hbm, eg_ref, eu_ref, ed_ref, sgu_ref, sd_ref
    ) = refs[:10]
    n_moves = 2 if call else 0
    n_before = 2 if call > 1 else 0
    call_refs, refs = refs[10 : 10 + 2 * call], refs[10 + 2 * call :]
    before, refs = refs[:n_before], refs[n_before:]
    (
        own_hbm, other_hbm, xs_hbm, dys_hbm, hid_ref, gg_ref, gu_ref, ggw_ref, shared_ref
    ) = refs[:9]
    arrivals, refs = refs[9 : 9 + n_moves], refs[9 + n_moves :]
    (
        x_ref, dy_ref, routes_ref, routes_t_ref, gates_ref,
        xs, dys, pick, back_pick, wide_out, wide_gx, slot_gate, stage,
        load_sems, slot_sems, own_sems, core_send, core_recv, *refs,
    ) = refs
    place = Place(rows_n, cols_n)
    my_core = place.core
    unit = jnp.int32(0)
    for chip, calls in enumerate(round_tables(place.chips)[0]):
        unit = unit + jnp.where(place.chip == chip, calls[call], 0)
    pair = pl.ds(2 * unit, 2)
    loads = [
        pltpu.make_async_copy(src.at[pair], dst, load_sems.at[i])
        for i, (src, dst) in enumerate(
            (
                (routes_hbm, routes_ref), (routes_t_hbm, routes_t_ref), (gates_hbm, gates_ref),
                (x_hbm, x_ref), (dy_hbm, dy_ref),
            )
        )
    ]
    moves = None
    if n_moves:
        line = RoundStart(place, call_refs, *refs[:4])
        moves = line.moves(arrivals, *refs[4:])
    e = pl.program_id(0)
    total = x_ref.shape[1]
    cap = xs.shape[1] // 2
    hidden_units = sd_ref.shape[0]
    first = place.col * EXP_DEV
    spans = [slice(at, at + 512) for at in range(0, x_ref.shape[2], 512)]

    def slot_copy(which):
        src, dst = ((xs, xs_hbm), (dys, dys_hbm))[which]
        return pltpu.make_async_copy(src, dst, slot_sems.at[which])

    def own_copy(which):
        return pltpu.make_async_copy(
            stage.at[which, my_core], own_hbm.at[which], own_sems.at[which]
        )

    def core_copy(which):
        return remote(
            stage.at[which, 1 - my_core], other_hbm.at[which], core_send.at[which],
            core_recv.at[which], (place.row, place.other),
        )

    @pl.when(e == 0)
    def _():
        for load in loads:
            load.start()
        place.greet(False)
        if n_moves:
            line.prepare(call - 1)
            if n_before:
                line.add(before)
            moves.start()
        ggw_ref[...] = jnp.zeros_like(ggw_ref)
        for load in loads:
            load.wait()
        row_at = lax.broadcasted_iota(jnp.int32, (total, total), 0)
        col_at = lax.broadcasted_iota(jnp.int32, (total, total), 1)
        upto = jnp.where(row_at <= col_at, 1.0, 0.0).astype(BF)
        since = jnp.where(row_at >= col_at, 1.0, 0.0).astype(BF)
        for core in range(2):
            gate_rows = gates_ref[core]
            route_rows = routes_ref[core]
            route_cols = routes_t_ref[core]
            hits = [
                jnp.sum(jnp.where(route_rows == first + i, 1.0, 0.0), axis=0, keepdims=True)
                for i in range(EXP_DEV)
            ]
            hits = jnp.concatenate(hits + [jnp.zeros((8 - EXP_DEV, total), F32)], axis=0)
            rank = jnp.where(hits > 0.0, mm(hits.astype(BF), upto) - 1.0, -1.0)
            hits_t = [
                jnp.sum(jnp.where(route_cols == first + i, 1.0, 0.0), axis=1, keepdims=True)
                for i in range(EXP_DEV)
            ]
            hits_t = jnp.concatenate(hits_t + [jnp.zeros((total, 8 - EXP_DEV), F32)], axis=1)
            rank_t = jnp.where(hits_t > 0.0, mm(since, hits_t.astype(BF)) - 1.0, -1.0)
            at = lax.broadcasted_iota(jnp.int32, (cap, total), 0).astype(F32)
            at_t = lax.broadcasted_iota(jnp.int32, (total, cap), 1).astype(F32)
            backs = []
            for i in range(EXP_DEV):
                here = at == rank[i : i + 1, :]
                gate_row = jnp.sum(
                    jnp.where(route_rows == first + i, gate_rows, 0.0), axis=0, keepdims=True
                )
                slot_gate[i, core * cap : (core + 1) * cap, :] = jnp.sum(
                    jnp.where(here, gate_row, 0.0), axis=1, keepdims=True
                )
                pick[core, i * cap : (i + 1) * cap, :] = jnp.where(here, 1.0, 0.0).astype(BF)
                backs.append(jnp.where(at_t == rank_t[:, i : i + 1], 1.0, 0.0).astype(BF))
            back_pick[core] = jnp.concatenate(backs, axis=1)
            for src, dst in ((x_ref, xs), (dy_ref, dys)):
                for cols in spans:
                    got = mm(pick[core], src[core, :, cols]).astype(BF)
                    for i in range(EXP_DEV):
                        dst[i, core * cap : (core + 1) * cap, cols] = got[
                            i * cap : (i + 1) * cap
                        ]
        slot_copy(0).start()
        slot_copy(1).start()

    rows_x = xs[e]
    gate_part = mm(rows_x, eg_ref[0])
    up_part = mm(rows_x, eu_ref[0])
    act, slope = silu_parts(gate_part)
    grad_hidden = mm_nt(dys[e], ed_ref[0])
    hidden = (act * up_part).astype(BF).astype(F32)
    weight = slot_gate[e]
    gated = (hidden * weight).astype(BF)
    hid_ref[0] = gated
    slot_ggw = jnp.sum(hidden * grad_hidden, axis=1, keepdims=True)
    grad_hidden = grad_hidden * weight
    geg = (grad_hidden * up_part * slope).astype(BF)
    geu = (grad_hidden * act).astype(BF)
    gg_ref[0] = geg
    gu_ref[0] = geu
    rows = pl.ds(pl.multiple_of(e * cap, cap), cap)
    for cols in spans:
        made = mm(gated, ed_ref[0, :, cols]).astype(BF)
        back = (mm_nt(geg, eg_ref[0, cols, :]) + mm_nt(geu, eu_ref[0, cols, :])).astype(BF)
        for core in range(2):
            wide_out[core, rows, cols] = made[core * cap : (core + 1) * cap]
            wide_gx[core, rows, cols] = back[core * cap : (core + 1) * cap]
    sub = lax.broadcasted_iota(jnp.int32, (8, total), 0)
    for core in range(2):
        back = jnp.sum(
            pick[core, rows, :].astype(F32) * slot_ggw[core * cap : (core + 1) * cap],
            axis=0,
            keepdims=True,
        )
        ggw_ref[core] = jnp.where(sub == e, back, ggw_ref[core])

    @pl.when(e == EXP_DEV - 1)
    def _():
        for core in range(2):
            both = mm(x_ref[core], sgu_ref[...])
            s_act, s_slope = silu_parts(both[:, :hidden_units])
            s_up = both[:, hidden_units:]
            s_hidden = (s_act * s_up).astype(BF)
            grad_shared = mm_nt(dy_ref[core], sd_ref[...])
            grad_both = jnp.concatenate(
                [(grad_shared * s_up * s_slope).astype(BF), (grad_shared * s_act).astype(BF)],
                axis=1,
            )
            for cols in spans:
                value = mm(back_pick[core], wide_gx[core, :, cols])
                value = value + mm_nt(grad_both, sgu_ref[cols, :])
                stage[1, core, :, cols] = value.astype(BF)
                value = mm(back_pick[core], wide_out[core, :, cols])
                value = value + mm(s_hidden, sd_ref[:, cols])
                stage[0, core, :, cols] = value.astype(BF)
                made = mm_tn(x_ref[core, :, cols], grad_both)
                made_d = mm_tn(dy_ref[core, :, cols], s_hidden)
                if core == 0:
                    shared_ref[cols, : 2 * hidden_units] = made
                    shared_ref[cols, 2 * hidden_units :] = made_d
                else:
                    shared_ref[cols, : 2 * hidden_units] += made
                    shared_ref[cols, 2 * hidden_units :] += made_d
        for which in (1, 0):
            core_copy(which).start()
            own_copy(which).start()
        slot_copy(0).wait()
        slot_copy(1).wait()
        if n_moves:
            moves.wait_send()
            moves.wait_recv()
        for which in (1, 0):
            own_copy(which).wait()
            core_copy(which).wait_send()
            core_copy(which).wait_recv()


def routed(
    call, rows_n, x_all, dy_all, routes, routes_t, gates, egate, eup, edown, sgu, sdown, calls,
    before,
):
    call_args = [part for pair in calls for part in pair] + list(before)
    n_moves = 2 if call else 0
    cols_n, total, width = x_all.shape
    cap = 4 * total * TOP // (3 * EXP_DEV * cols_n)
    slots = 2 * cap
    ffn = egate.shape[2]
    hidden_units = sdown.shape[0]

    def each(*shape):
        return pl.BlockSpec((1,) + shape, lambda e: (e,) + (0,) * len(shape))

    def whole(*shape):
        return pl.BlockSpec(
            shape, lambda e: (0,) * len(shape), pipeline_mode=pl.Buffered(1)
        )

    slot_block = each(slots, ffn)
    return pl.pallas_call(
        functools.partial(routed_kernel, call, rows_n, cols_n),
        grid=(EXP_DEV,),
        in_specs=[ANY] * 5
        + [
            each(width, ffn), each(width, ffn), each(ffn, width), whole(*sgu.shape),
            whole(*sdown.shape),
        ]
        + [ANY] * len(call_args),
        out_specs=[
            ANY, ANY, ANY, ANY, slot_block, slot_block, slot_block,
            whole(2, 8, total), whole(width, 3 * hidden_units),
        ]
        + [ANY] * n_moves,
        out_shape=[
            jax.ShapeDtypeStruct((2, total, width), BF),
            jax.ShapeDtypeStruct((2, total, width), BF),
            jax.ShapeDtypeStruct((EXP_DEV, slots, width), BF),
            jax.ShapeDtypeStruct((EXP_DEV, slots, width), BF),
            jax.ShapeDtypeStruct((EXP_DEV, slots, ffn), BF),
            jax.ShapeDtypeStruct((EXP_DEV, slots, ffn), BF),
            jax.ShapeDtypeStruct((EXP_DEV, slots, ffn), BF),
            jax.ShapeDtypeStruct((2, 8, total), F32),
            jax.ShapeDtypeStruct((width, 3 * hidden_units), F32),
        ]
        + [jax.ShapeDtypeStruct((total, width), BF)] * n_moves,
        scratch_shapes=[
            pltpu.VMEM((2, total, width), BF),
            pltpu.VMEM((2, total, width), BF),
            pltpu.VMEM((2, 8, total), jnp.int32),
            pltpu.VMEM((2, total, 8), jnp.int32),
            pltpu.VMEM((2, 8, total), F32),
            pltpu.VMEM((EXP_DEV, slots, width), BF),
            pltpu.VMEM((EXP_DEV, slots, width), BF),
            pltpu.VMEM((2, EXP_DEV * cap, total), BF),
            pltpu.VMEM((2, total, EXP_DEV * cap), BF),
            pltpu.VMEM((2, EXP_DEV * cap, width), BF),
            pltpu.VMEM((2, EXP_DEV * cap, width), BF),
            pltpu.VMEM((EXP_DEV, slots, 1), F32),
            pltpu.VMEM((2, 2, total, width), BF),
            pltpu.SemaphoreType.DMA((5,)),
            pltpu.SemaphoreType.DMA((2,)),
            pltpu.SemaphoreType.DMA((2,)),
            pltpu.SemaphoreType.DMA((2,)),
            pltpu.SemaphoreType.DMA((2,)),
        ]
        + (
            RoundStart.scratch((total, width))
            + [pltpu.SemaphoreType.DMA((2,)), pltpu.SemaphoreType.DMA((2,))]
            if call
            else []
        ),
        compiler_params=pltpu.CompilerParams(
            collective_id=4 + call, has_side_effects=True, vmem_limit_bytes=60 * 1024 * 1024
        ),
        cost_estimate=pl.CostEstimate(
            flops=24_000_000_000, bytes_accessed=100_000_000, transcendentals=0
        ),
        name="routed",
    )(
        x_all, dy_all, routes, routes_t, gates, egate, eup, edown, sgu, sdown, *call_args
    )


def expert_grads_kernel(units_n, rows_n, cut_left, *refs):
    left, right, out_ref = refs[:units_n], refs[units_n : 2 * units_n], refs[-1]
    inner = (left if cut_left else right)[0].shape[2] // rows_n

    def joined(parts, cols=slice(None)):
        return jnp.concatenate([part[0, :, cols] for part in parts], axis=0)

    other = joined(right if cut_left else left)
    for row in range(rows_n):
        cut = joined(left if cut_left else right, slice(row * inner, (row + 1) * inner))
        pair = (cut, other) if cut_left else (other, cut)
        out_ref[row, 0] = mm_tn(*pair).astype(BF)


def expert_grads(left, right, rows_n, cut_left):
    slots = left[0].shape[1]
    units_n = len(left)
    sizes = [left[0].shape[2], right[0].shape[2]]
    specs = [
        pl.BlockSpec((1, slots, size), lambda e: (e, 0, 0)) for size in sizes for _ in left
    ]
    sizes[0 if cut_left else 1] //= rows_n
    return pl.pallas_call(
        functools.partial(expert_grads_kernel, units_n, rows_n, cut_left),
        grid=(EXP_DEV,),
        in_specs=specs,
        out_specs=pl.BlockSpec((rows_n, 1) + tuple(sizes), lambda e: (0, e, 0, 0)),
        out_shape=jax.ShapeDtypeStruct((rows_n, EXP_DEV) + tuple(sizes), BF),
        compiler_params=pltpu.CompilerParams(vmem_limit_bytes=60 * 1024 * 1024),
        cost_estimate=pl.CostEstimate(
            flops=7_000_000_000, bytes_accessed=30_000_000, transcendentals=0
        ),
        name="expert_grads",
    )(*left, *right)


def on_device(
    tokens,
    g_attn,
    w_query,
    key_projection,
    value_projection,
    w_out,
    g_moe,
    w_router,
    e_gate,
    e_up,
    e_down,
    s_gate,
    s_up,
    s_down,
    routes,
    deal,
    lengths,
    cotangent,
):
    rows_n = lax.axis_size("row")
    cols_n = lax.axis_size("col")
    row_here = lax.axis_index("row")
    col_here = lax.axis_index("col")
    both = ("row", "col")
    total = tokens.shape[0]
    width = MODEL_WIDTH
    experts = EXP_DEV * cols_n

    q_w, k_w = w_query.shape[1], key_projection.shape[1]
    inner = w_query.shape[0]
    gains = jnp.stack([g_attn, g_moe])
    gains = jnp.pad(gains, ((0, 0), (0, inner - gains.shape[1])))
    tail = jnp.concatenate([w_router.T, gains], axis=0)
    tail = jnp.pad(tail, ((0, 16 - tail.shape[0]), (0, 0)))
    bundle = jnp.concatenate(
        [w_query.T, key_projection.T, value_projection.T, w_out.T, tail], axis=0
    )
    routes_t = jnp.pad(routes.T, ((0, 8 - TOP), (0, 0)), constant_values=-1)
    units = s_gate.shape[1]
    shared = jnp.concatenate([s_gate, s_up], axis=1)
    per_row = s_down.shape[0] // units
    downs = s_down.reshape(per_row, units, s_down.shape[1])
    full, dy_all, routes_all, sgu, sdown, egate, e_up, e_down, _ = first_gather(
        bundle, cotangent, routes_t, shared, downs, e_gate, [e_up, e_down], 0, rows_n, cols_n
    )
    sdown = jnp.swapaxes(sdown, 0, 1).reshape(units, width)
    sgu = sgu.reshape(width, 2 * units)

    t_at = 2 * q_w + 2 * k_w
    extents = [q_w, k_w, k_w, q_w, 16]
    n_gain = g_attn.shape[0]
    gains = full[:, :, t_at + EXP_DEV : t_at + EXP_DEV + 2, :n_gain].transpose(2, 0, 1, 3)
    gains = gains.reshape(2, width).astype(F32)
    eup = lax.all_gather(e_up, "row", axis=1, tiled=True)
    edown = lax.all_gather(e_down, "row", axis=2, tiled=True)
    by_row = lengths.reshape(rows_n, cols_n, rows_n)
    by_row = lax.dynamic_slice(by_row, (0, col_here, row_here), (rows_n, 1, 1)).reshape(1, rows_n)
    row_ids = jnp.arange(rows_n, dtype=jnp.int32)
    own_lens = jnp.sum(jnp.where(deal.reshape(-1, 1) == row_ids, by_row, 0), axis=1)
    seq_ends = jnp.sum(jnp.where(row_ids[None, :] <= row_ids[:, None], own_lens, 0), axis=1)
    places = jnp.arange(total, dtype=jnp.int32)
    segment = jnp.sum((places[:, None] >= seq_ends[None, :]).astype(jnp.int32), axis=1)

    (
        normed_one, queries, keys, values, mixed, log_totals, after_attn, normed_two, scale_one,
        scale_two, gates, gates_t,
    ) = block_start(tokens, full, extents, gains, segment, routes)

    x_all, gates_all = line_gather([normed_two, gates_t], 1, rows_n, cols_n)
    chips = cols_n // 2
    my_order = jnp.array(round_tables(chips)[0], jnp.int32)[col_here // 2]
    routes_rows = jnp.swapaxes(routes_all, 1, 2)
    moe_sum = LineRounds(cols_n)
    saved, calls, before, ggw, grad_sh = [], [], (), [], 0.0
    for call in range(chips):
        own, other, *keep = routed(
            call, rows_n, x_all, dy_all, routes_all, routes_rows, gates_all, egate, eup, edown,
            sgu, sdown, calls, before,
        )
        saved.append(keep[:5])
        ggw_part, sh_part, *arrivals = keep[5:]
        before = tuple(arrivals)
        grad_sh = grad_sh + sh_part
        ggw.append(ggw_part)
        calls.append((own, other))
    xs, dys, hid, gg, gu = zip(*saved)
    grad_edown = expert_grads(hid, dys, rows_n, False)
    grad_egate = expert_grads(xs, gg, rows_n, True)
    grad_eup = expert_grads(xs, gu, rows_n, True)
    ggw = jnp.stack(ggw)[:, None, :, :EXP_DEV]
    is_unit = my_order[:, None] == jnp.arange(chips, dtype=jnp.int32)
    ggw = jnp.sum(jnp.where(is_unit[:, :, None, None, None], ggw, 0.0), axis=0)
    ggw = ggw.reshape(cols_n, EXP_DEV, total)

    ggw_home = lax.all_to_all(ggw, "col", split_axis=0, concat_axis=0, tiled=True)
    grad_tokens, gq, gk, gv, grad_attn_b, logits_left, gain_grads = block_end(
        tokens, cotangent, full, extents, gains, segment, routes, gates,
        ggw_home.reshape(experts, total),
        (calls[-1][0][1], calls[-1][1][1], *before),
        queries, keys, values, log_totals, after_attn, scale_one, scale_two,
    )

    def gain_rows(grad):
        part = grad.reshape(rows_n, cols_n, 1, n_gain)
        return jnp.pad(part, ((0, 0),) * 3 + ((0, inner - n_gain),))

    tails = jnp.concatenate([gain_rows(gain_grads[0]), gain_rows(gain_grads[1])], axis=2)
    tails = jnp.pad(tails, ((0, 0), (0, 0), (EXP_DEV, 16 - EXP_DEV - 2), (0, 0)))
    tails = tails.reshape(rows_n, cols_n * 16, inner)
    grads_sh = grad_sh.astype(BF).reshape(rows_n, inner, 3 * units)
    dense, dense_sh, sd_parts, arrivals = dense_sum(
        [gq, gk, gv, grad_attn_b, logits_left],
        [normed_one, normed_one, normed_one, mixed, normed_two],
        tails, grads_sh, calls, 2, rows_n, cols_n,
    )
    moe_sum.add(calls[-1][0][0], calls[-1][1][0])
    moe_sum.arrived(arrivals[-1, 0], arrivals[-1, 1])
    output = (after_attn + moe_sum.result()).astype(BF)
    out_wq = dense[:q_w].T
    out_wk = dense[q_w : q_w + k_w].T
    out_wv = dense[q_w + k_w : q_w + 2 * k_w].T
    out_wo = dense[q_w + 2 * k_w : t_at].T
    out_router = dense[t_at : t_at + EXP_DEV].T
    out_g_attn = dense[t_at + EXP_DEV, :n_gain]
    out_g_moe = dense[t_at + EXP_DEV + 1, :n_gain]
    out_sg = dense_sh[:, :units]
    out_su = dense_sh[:, units:]
    out_sd = sd_parts.transpose(0, 2, 1).reshape(per_row * units, inner // per_row)

    def row_sum(grad):
        return lax.psum_scatter(grad, "row", scatter_dimension=0).astype(F32)

    out_eg = row_sum(grad_egate)
    out_eu = row_sum(grad_eup)
    out_ed = row_sum(grad_edown)
    return (
        output,
        grad_tokens,
        out_g_attn,
        out_wq,
        out_wk,
        out_wv,
        out_wo,
        out_g_moe,
        out_router,
        out_eg,
        out_eu,
        out_ed,
        out_sg,
        out_su,
        out_sd,
    )


def solution(mesh):
    both = P(("row", "col"), None)
    flat = P(("row", "col"))
    tile = P("row", "col")
    wide = P("col", "row", None)
    down = P("col", None, "row")
    return jax.shard_map(
        on_device,
        mesh=mesh,
        in_specs=(
            both, flat, tile, tile, tile, tile, flat, tile, wide, wide, down,
            tile, tile, tile, both, both, P(), both,
        ),
        out_specs=(
            both, both, flat, tile, tile, tile, tile, flat, tile, wide, wide, down,
            tile, tile, tile,
        ),
        check_vma=False,
    )
```

```python
import functools

import jax
import jax.numpy as jnp
from jax import lax
from jax.experimental import pallas as pl
from jax.experimental.pallas import tpu as pltpu
from jax.sharding import PartitionSpec as P

MODEL_WIDTH = 1536
QUERY_HEADS = 12
KEY_VALUE_HEADS = 4
GROUP = QUERY_HEADS // KEY_VALUE_HEADS
HEAD_SIZE = 128
TOP = 6
EXP_DEV = 4

norm_eps = 1e-05
masked_score = -1e30
BF = jnp.bfloat16
F32 = jnp.float32


def rms_scale(rows):
    return lax.rsqrt(jnp.mean(rows * rows, axis=-1, keepdims=True) + norm_eps)


def silu_parts(values):
    sigmoid_of = jax.nn.sigmoid(values)
    return (values * sigmoid_of, sigmoid_of * (1.0 + values * (1.0 - sigmoid_of)))


def norm_back(grad_normed, unit_rows, scale_rows, gain):
    grad_unit = grad_normed * gain
    grad_rows = scale_rows * (
        grad_unit - unit_rows * jnp.mean(grad_unit * unit_rows, axis=-1, keepdims=True)
    )
    return (grad_rows, jnp.sum(grad_normed * unit_rows, axis=0))


def mm(left, right):
    return jnp.dot(left, right, preferred_element_type=F32)


def mm_nt(left, right):
    return lax.dot_general(left, right, (((1,), (1,)), ((), ())), preferred_element_type=F32)


def mm_tn(left, right):
    return lax.dot_general(left, right, (((0,), (0,)), ((), ())), preferred_element_type=F32)


def ein(spec, a, b):
    return jnp.einsum(spec, a, b, preferred_element_type=F32)


def allowed_mask(seg_col, seg_row):
    total = seg_col.shape[0]
    q_at = lax.broadcasted_iota(jnp.int32, (total, total), 0)
    k_at = lax.broadcasted_iota(jnp.int32, (total, total), 1)
    return (seg_col == seg_row) & (k_at <= q_at)


def attend_forward_group(h, q_ref, k_ref, v_ref, allowed, mixed_ref, lse_ref):
    here = pl.ds(pl.multiple_of(h * HEAD_SIZE, HEAD_SIZE), HEAD_SIZE)
    keys = k_ref[:, here]
    values = v_ref[:, here]
    for g in range(GROUP):
        at = pl.multiple_of((h * GROUP + g) * HEAD_SIZE, HEAD_SIZE)
        cols = pl.ds(at, HEAD_SIZE)
        scores = mm_nt(q_ref[:, cols], keys) * HEAD_SIZE ** (-0.5)
        scores = jnp.where(allowed, scores, masked_score)
        peak = jnp.max(scores, axis=-1, keepdims=True)
        raw = jnp.exp(scores - peak)
        total = jnp.sum(raw, axis=-1, keepdims=True)
        probs = (raw * (1.0 / total)).astype(BF)
        mixed_ref[:, cols] = mm(probs, values).astype(BF)
        lse_ref[h, :, g : g + 1] = peak + jnp.log(total)


def attend_backward_group(h, q_ref, k_ref, v_ref, gm_ref, allowed, lse_ref, gq_ref, gk_ref, gv_ref):
    here = pl.ds(pl.multiple_of(h * HEAD_SIZE, HEAD_SIZE), HEAD_SIZE)
    keys = k_ref[:, here]
    values = v_ref[:, here]
    scale = HEAD_SIZE ** (-0.5)
    grad_key = grad_value = None
    for g in range(GROUP):
        at = pl.multiple_of((h * GROUP + g) * HEAD_SIZE, HEAD_SIZE)
        cols = pl.ds(at, HEAD_SIZE)
        query = q_ref[:, cols]
        grad_mixed = gm_ref[:, cols]
        scores = mm_nt(query, keys) * scale
        probs = jnp.where(allowed, jnp.exp(scores - lse_ref[h, :, g : g + 1]), 0.0)
        grad_probs = mm_nt(grad_mixed, values)
        inner = jnp.sum(probs * grad_probs, axis=-1, keepdims=True)
        grad_scores = (probs * (grad_probs - inner)).astype(BF)
        gq_ref[:, cols] = (mm(grad_scores, keys) * scale).astype(BF)
        part_key = mm_tn(grad_scores, query)
        part_value = mm_tn(probs.astype(BF), grad_mixed)
        grad_key = part_key if g == 0 else grad_key + part_key
        grad_value = part_value if g == 0 else grad_value + part_value
    gk_ref[:, here] = (grad_key * scale).astype(BF)
    gv_ref[:, here] = grad_value.astype(BF)


class DenseWeights:
    def __init__(self, full, extents):
        self.rows_n, self.cols_n, _, self.inner = full.shape
        self.extents = extents
        self.width = self.rows_n * self.inner
        self.cut = self.inner % 128 == 0
        self.operands = [full]
        if not self.cut:
            self.operands = []
            at = 0
            for extent in extents:
                part = full[:, :, at : at + extent].transpose(1, 2, 0, 3)
                self.operands.append(part.reshape(self.cols_n, extent, self.width))
                at += extent
        self.count = len(self.operands)
        self.scratch = [
            pltpu.VMEM((self.cols_n, extent, self.width), BF) for extent in extents
        ] + [pltpu.SemaphoreType.DMA((len(extents), self.rows_n))]

    def copies(self, sources, held, sems):
        made = []
        at = 0
        for part, extent in enumerate(self.extents):
            if self.cut:
                made.append(
                    [
                        pltpu.make_async_copy(
                            sources[0].at[r, :, pl.ds(at, extent), :],
                            held[part].at[:, :, pl.ds(r * self.inner, self.inner)],
                            sems.at[part, r],
                        )
                        for r in range(self.rows_n)
                    ]
                )
            else:
                made.append(
                    [pltpu.make_async_copy(sources[part], held[part], sems.at[part, 0])]
                )
            at += extent
        return made


ROW_STEP = 64


def flat(value):
    return value.reshape(value.shape[0] * value.shape[1], value.shape[2])


def route_columns(routes):
    return lax.div(routes, EXP_DEV) * 16 + lax.rem(routes, EXP_DEV)


def column_spans(width, count=KEY_VALUE_HEADS):
    step = width // count
    return [slice(at, at + step) for at in range(0, width, step)]


def block_start(tokens, full, extents, gains, segment, routes):
    total, width = tokens.shape
    weights = DenseWeights(full, extents)
    n = weights.count
    per_group = weights.cols_n // KEY_VALUE_HEADS

    def kernel(*refs):
        sources = refs[:n]
        (
            tok_ref, gain_ref, segc_ref, segr_ref, routes_ref,
            n1_ref, q_ref, k_ref, v_ref, mixed_ref, lse_ref, after_ref, n2_ref, s1_ref, s2_ref,
            gates_ref, gates_t_ref, *held, sems,
        ) = refs[n:]
        copies = weights.copies(sources, held, sems)
        for part in copies:
            for copy in part:
                copy.start()

        @pl.loop(0, total // ROW_STEP)
        def _(step):
            rows = pl.ds(pl.multiple_of(step * ROW_STEP, ROW_STEP), ROW_STEP)
            x = tok_ref[rows].astype(F32)
            scale = rms_scale(x)
            n1_ref[rows] = (x * scale * gain_ref[0:1]).astype(BF)
            s1_ref[rows] = scale

        for part in copies:
            for copy in part:
                copy.wait()
        normed = n1_ref[...]
        for h, cols in enumerate(column_spans(width)):
            mine = slice(h * per_group, (h + 1) * per_group)
            q_ref[:, cols] = mm_nt(normed, flat(held[0][mine])).astype(BF)
        k_ref[...] = mm_nt(normed, flat(held[1][...])).astype(BF)
        v_ref[...] = mm_nt(normed, flat(held[2][...])).astype(BF)
        allowed = allowed_mask(segc_ref[...], segr_ref[...])

        @pl.loop(0, KEY_VALUE_HEADS)
        def _(h):
            attend_forward_group(h, q_ref, k_ref, v_ref, allowed, mixed_ref, lse_ref)

        mixed = mixed_ref[...]
        for h, cols in enumerate(column_spans(width)):
            mine = slice(h * per_group, (h + 1) * per_group)
            after_ref[:, cols] = tok_ref[:, cols].astype(F32) + mm_nt(mixed, flat(held[3][mine]))

        @pl.loop(0, total // ROW_STEP)
        def _(step):
            rows = pl.ds(pl.multiple_of(step * ROW_STEP, ROW_STEP), ROW_STEP)
            after = after_ref[rows]
            scale = rms_scale(after)
            n2_ref[rows] = (after * scale * gain_ref[1:2]).astype(BF)
            s2_ref[rows] = scale

        logits = mm_nt(n2_ref[...], flat(held[4][...]))
        lane = lax.broadcasted_iota(jnp.int32, logits.shape, 1)
        goal = route_columns(routes_ref[...])
        chosen = [
            jnp.sum(jnp.where(lane == goal[:, i : i + 1], logits, 0.0), axis=1, keepdims=True)
            for i in range(TOP)
        ]
        peak = functools.reduce(jnp.maximum, chosen)
        raw = [jnp.exp(value - peak) for value in chosen]
        whole = functools.reduce(jnp.add, raw)
        lane = lax.broadcasted_iota(jnp.int32, (total, 128), 1)
        wide = jnp.zeros((total, 128), F32)
        for i in range(TOP):
            wide = jnp.where(lane == i, raw[i] / whole, wide)
        gates_ref[...] = wide[:, :8]
        gates_t_ref[...] = wide.T[:8]

    vmem = pl.BlockSpec(memory_space=pltpu.VMEM)
    kv = KEY_VALUE_HEADS * HEAD_SIZE
    shapes = [
        ((total, width), BF), ((total, width), BF), ((total, kv), BF), ((total, kv), BF),
        ((total, width), BF), ((KEY_VALUE_HEADS, total, GROUP), F32), ((total, width), F32),
        ((total, width), BF), ((total, 1), F32), ((total, 1), F32), ((total, 8), F32),
        ((8, total), F32),
    ]
    return pl.pallas_call(
        kernel,
        in_specs=[pl.BlockSpec(memory_space=pl.ANY)] * n + [vmem] * 5,
        out_specs=[vmem] * len(shapes),
        out_shape=[jax.ShapeDtypeStruct(shape, kind) for shape, kind in shapes],
        scratch_shapes=weights.scratch,
        compiler_params=pltpu.CompilerParams(vmem_limit_bytes=60 * 1024 * 1024),
        cost_estimate=pl.CostEstimate(
            flops=10_000_000_000, bytes_accessed=30_000_000, transcendentals=0
        ),
        name="block_start",
    )(*weights.operands, tokens, gains, segment[:, None], segment[None, :], routes)


def block_end(
    tokens, cotangent, full, extents, gains, segment, routes, gates, ggw, sums,
    queries, keys, values, log_totals, after, scale_one, scale_two,
):
    total, width = tokens.shape
    weights = DenseWeights(full, extents)
    n = weights.count
    chips = weights.cols_n // 2
    experts = ggw.shape[0]

    def kernel(*refs):
        sources = refs[:n]
        (
            tok_ref, dy_ref, gain_ref, segc_ref, segr_ref, routes_ref, gates_ref, ggw_ref,
            own_ref, other_ref, below_ref, above_ref, q_ref, k_ref, v_ref, lse_ref, after_ref,
            s1_ref, s2_ref,
            gtok_ref, gq_ref, gk_ref, gv_ref, gab_ref, glog_ref, ggain_ref,
            acc, grad_mixed, *held, sems,
        ) = refs[n:]
        copies = weights.copies(sources, held, sems)
        for part in (4, 3, 0, 1, 2):
            for copy in copies[part]:
                copy.start()
        chip = lax.div(lax.axis_index("col"), 2)
        not_first, not_last = chip > 0, chip < chips - 1

        per_expert = jnp.pad(ggw_ref[...], ((0, 128 - experts), (0, 0))).T
        lane = lax.broadcasted_iota(jnp.int32, (total, 128), 1)
        goals = routes_ref[...]
        weight = [gates_ref[:, i : i + 1] for i in range(TOP)]
        grads = [
            jnp.sum(jnp.where(lane == goals[:, i : i + 1], per_expert, 0.0), axis=1, keepdims=True)
            for i in range(TOP)
        ]
        mean = functools.reduce(jnp.add, [w * g for w, g in zip(weight, grads)])
        goals = route_columns(goals)
        lane = lax.broadcasted_iota(jnp.int32, glog_ref.shape, 1)
        spread = jnp.zeros(glog_ref.shape, F32)
        for i in range(TOP):
            spread = jnp.where(lane == goals[:, i : i + 1], weight[i] * (grads[i] - mean), spread)
        glog = spread.astype(BF)
        glog_ref[...] = glog
        for copy in copies[4]:
            copy.wait()
        for cols in column_spans(width):
            acc[:, cols] = mm(glog, flat(held[4][:, :, cols]))
        ggain_ref[...] = jnp.zeros_like(ggain_ref)

        @pl.loop(0, total // ROW_STEP)
        def _(step):
            rows = pl.ds(pl.multiple_of(step * ROW_STEP, ROW_STEP), ROW_STEP)
            grad = acc[rows] + own_ref[rows].astype(F32) + other_ref[rows].astype(F32)
            grad = grad + jnp.where(not_first, below_ref[rows].astype(F32), 0.0)
            grad = grad + jnp.where(not_last, above_ref[rows].astype(F32), 0.0)
            scale = s2_ref[rows]
            unit = after_ref[rows] * scale
            back, gain = norm_back(grad, unit, scale, gain_ref[1:2])
            ggain_ref[1:2] += gain[None]
            value = dy_ref[rows].astype(F32) + back
            acc[rows] = value
            gab_ref[rows] = value.astype(BF)

        for copy in copies[3]:
            copy.wait()
        rounded = gab_ref[...]
        for cols in column_spans(width):
            grad_mixed[:, cols] = mm(rounded, flat(held[3][:, :, cols])).astype(BF)
        allowed = allowed_mask(segc_ref[...], segr_ref[...])

        @pl.loop(0, KEY_VALUE_HEADS)
        def _(h):
            attend_backward_group(
                h, q_ref, k_ref, v_ref, grad_mixed, allowed, lse_ref, gq_ref, gk_ref, gv_ref
            )

        for part in range(3):
            for copy in copies[part]:
                copy.wait()
        for cols in column_spans(width):
            gtok_ref[:, cols] = (
                mm(gq_ref[...], flat(held[0][:, :, cols]))
                + mm(gk_ref[...], flat(held[1][:, :, cols]))
                + mm(gv_ref[...], flat(held[2][:, :, cols]))
            )

        @pl.loop(0, total // ROW_STEP)
        def _(step):
            rows = pl.ds(pl.multiple_of(step * ROW_STEP, ROW_STEP), ROW_STEP)
            scale = s1_ref[rows]
            unit = tok_ref[rows].astype(F32) * scale
            back, gain = norm_back(gtok_ref[rows], unit, scale, gain_ref[0:1])
            ggain_ref[0:1] += gain[None]
            gtok_ref[rows] = acc[rows] + back

    vmem = pl.BlockSpec(memory_space=pltpu.VMEM)
    kv = KEY_VALUE_HEADS * HEAD_SIZE
    shapes = [
        ((total, width), F32), ((total, width), BF), ((total, kv), BF), ((total, kv), BF),
        ((total, width), BF), ((total, weights.cols_n * 16), BF), ((2, width), F32),
    ]
    args = (
        tokens, cotangent, gains, segment[:, None], segment[None, :], routes, gates, ggw, *sums,
        queries, keys, values, log_totals, after, scale_one, scale_two,
    )
    return pl.pallas_call(
        kernel,
        in_specs=[pl.BlockSpec(memory_space=pl.ANY)] * n + [vmem] * len(args),
        out_specs=[vmem] * len(shapes),
        out_shape=[jax.ShapeDtypeStruct(shape, kind) for shape, kind in shapes],
        scratch_shapes=[pltpu.VMEM((total, width), F32), pltpu.VMEM((total, width), BF)]
        + weights.scratch,
        compiler_params=pltpu.CompilerParams(vmem_limit_bytes=60 * 1024 * 1024),
        cost_estimate=pl.CostEstimate(
            flops=20_000_000_000, bytes_accessed=40_000_000, transcendentals=0
        ),
        name="block_end",
    )(*weights.operands, *args)


def remote(src, dst, send_sem, recv_sem, device):
    return pltpu.make_async_remote_copy(
        src_ref=src,
        dst_ref=dst,
        send_sem=send_sem,
        recv_sem=recv_sem,
        device_id=device,
        device_id_type=pl.DeviceIdType.MESH,
    )


class Place:
    def __init__(self, rows_n, cols_n):
        self.rows_n = rows_n
        self.chips = cols_n // 2
        self.row = lax.axis_index("row")
        self.col = lax.axis_index("col")
        self.chip = lax.div(self.col, 2)
        self.core = lax.rem(self.col, 2)
        self.other = self.col + 1 - 2 * self.core

    def peer_row(self, step):
        return lax.rem(self.row + step, self.rows_n)

    def square(self):
        across = self.row + 1 - 2 * lax.rem(self.row, 2)
        along = lax.rem(self.row + 2, 4)
        return across, along, along + 1 - 2 * lax.rem(along, 2)

    def greet(self, with_rows, downs_back=0):
        barrier = pltpu.get_barrier_semaphore()

        def hello(row, col):
            pl.semaphore_signal(
                barrier, inc=1, device_id=(row, col), device_id_type=pl.DeviceIdType.MESH
            )

        hello(self.row, self.other)

        @pl.when(self.chip > 0)
        def _():
            hello(self.row, self.col - 2)

        @pl.when(self.chip < self.chips - 1)
        def _():
            hello(self.row, self.col + 2)

        count = (
            1
            + (self.chip > 0).astype(jnp.int32)
            + (self.chip < self.chips - 1).astype(jnp.int32)
        )
        if with_rows:
            for step in range(1, self.rows_n):
                hello(self.peer_row(step), self.col)
            count = count + (self.rows_n - 1)
        if downs_back:
            goal = lax.div(self.col, downs_back)
            for turn in range(downs_back):
                goal_col = downs_back * self.row + turn

                @pl.when(jnp.logical_not((goal == self.row) & (goal_col == self.col)))
                def _():
                    hello(goal, goal_col)

            count = count + downs_back - (goal == self.row).astype(jnp.int32)
        pl.semaphore_wait(barrier, count)


class Moves:
    def __init__(self, place, up, down, from_below, from_above, send_sems, recv_sems):
        self.place = place
        self.copies = [
            remote(
                src, dst, send_sems.at[which], recv_sems.at[which],
                (place.row, place.col + way),
            )
            for which, (src, dst, way) in enumerate(
                ((up, from_below, 2), (down, from_above, -2))
            )
        ]
        self.ends = (place.chip < place.chips - 1, place.chip > 0)

    def start(self):
        for which in range(2):

            @pl.when(self.ends[which])
            def _():
                self.copies[which].start()

    def wait_send(self):
        for which in range(2):

            @pl.when(self.ends[which])
            def _():
                self.copies[which].wait_send()

    def wait_recv(self):
        for which in range(2):

            @pl.when(self.ends[1 - which])
            def _():
                self.copies[which].wait_recv()


class RoundStart:
    PARTS = 4

    def __init__(self, place, call_refs, after, held, came, brought, load_sems, sends, recvs):
        self.place, self.call_refs, self.after = place, call_refs, after
        self.held, self.came, self.brought = held, came, brought
        self.load_sems, self.sends, self.recvs = load_sems, sends, recvs
        self.tables = round_tables(place.chips)[1:]
        self.leaves = (place.chip < place.chips - 1, place.chip > 0)
        self.comes = (place.chip > 0, place.chip < place.chips - 1)

    def loads(self, which, call):
        pair = (self.held, self.came)
        return [
            pltpu.make_async_copy(
                self.call_refs[2 * call + i].at[1], pair[i].at[which], self.load_sems.at[which, i]
            )
            for i in range(2)
        ]

    def earlier(self, which, before):
        return pltpu.make_async_copy(
            before[which], self.brought.at[which], self.load_sems.at[which, 2]
        )

    def copy(self, which, part):
        rows = self.held.shape[1] // self.PARTS
        span = pl.ds(part * rows, rows)
        return remote(
            self.held.at[which, span], self.after[which].at[span], self.sends.at[which, part],
            self.recvs.at[which, part],
            (self.place.row, self.place.col + (2, -2)[which]),
        )

    def load(self, turn, before):
        for which in range(2):
            call = jnp.int32(0)
            for chip in range(self.place.chips):
                number = self.tables[which][chip][turn]
                call = call + jnp.where(self.place.chip == chip, number, 0)
            for i in range(turn + 1):

                @pl.when(call == i)
                def _():
                    for copy in self.loads(which, i):
                        copy.start()

            if before:

                @pl.when(self.comes[which])
                def _():
                    self.earlier(which, before).start()

    def send(self, before):
        for which in range(2):
            for copy in self.loads(which, 0):
                copy.wait()
            if before:

                @pl.when(self.comes[which])
                def _():
                    self.earlier(which, before).wait()

        rows = self.held.shape[1] // self.PARTS
        for part in range(self.PARTS):
            span = slice(part * rows, (part + 1) * rows)
            for which in range(2):

                @pl.when(self.leaves[which])
                def _():
                    total = self.held[which, span].astype(F32) + self.came[which, span].astype(F32)
                    if before:
                        more = self.brought[which, span].astype(F32)
                        total = total + jnp.where(self.comes[which], more, 0.0)
                    self.held[which, span] = total.astype(BF)
                    self.copy(which, part).start()

    def wait(self):
        for which in range(2):
            for part in range(self.PARTS):

                @pl.when(self.leaves[which])
                def _():
                    self.copy(which, part).wait_send()

                @pl.when(self.comes[which])
                def _():
                    self.copy(which, part).wait_recv()

    @classmethod
    def scratch(cls, block):
        return [
            pltpu.VMEM((2,) + block, BF),
            pltpu.VMEM((2,) + block, BF),
            pltpu.VMEM((2,) + block, BF),
            pltpu.SemaphoreType.DMA((2, 3)),
            pltpu.SemaphoreType.DMA((2, cls.PARTS)),
            pltpu.SemaphoreType.DMA((2, cls.PARTS)),
        ]


class LineGather:
    def __init__(self, place, src, dst, core_sems, line_sems, recv_sems, local_sem):
        self.at = place
        self.src, self.dst = src, dst
        self.core_sems, self.line_sems, self.recv_sems = core_sems, line_sems, recv_sems
        self.local = pltpu.make_async_copy(src, dst.at[place.col], local_sem)

    def to_core(self, block, src=None):
        at = self.at
        src = self.dst.at[block] if src is None else src
        return remote(
            src, self.dst.at[block], self.core_sems.at[block], self.recv_sems.at[block],
            (at.row, at.other),
        )

    def to_line(self, block, way, src=None):
        at = self.at
        src = self.dst.at[block] if src is None else src
        return remote(
            src,
            self.dst.at[block],
            self.line_sems.at[block, (way + 1) // 2],
            self.recv_sems.at[block],
            (at.row, at.col + 2 * way),
        )

    def ends(self, way):
        return self.at.chip < self.at.chips - 1 if way > 0 else self.at.chip > 0

    def start(self):
        self.local.start()
        for way in (1, -1):

            @pl.when(self.ends(way))
            def _():
                self.to_line(self.at.col, way, self.src).start()

        self.to_core(self.at.col, self.src).start()

    def arrivals(self, dist, act):
        for way in (1, -1):
            chip = self.at.chip - way * dist
            near = chip >= 0 if way > 0 else chip < self.at.chips

            @pl.when(near)
            def _():
                act(2 * chip + self.at.core, way)

    def step(self, dist, extra=None):
        def act(block, way):
            self.to_core(block).wait_recv()

            @pl.when(self.ends(way))
            def _():
                self.to_line(block, way).start()

            self.to_core(block).start()
            if extra is not None:
                extra(block)

        self.arrivals(dist, act)

    def finish(self):
        self.local.wait()
        self.to_core(self.at.col, self.src).wait_send()
        for way in (1, -1):

            @pl.when(self.ends(way))
            def _():
                self.to_line(self.at.col, way, self.src).wait_send()

        def act(block, way):
            self.to_core(block).wait_send()

            @pl.when(self.ends(way))
            def _():
                self.to_line(block, way).wait_send()

        for dist in range(1, self.at.chips):
            self.arrivals(dist, act)
        for chip in range(self.at.chips):
            self.to_core(2 * chip + 1 - self.at.core).wait_recv()


def gather_sems(cols_n):
    return [
        pltpu.SemaphoreType.DMA((cols_n,)),
        pltpu.SemaphoreType.DMA((cols_n, 2)),
        pltpu.SemaphoreType.DMA((cols_n,)),
        pltpu.SemaphoreType.DMA,
    ]


ANY = pl.BlockSpec(memory_space=pl.ANY)


def line_gather(arrays, collective_id, rows_n, cols_n):
    n = len(arrays)

    def kernel(*refs):
        srcs, dsts, sems = refs[:n], refs[n : 2 * n], refs[2 * n :]
        place = Place(rows_n, cols_n)
        place.greet(False)
        jobs = [
            LineGather(place, srcs[i], dsts[i], *sems[4 * i : 4 * i + 4]) for i in range(n)
        ]
        for job in jobs:
            job.start()
        for dist in range(1, place.chips):
            for job in jobs:
                job.step(dist)
        for job in jobs:
            job.finish()

    return pl.pallas_call(
        kernel,
        in_specs=[ANY] * n,
        out_specs=[ANY] * n,
        out_shape=[jax.ShapeDtypeStruct((cols_n,) + a.shape, a.dtype) for a in arrays],
        scratch_shapes=gather_sems(cols_n) * n,
        compiler_params=pltpu.CompilerParams(collective_id=collective_id, has_side_effects=True),
        name="line_gather",
    )(*arrays)


def first_gather(
    bundle, cotangent, routes_t, shared, downs, expert, later, collective_id, rows_n, cols_n
):
    per_row = downs.shape[0]
    square = rows_n == 4
    n_goals = 2 if square else rows_n - 1
    n_later = len(later)
    inner = expert.shape[1]
    half_experts = expert.shape[0] // 2

    def kernel(*refs):
        bundle_ref, dy_ref, rt_ref, sh_ref, sd_ref, ex_ref = refs[:6]
        refs = refs[6 + n_later :]
        full_ref, dy_all, rt_all, sh_all, sd_all, ex_all = refs[:6]
        down_line, *sems = refs[6 + n_later :]
        place = Place(rows_n, cols_n)
        b_sems, sems = sems[:4], sems[4:]
        d_sems, sems = sems[:4], sems[4:]
        r_sems, sems = sems[:4], sems[4:]
        l_sems, sems = sems[:4], sems[4:]
        (
            row_send, row_core, row_recv, sh_send, sh_recv, sh_local, sd_send, sd_recv,
            sd_local, ex_send, ex_recv, ex_local,
        ) = sems
        place.greet(True)
        row, col = place.row, place.col
        across = along = corner = None
        goals = [place.peer_row(step) for step in range(1, rows_n)]
        sources = goals
        if square:
            across, along, corner = place.square()
            goals, sources = [across, along], [across, along, corner]
        weights = LineGather(place, bundle_ref, full_ref.at[row], *b_sems)
        grads = LineGather(place, dy_ref, dy_all, *d_sems)
        picks = LineGather(place, rt_ref, rt_all, *r_sems)

        def to_row(block, n, src=None):
            home = full_ref.at[row, block]
            return remote(
                home if src is None else src, home, row_send.at[block, n],
                row_recv.at[row, block], (goals[n], col),
            )

        def push(block, src=None):
            for n in range(n_goals):
                to_row(block, n, src).start()

        def from_row(source, block):
            home = full_ref.at[source, block]
            return remote(
                home, home, row_core.at[source, block], row_recv.at[source, block],
                (row, place.other),
            )

        def onward(source, block, goal):
            home = full_ref.at[source, block]
            return remote(
                home, home, row_send.at[block, 2], row_recv.at[source, block], (goal, col)
            )

        def take(source, block):
            copy = from_row(source, block)
            copy.wait_recv()
            copy.start()

        def expert_rows(source, half):
            return ex_all.at[
                pl.ds(half * half_experts, half_experts),
                pl.ds(pl.multiple_of(source * inner, inner), inner),
            ]

        def expert_to(n, half):
            return remote(
                ex_ref.at[pl.ds(half * half_experts, half_experts)], expert_rows(row, half),
                ex_send.at[n, half], ex_recv.at[row, half], (goals[n], col),
            )

        def expert_onward(source, half, goal):
            home = expert_rows(source, half)
            return remote(
                home, home, ex_send.at[2, half], ex_recv.at[source, half], (goal, col)
            )

        def shared_to(step):
            return remote(
                sh_ref, sh_all.at[row], sh_send.at[step], sh_recv.at[row],
                (place.peer_row(step), col),
            )

        lines = LineGather(place, sd_ref, down_line, *l_sems)
        holder = lax.div(col, per_row) == row
        pieces = down_line.at[:, lax.rem(col, per_row)]
        pieces_here = pltpu.make_async_copy(pieces, sd_all, sd_local)

        def downs_to(step):
            return remote(
                pieces, sd_all, sd_send.at[step], sd_recv, (place.peer_row(step), col)
            )

        weights.start()
        push(col, bundle_ref)
        if square:
            for n, half in ((0, 0), (1, 1)):
                expert_to(n, half).start()
        lines.start()
        for dist in range(1, place.chips):
            weights.step(dist, push)
            lines.step(dist)
        grads.start()
        picks.start()
        lines.finish()

        @pl.when(holder)
        def _():
            pieces_here.start()
            for step in range(1, rows_n):
                downs_to(step).start()

        if square:
            for n, half in ((0, 1), (1, 0)):
                expert_to(n, half).start()
        else:
            for n in range(n_goals):
                for half in range(2):
                    expert_to(n, half).start()
        shared_here = pltpu.make_async_copy(sh_ref, sh_all.at[row], sh_local)
        shared_here.start()
        expert_here = [
            pltpu.make_async_copy(
                ex_ref.at[pl.ds(half * half_experts, half_experts)], expert_rows(row, half),
                ex_local.at[half],
            )
            for half in range(2)
        ]
        for copy in expert_here:
            copy.start()
        for step in range(1, rows_n):
            shared_to(step).start()
        for dist in range(1, place.chips - 1):
            grads.step(dist)
            picks.step(dist)
            if square and dist == 1:

                @pl.loop(0, place.chips)
                def _(i):
                    chip = lax.rem(place.chip + i, place.chips)
                    block = 2 * chip + place.core
                    even = lax.rem(chip, 2) == 0
                    take(across, block)

                    @pl.when(even)
                    def _():
                        onward(across, block, along).start()

                    take(along, block)

                    @pl.when(jnp.logical_not(even))
                    def _():
                        onward(along, block, across).start()

                expert_onward(across, 0, along).wait_recv()
                expert_onward(across, 0, along).start()
                expert_onward(along, 1, across).wait_recv()
                expert_onward(along, 1, across).start()
        for source in [corner] if square else sources:

            @pl.loop(0, place.chips)
            def _(chip):
                take(source, 2 * chip + place.core)

        grads.step(place.chips - 1)
        picks.step(place.chips - 1)
        weights.finish()
        grads.finish()
        picks.finish()
        shared_here.wait()
        for copy in expert_here:
            copy.wait()

        @pl.when(holder)
        def _():
            pieces_here.wait()
            for step in range(1, rows_n):
                downs_to(step).wait_send()

        @pl.when(jnp.logical_not(holder))
        def _():
            downs_to(1).wait_recv()

        for n in range(n_goals):
            for half in range(2):
                expert_to(n, half).wait_send()
        if square:
            expert_onward(across, 0, along).wait_send()
            expert_onward(along, 1, across).wait_send()
            expert_onward(across, 1, along).wait_recv()
            expert_onward(along, 0, across).wait_recv()
            expert_onward(corner, 0, along).wait_recv()
            expert_onward(corner, 1, along).wait_recv()
        else:
            for source in sources:
                for half in range(2):
                    expert_onward(source, half, source).wait_recv()
        for step in range(1, rows_n):
            other_row = place.peer_row(step)
            shared_to(step).wait_send()
            remote(
                sh_ref, sh_all.at[other_row], sh_send.at[0], sh_recv.at[other_row],
                (other_row, col),
            ).wait_recv()

        @pl.loop(0, place.chips)
        def _(chip):
            block = 2 * chip + place.core
            for n in range(n_goals):
                to_row(block, n).wait_send()
            if square:
                onward(across, block, along).wait_send()
            for source in sources:
                from_row(source, block).wait_send()
                from_row(source, 2 * chip + 1 - place.core).wait_recv()

    outs = [
        jax.ShapeDtypeStruct((rows_n, cols_n) + bundle.shape, bundle.dtype),
        jax.ShapeDtypeStruct((cols_n,) + cotangent.shape, cotangent.dtype),
        jax.ShapeDtypeStruct((cols_n,) + routes_t.shape, routes_t.dtype),
        jax.ShapeDtypeStruct((rows_n,) + shared.shape, shared.dtype),
        jax.ShapeDtypeStruct((cols_n,) + downs.shape[1:], downs.dtype),
        jax.ShapeDtypeStruct(
            (expert.shape[0], rows_n * inner, expert.shape[2]), expert.dtype
        ),
    ] + [jax.ShapeDtypeStruct(a.shape, a.dtype) for a in later]
    outs.append(jax.ShapeDtypeStruct((cols_n,) + downs.shape, downs.dtype))
    return pl.pallas_call(
        kernel,
        in_specs=[ANY] * (6 + n_later),
        out_specs=[ANY] * (7 + n_later),
        out_shape=outs,
        input_output_aliases={6 + i: 6 + i for i in range(n_later)},
        scratch_shapes=gather_sems(cols_n) * 4
        + [
            pltpu.SemaphoreType.DMA((cols_n, max(rows_n, 3))),
            pltpu.SemaphoreType.DMA((rows_n, cols_n)),
            pltpu.SemaphoreType.DMA((rows_n, cols_n)),
            pltpu.SemaphoreType.DMA((rows_n,)),
            pltpu.SemaphoreType.DMA((rows_n,)),
            pltpu.SemaphoreType.DMA,
            pltpu.SemaphoreType.DMA((rows_n,)),
            pltpu.SemaphoreType.DMA,
            pltpu.SemaphoreType.DMA,
            pltpu.SemaphoreType.DMA((max(rows_n, 3), 2)),
            pltpu.SemaphoreType.DMA((rows_n, 2)),
            pltpu.SemaphoreType.DMA((2,)),
        ],
        compiler_params=pltpu.CompilerParams(collective_id=collective_id, has_side_effects=True),
        name="first_gather",
    )(bundle, cotangent, routes_t, shared, downs, expert, *later)


def line_sum_loop(place, mine, recv, send_sems, recv_sems, parts, ready):
    chips, here = place.chips, place.chip
    rows = mine.shape[1] // parts
    items = (chips - 1) * parts

    def copy(chip, part, way):
        span = pl.ds(part * rows, rows)
        goal = here + way
        land = chip if way > 0 else jnp.where(chip == goal, chips, chip)
        return remote(
            mine.at[chip, span],
            recv.at[land, span],
            send_sems.at[chip, part],
            recv_sems.at[land, part],
            (place.row, place.col + 2 * way),
        )

    def incoming(land, part):
        span = pl.ds(part * rows, rows)
        return remote(
            mine.at[0, span], recv.at[land, span], send_sems.at[0, part],
            recv_sems.at[land, part], (place.row, place.other),
        )

    def handle(chip, part, way):
        @pl.when(part == 0)
        def _():
            ready(chip)

        span = pl.ds(part * rows, rows)
        comes = here > 0 if way > 0 else here < chips - 1

        @pl.when(comes)
        def _():
            incoming(chip, part).wait_recv()
            total = mine[chip, span].astype(F32) + recv[chip, span].astype(F32)
            mine[chip, span] = total.astype(mine.dtype)

        copy(chip, part, way).start()

    lag = 2 * (chips - 2 - here)

    @pl.loop(0, items + 2 * (chips - 2))
    def _(at):
        up = jnp.minimum(at, items - 1)
        up_chip = chips - 1 - lax.div(up, parts)

        @pl.when((at < items) & (up_chip > here))
        def _():
            handle(up_chip, lax.rem(up, parts), 1)

        down = at - jnp.maximum(lag, 0)
        safe = jnp.clip(down, 0, items - 1)
        down_chip = lax.div(safe, parts)

        @pl.when((down >= 0) & (down < items) & (down_chip < here))
        def _():
            handle(down_chip, lax.rem(safe, parts), -1)

    ready(here)

    def result(part, store):
        span = pl.ds(part * rows, rows)
        total = mine[here, span].astype(F32)

        @pl.when((here > 0) & (here < chips - 1))
        def _():
            incoming(here, part).wait_recv()
            incoming(chips, part).wait_recv()
            store(span, total + recv[here, span].astype(F32) + recv[chips, span].astype(F32))

        @pl.when((here > 0) & (here == chips - 1))
        def _():
            incoming(here, part).wait_recv()
            store(span, total + recv[here, span].astype(F32))

        @pl.when((here == 0) & (here < chips - 1))
        def _():
            incoming(chips, part).wait_recv()
            store(span, total + recv[chips, span].astype(F32))

    def drain():
        @pl.loop(0, chips)
        def _(chip):
            for part in range(parts):

                @pl.when(chip > here)
                def _():
                    copy(chip, part, 1).wait_send()

                @pl.when(chip < here)
                def _():
                    copy(chip, part, -1).wait_send()

    return result, drain


def dense_sum(lefts, rights, tails, shared, calls, collective_id, rows_n, cols_n):
    chips = cols_n // 2
    n_rounds = chips - 1
    moved = jax.ShapeDtypeStruct(calls[0][0].shape[1:], BF)
    square = rows_n == 4
    inner = shared.shape[1]
    units = shared.shape[2] // 3
    per_row = cols_n // rows_n
    extents = [left.shape[1] // cols_n for left in lefts]
    block = (sum(extents), inner)
    n = len(lefts)

    def kernel(*refs):
        left_refs, right_refs = refs[:n], refs[n : 2 * n]
        (
            tail_ref, sh_ref, *call_refs
        ) = refs[2 * n : 2 * n + 2 + 2 * chips]
        (
            out_ref, sh_out, sd_out, arrivals,
            both, extra, rows_in, recv, sh_in, sd_cut, held, came, held_sems, came_sems,
            core_send, core_recv, row_send, row_recv, send_sems, recv_sems,
            sh_send, sh_recv, sh_local, move_send, move_recv, sd_send, sd_recv,
        ) = refs[2 * n + 2 + 2 * chips :]
        place = Place(rows_n, cols_n)
        row, col = place.row, place.col
        mine = both.at[place.core]
        shared_here = pltpu.make_async_copy(sh_ref.at[row], sh_in.at[row], sh_local)
        shared_here.start()
        down_row = lax.div(col, per_row)
        place.greet(True, downs_back=per_row)

        tables = round_tables(chips)[1:]

        def moves(turn):
            return Moves(
                place, held.at[0], held.at[1], arrivals.at[turn, 0], arrivals.at[turn, 1],
                move_send.at[turn], move_recv.at[turn],
            )

        def add_came(which):
            part = came.shape[1] // 4
            for at in range(0, came.shape[1], part):
                span = slice(at, at + part)
                held[which, span] = (
                    held[which, span].astype(F32) + came[which, span].astype(F32)
                ).astype(BF)

        def bring(which, own, other):
            return (
                pltpu.make_async_copy(own, held.at[which], held_sems.at[which]),
                pltpu.make_async_copy(other, came.at[which], came_sems.at[which]),
            )

        def next_round(turn):
            if turn:
                moves(turn - 1).wait_send()
            for which in range(2):
                call = jnp.int32(0)
                for chip in range(chips):
                    call = call + jnp.where(place.chip == chip, tables[which][chip][turn], 0)
                for i in range(turn + 1):

                    @pl.when(call == i)
                    def _():
                        for copy in bring(which, call_refs[2 * i].at[0], call_refs[2 * i + 1].at[0]):
                            copy.start()

            for which in range(2):
                for copy in bring(which, call_refs[0].at[0], call_refs[1].at[0]):
                    copy.wait()
                add_came(which)
            if turn:
                moves(turn - 1).wait_recv()
                comes = (place.chip > 0, place.chip < chips - 1)
                for which in range(2):

                    @pl.when(comes[which])
                    def _():
                        pltpu.make_async_copy(
                            arrivals.at[turn - 1, which], came.at[which], came_sems.at[which]
                        ).start()

                for which in range(2):

                    @pl.when(comes[which])
                    def _():
                        pltpu.make_async_copy(
                            arrivals.at[turn - 1, which], came.at[which], came_sems.at[which]
                        ).wait()
                        add_came(which)

            moves(turn).start()

        next_round(0)

        def downs_to(turn, act_far, act_here):
            goal_col = per_row * row + turn
            here = (goal_col == col) & (down_row == row)
            source = lax.rem(col, per_row)

            @pl.when(here)
            def _():
                act_here(
                    pltpu.make_async_copy(
                        sd_cut.at[turn], sd_out.at[source], sd_recv.at[source]
                    )
                )

            @pl.when(jnp.logical_not(here))
            def _():
                act_far(
                    remote(
                        sd_cut.at[turn], sd_out.at[source], sd_send.at[turn],
                        sd_recv.at[source], (down_row, goal_col),
                    )
                )

        def swap(goal):
            return remote(
                both.at[1 - place.core, goal], extra.at[goal], core_send.at[goal],
                core_recv.at[goal], (row, place.other),
            )

        def shared_to(step):
            goal = place.peer_row(step)
            return remote(
                sh_ref.at[goal], sh_in.at[row], sh_send.at[step], sh_recv.at[row], (goal, col)
            )

        def shared_from(step):
            source = place.peer_row(step)
            return remote(
                sh_ref.at[source], sh_in.at[source], sh_send.at[0], sh_recv.at[source],
                (source, col),
            )

        across = along = corner = None
        if square:
            across, along, corner = place.square()

        def ways(chip):
            return (across, along) if chip % 2 == 0 else (along, across)

        def to_near(goal, slot, chip):
            near = ways(chip)[1 if slot == 2 else 0]
            return remote(
                mine.at[goal, chip], rows_in.at[slot, chip], row_send.at[slot, chip],
                row_recv.at[slot, chip], (near, col),
            )

        def to_row(goal, chip):
            return remote(
                mine.at[goal, chip], rows_in.at[row, chip], row_send.at[goal, chip],
                row_recv.at[row, chip], (goal, col),
            )

        def from_row(step, chip):
            source = place.peer_row(step)
            return remote(
                mine.at[source, chip], rows_in.at[source, chip], row_send.at[0, chip],
                row_recv.at[source, chip], (source, col),
            )

        order = []
        for i in range((chips + 1) // 2):
            order += [chips - 1 - i, i] if chips - 1 - i != i else [i]

        def push(goal):
            swap(goal).wait_recv()

            @pl.when(goal != row)
            def _():
                for chip in order:
                    mine[goal, chip] = (
                        mine[goal, chip].astype(F32) + extra[goal, chip].astype(F32)
                    ).astype(BF)
                    if not square:
                        to_row(goal, chip).start()
                        continue

                    @pl.when(goal == ways(chip)[0])
                    def _():
                        to_near(goal, 0, chip).start()

                    @pl.when(goal == corner)
                    def _():
                        to_near(goal, 1, chip).start()

        def hand_on():
            for chip in order:
                goal = ways(chip)[1]
                to_near(goal, 1, chip).wait_recv()
                mine[goal, chip] = (
                    mine[goal, chip].astype(F32) + rows_in[1, chip].astype(F32)
                ).astype(BF)
                to_near(goal, 2, chip).start()

        for step in range(1, rows_n):
            shared_to(step).start()
        for goal in range(rows_n):
            cols = slice(goal * inner, (goal + 1) * inner)
            at = 0
            for i in range(n):
                made = mm_tn(left_refs[i][...], right_refs[i][:, cols])
                if i == n - 1:
                    made = made + tail_ref[goal]
                made = made.astype(BF)
                for owner in range(cols_n):
                    both[owner % 2, goal, owner // 2, at : at + extents[i], :] = made[
                        owner * extents[i] : (owner + 1) * extents[i]
                    ]
                at += extents[i]
            swap(goal).start()
            if goal > 0:
                push(goal - 1)
        push(rows_n - 1)
        for turn in range(1, n_rounds):
            next_round(turn)
            if square and turn == 1:
                hand_on()
        shared_here.wait()
        for step in range(1, rows_n):
            shared_from(step).wait_recv()
        total = sh_in[0].astype(F32)
        for other in range(1, rows_n):
            total = total + sh_in[other].astype(F32)
        sh_out[...] = total[:, : 2 * units]
        cut = inner // per_row
        for turn in range(per_row):
            sd_cut[turn] = total[turn * cut : (turn + 1) * cut, 2 * units :]
            downs_to(turn, lambda far: far.start(), lambda here: here.start())

        def ready(chip):
            total = mine[row, chip].astype(F32) + extra[row, chip].astype(F32)
            if square:
                for slot in (0, 2):
                    remote(
                        mine.at[row, chip], rows_in.at[slot, chip], row_send.at[slot, chip],
                        row_recv.at[slot, chip], (across, col),
                    ).wait_recv()
                    total = total + rows_in[slot, chip].astype(F32)
            else:
                for step in range(1, rows_n):
                    from_row(step, chip).wait_recv()
                    total = total + rows_in[place.peer_row(step), chip].astype(F32)
            mine[row, chip] = total.astype(BF)

        result, drain = line_sum_loop(
            place, mine.at[row], recv, send_sems, recv_sems, 1, ready
        )

        def store(span, value):
            out_ref[span] = value

        result(0, store)
        drain()

        moves(n_rounds - 1).wait_send()
        moves(n_rounds - 1).wait_recv()
        for turn in range(per_row):
            downs_to(turn, lambda far: far.wait_send(), lambda here: here.wait())
            at_home = per_row * row + turn
            mine_here = (at_home == col) & (down_row == row)

            @pl.when(jnp.logical_not(mine_here))
            def _():
                remote(
                    sd_cut.at[0], sd_out.at[turn], sd_send.at[turn], sd_recv.at[turn],
                    (down_row, at_home),
                ).wait_recv()

        for step in range(1, rows_n):
            shared_to(step).wait_send()
        for goal in range(rows_n):
            swap(goal).wait_send()

            if not square:

                @pl.when(goal != row)
                def _():
                    for chip in range(chips):
                        to_row(goal, chip).wait_send()

        if square:
            for chip in range(chips):
                for slot in range(3):
                    to_near(row, slot, chip).wait_send()

    vmem = pl.BlockSpec(memory_space=pltpu.VMEM)
    return pl.pallas_call(
        kernel,
        in_specs=[vmem] * (2 * n + 1) + [ANY] * (1 + 2 * chips),
        out_specs=[vmem, vmem, vmem, ANY],
        out_shape=[
            jax.ShapeDtypeStruct(block, F32),
            jax.ShapeDtypeStruct((inner, 2 * units), F32),
            jax.ShapeDtypeStruct((per_row, inner // per_row, units), F32),
            jax.ShapeDtypeStruct((n_rounds, 2) + moved.shape, moved.dtype),
        ],
        scratch_shapes=[
            pltpu.VMEM((2, rows_n, chips) + block, BF),
            pltpu.VMEM((rows_n, chips) + block, BF),
            pltpu.VMEM((rows_n, chips) + block, BF),
            pltpu.VMEM((chips + 1,) + block, BF),
            pltpu.VMEM(shared.shape, BF),
            pltpu.VMEM((per_row, inner // per_row, units), F32),
            pltpu.VMEM((2,) + moved.shape, BF),
            pltpu.VMEM((2,) + moved.shape, BF),
            pltpu.SemaphoreType.DMA((2,)),
            pltpu.SemaphoreType.DMA((2,)),
            pltpu.SemaphoreType.DMA((rows_n,)),
            pltpu.SemaphoreType.DMA((rows_n,)),
            pltpu.SemaphoreType.DMA((rows_n, chips)),
            pltpu.SemaphoreType.DMA((rows_n, chips)),
            pltpu.SemaphoreType.DMA((chips, 1)),
            pltpu.SemaphoreType.DMA((chips + 1, 1)),
            pltpu.SemaphoreType.DMA((rows_n,)),
            pltpu.SemaphoreType.DMA((rows_n,)),
            pltpu.SemaphoreType.DMA,
            pltpu.SemaphoreType.DMA((n_rounds, 2)),
            pltpu.SemaphoreType.DMA((n_rounds, 2)),
            pltpu.SemaphoreType.DMA((per_row,)),
            pltpu.SemaphoreType.DMA((per_row,)),
        ],
        compiler_params=pltpu.CompilerParams(
            collective_id=collective_id, has_side_effects=True,
            vmem_limit_bytes=60 * 1024 * 1024,
        ),
        cost_estimate=pl.CostEstimate(
            flops=2 * 512 * 1536 * 4096, bytes_accessed=350_000_000, transcendentals=0
        ),
        name="dense_sum",
    )(*lefts, *rights, tails, shared, *[part for pair in calls for part in pair])


def round_tables(chips):
    order, up, down = [], [], []
    for here in range(chips):
        due = {q: chips - 1 - q + here for q in range(here + 1, chips)}
        due.update({q: q + chips - 1 - here for q in range(here)})
        calls = sorted(due, key=lambda q: (due[q], -q)) + [here]
        order.append(calls)
        at = {q: i for i, q in enumerate(calls)}
        up.append([at.get(chips - 1 - t + here, 0) for t in range(chips - 1)])
        down.append([at.get(t - (chips - 1 - here), 0) for t in range(chips - 1)])
    return order, up, down


class LineRounds:
    def __init__(self, cols_n):
        self.chips = cols_n // 2
        here = lax.axis_index("col") // 2
        self.not_first, self.not_last = here > 0, here < self.chips - 1
        self.sums = []
        self.below = self.above = None

    def add(self, own, other):
        self.sums.append((own, other))

    def arrived(self, below, above):
        self.below, self.above = below, above

    def result(self):
        own, other = self.sums[-1]
        total = own.astype(F32) + other.astype(F32)
        total = total + jnp.where(self.not_first, self.below.astype(F32), 0.0)
        return total + jnp.where(self.not_last, self.above.astype(F32), 0.0)


def routed_kernel(call, rows_n, cols_n, *refs):
    (
        x_hbm, dy_hbm, routes_hbm, routes_t_hbm, gates_hbm, eg_ref, eu_ref, ed_ref, sgu_ref, sd_ref
    ) = refs[:10]
    n_moves = 2 if call else 0
    n_before = 2 if call > 1 else 0
    call_refs, refs = refs[10 : 10 + 2 * call], refs[10 + 2 * call :]
    before, refs = refs[:n_before], refs[n_before:]
    (
        own_hbm, other_hbm, xs_hbm, dys_hbm, hid_ref, gg_ref, gu_ref, ggw_ref, shared_ref
    ) = refs[:9]
    arrivals, refs = refs[9 : 9 + n_moves], refs[9 + n_moves :]
    (
        x_ref, dy_ref, routes_ref, routes_t_ref, gates_ref,
        xs, dys, pick, back_pick, wide_out, wide_gx, slot_gate, stage,
        load_sems, slot_sems, own_sems, core_send, core_recv, *refs,
    ) = refs
    place = Place(rows_n, cols_n)
    my_core = place.core
    unit = jnp.int32(0)
    for chip, calls in enumerate(round_tables(place.chips)[0]):
        unit = unit + jnp.where(place.chip == chip, calls[call], 0)
    pair = pl.ds(2 * unit, 2)
    loads = [
        pltpu.make_async_copy(src.at[pair], dst, load_sems.at[i])
        for i, (src, dst) in enumerate(
            (
                (routes_hbm, routes_ref), (routes_t_hbm, routes_t_ref), (gates_hbm, gates_ref),
                (x_hbm, x_ref), (dy_hbm, dy_ref),
            )
        )
    ]
    line = RoundStart(place, call_refs, arrivals, *refs) if n_moves else None
    e = pl.program_id(0)
    total = x_ref.shape[1]
    cap = xs.shape[1] // 2
    hidden_units = sd_ref.shape[0]
    first = place.col * EXP_DEV
    spans = [slice(at, at + 512) for at in range(0, x_ref.shape[2], 512)]

    def slot_copy(which):
        src, dst = ((xs, xs_hbm), (dys, dys_hbm))[which]
        return pltpu.make_async_copy(src, dst, slot_sems.at[which])

    def own_copy(which):
        return pltpu.make_async_copy(
            stage.at[which, my_core], own_hbm.at[which], own_sems.at[which]
        )

    def core_copy(which):
        return remote(
            stage.at[which, 1 - my_core], other_hbm.at[which], core_send.at[which],
            core_recv.at[which], (place.row, place.other),
        )

    @pl.when(e == 0)
    def _():
        if n_moves:
            line.load(call - 1, before)
        for load in loads:
            load.start()
        place.greet(False)
        if n_moves:
            line.send(before)
        ggw_ref[...] = jnp.zeros_like(ggw_ref)
        for load in loads:
            load.wait()
        row_at = lax.broadcasted_iota(jnp.int32, (total, total), 0)
        col_at = lax.broadcasted_iota(jnp.int32, (total, total), 1)
        upto = jnp.where(row_at <= col_at, 1.0, 0.0).astype(BF)
        since = jnp.where(row_at >= col_at, 1.0, 0.0).astype(BF)
        for core in range(2):
            gate_rows = gates_ref[core]
            route_rows = routes_ref[core]
            route_cols = routes_t_ref[core]
            hits = [
                jnp.sum(jnp.where(route_rows == first + i, 1.0, 0.0), axis=0, keepdims=True)
                for i in range(EXP_DEV)
            ]
            hits = jnp.concatenate(hits + [jnp.zeros((8 - EXP_DEV, total), F32)], axis=0)
            rank = jnp.where(hits > 0.0, mm(hits.astype(BF), upto) - 1.0, -1.0)
            hits_t = [
                jnp.sum(jnp.where(route_cols == first + i, 1.0, 0.0), axis=1, keepdims=True)
                for i in range(EXP_DEV)
            ]
            hits_t = jnp.concatenate(hits_t + [jnp.zeros((total, 8 - EXP_DEV), F32)], axis=1)
            rank_t = jnp.where(hits_t > 0.0, mm(since, hits_t.astype(BF)) - 1.0, -1.0)
            at = lax.broadcasted_iota(jnp.int32, (cap, total), 0).astype(F32)
            at_t = lax.broadcasted_iota(jnp.int32, (total, cap), 1).astype(F32)
            backs = []
            for i in range(EXP_DEV):
                here = at == rank[i : i + 1, :]
                gate_row = jnp.sum(
                    jnp.where(route_rows == first + i, gate_rows, 0.0), axis=0, keepdims=True
                )
                slot_gate[i, core * cap : (core + 1) * cap, :] = jnp.sum(
                    jnp.where(here, gate_row, 0.0), axis=1, keepdims=True
                )
                pick[core, i * cap : (i + 1) * cap, :] = jnp.where(here, 1.0, 0.0).astype(BF)
                backs.append(jnp.where(at_t == rank_t[:, i : i + 1], 1.0, 0.0).astype(BF))
            back_pick[core] = jnp.concatenate(backs, axis=1)
            for src, dst in ((x_ref, xs), (dy_ref, dys)):
                for cols in spans:
                    got = mm(pick[core], src[core, :, cols]).astype(BF)
                    for i in range(EXP_DEV):
                        dst[i, core * cap : (core + 1) * cap, cols] = got[
                            i * cap : (i + 1) * cap
                        ]
        slot_copy(0).start()
        slot_copy(1).start()

    rows_x = xs[e]
    gate_part = mm(rows_x, eg_ref[0])
    up_part = mm(rows_x, eu_ref[0])
    act, slope = silu_parts(gate_part)
    grad_hidden = mm_nt(dys[e], ed_ref[0])
    hidden = (act * up_part).astype(BF).astype(F32)
    weight = slot_gate[e]
    gated = (hidden * weight).astype(BF)
    hid_ref[0] = gated
    slot_ggw = jnp.sum(hidden * grad_hidden, axis=1, keepdims=True)
    grad_hidden = grad_hidden * weight
    geg = (grad_hidden * up_part * slope).astype(BF)
    geu = (grad_hidden * act).astype(BF)
    gg_ref[0] = geg
    gu_ref[0] = geu
    rows = pl.ds(pl.multiple_of(e * cap, cap), cap)
    for cols in spans:
        made = mm(gated, ed_ref[0, :, cols]).astype(BF)
        back = (mm_nt(geg, eg_ref[0, cols, :]) + mm_nt(geu, eu_ref[0, cols, :])).astype(BF)
        for core in range(2):
            wide_out[core, rows, cols] = made[core * cap : (core + 1) * cap]
            wide_gx[core, rows, cols] = back[core * cap : (core + 1) * cap]
    sub = lax.broadcasted_iota(jnp.int32, (8, total), 0)
    for core in range(2):
        back = jnp.sum(
            pick[core, rows, :].astype(F32) * slot_ggw[core * cap : (core + 1) * cap],
            axis=0,
            keepdims=True,
        )
        ggw_ref[core] = jnp.where(sub == e, back, ggw_ref[core])

    @pl.when(e == EXP_DEV - 1)
    def _():
        for part in range(2):
            core = my_core if part else 1 - my_core
            both = mm(x_ref[core], sgu_ref[...])
            s_act, s_slope = silu_parts(both[:, :hidden_units])
            s_up = both[:, hidden_units:]
            s_hidden = (s_act * s_up).astype(BF)
            grad_shared = mm_nt(dy_ref[core], sd_ref[...])
            grad_both = jnp.concatenate(
                [(grad_shared * s_up * s_slope).astype(BF), (grad_shared * s_act).astype(BF)],
                axis=1,
            )
            for cols in spans:
                value = mm(back_pick[core], wide_gx[core, :, cols])
                value = value + mm_nt(grad_both, sgu_ref[cols, :])
                stage[1, core, :, cols] = value.astype(BF)
                value = mm(back_pick[core], wide_out[core, :, cols])
                value = value + mm(s_hidden, sd_ref[:, cols])
                stage[0, core, :, cols] = value.astype(BF)
                made = mm_tn(x_ref[core, :, cols], grad_both)
                made_d = mm_tn(dy_ref[core, :, cols], s_hidden)
                if part == 0:
                    shared_ref[cols, : 2 * hidden_units] = made
                    shared_ref[cols, 2 * hidden_units :] = made_d
                else:
                    shared_ref[cols, : 2 * hidden_units] += made
                    shared_ref[cols, 2 * hidden_units :] += made_d
            for which in (1, 0):
                (own_copy if part else core_copy)(which).start()
        slot_copy(0).wait()
        slot_copy(1).wait()
        if n_moves:
            line.wait()
        for which in (1, 0):
            own_copy(which).wait()
            core_copy(which).wait_send()
            core_copy(which).wait_recv()


def routed(
    call, rows_n, x_all, dy_all, routes, routes_t, gates, egate, eup, edown, sgu, sdown, calls,
    before,
):
    call_args = [part for pair in calls for part in pair] + list(before)
    n_moves = 2 if call else 0
    cols_n, total, width = x_all.shape
    cap = 4 * total * TOP // (3 * EXP_DEV * cols_n)
    slots = 2 * cap
    ffn = egate.shape[2]
    hidden_units = sdown.shape[0]

    def each(*shape):
        return pl.BlockSpec((1,) + shape, lambda e: (e,) + (0,) * len(shape))

    def whole(*shape):
        return pl.BlockSpec(
            shape, lambda e: (0,) * len(shape), pipeline_mode=pl.Buffered(1)
        )

    slot_block = each(slots, ffn)
    return pl.pallas_call(
        functools.partial(routed_kernel, call, rows_n, cols_n),
        grid=(EXP_DEV,),
        in_specs=[ANY] * 5
        + [
            each(width, ffn), each(width, ffn), each(ffn, width), whole(*sgu.shape),
            whole(*sdown.shape),
        ]
        + [ANY] * len(call_args),
        out_specs=[
            ANY, ANY, ANY, ANY, slot_block, slot_block, slot_block,
            whole(2, 8, total), whole(width, 3 * hidden_units),
        ]
        + [ANY] * n_moves,
        out_shape=[
            jax.ShapeDtypeStruct((2, total, width), BF),
            jax.ShapeDtypeStruct((2, total, width), BF),
            jax.ShapeDtypeStruct((EXP_DEV, slots, width), BF),
            jax.ShapeDtypeStruct((EXP_DEV, slots, width), BF),
            jax.ShapeDtypeStruct((EXP_DEV, slots, ffn), BF),
            jax.ShapeDtypeStruct((EXP_DEV, slots, ffn), BF),
            jax.ShapeDtypeStruct((EXP_DEV, slots, ffn), BF),
            jax.ShapeDtypeStruct((2, 8, total), F32),
            jax.ShapeDtypeStruct((width, 3 * hidden_units), F32),
        ]
        + [jax.ShapeDtypeStruct((total, width), BF)] * n_moves,
        scratch_shapes=[
            pltpu.VMEM((2, total, width), BF),
            pltpu.VMEM((2, total, width), BF),
            pltpu.VMEM((2, 8, total), jnp.int32),
            pltpu.VMEM((2, total, 8), jnp.int32),
            pltpu.VMEM((2, 8, total), F32),
            pltpu.VMEM((EXP_DEV, slots, width), BF),
            pltpu.VMEM((EXP_DEV, slots, width), BF),
            pltpu.VMEM((2, EXP_DEV * cap, total), BF),
            pltpu.VMEM((2, total, EXP_DEV * cap), BF),
            pltpu.VMEM((2, EXP_DEV * cap, width), BF),
            pltpu.VMEM((2, EXP_DEV * cap, width), BF),
            pltpu.VMEM((EXP_DEV, slots, 1), F32),
            pltpu.VMEM((2, 2, total, width), BF),
            pltpu.SemaphoreType.DMA((5,)),
            pltpu.SemaphoreType.DMA((2,)),
            pltpu.SemaphoreType.DMA((2,)),
            pltpu.SemaphoreType.DMA((2,)),
            pltpu.SemaphoreType.DMA((2,)),
        ]
        + (
            RoundStart.scratch((total, width)) if call else []
        ),
        compiler_params=pltpu.CompilerParams(
            collective_id=4 + call, has_side_effects=True, vmem_limit_bytes=60 * 1024 * 1024
        ),
        cost_estimate=pl.CostEstimate(
            flops=24_000_000_000, bytes_accessed=100_000_000, transcendentals=0
        ),
        name="routed",
    )(
        x_all, dy_all, routes, routes_t, gates, egate, eup, edown, sgu, sdown, *call_args
    )


def expert_grads_kernel(units_n, rows_n, cut_left, *refs):
    left, right, out_ref = refs[:units_n], refs[units_n : 2 * units_n], refs[-1]
    inner = (left if cut_left else right)[0].shape[2] // rows_n

    def joined(parts, cols=slice(None)):
        return jnp.concatenate([part[0, :, cols] for part in parts], axis=0)

    other = joined(right if cut_left else left)
    for row in range(rows_n):
        cut = joined(left if cut_left else right, slice(row * inner, (row + 1) * inner))
        pair = (cut, other) if cut_left else (other, cut)
        out_ref[row, 0] = mm_tn(*pair).astype(BF)


def expert_grads(left, right, rows_n, cut_left):
    slots = left[0].shape[1]
    units_n = len(left)
    sizes = [left[0].shape[2], right[0].shape[2]]
    specs = [
        pl.BlockSpec((1, slots, size), lambda e: (e, 0, 0)) for size in sizes for _ in left
    ]
    sizes[0 if cut_left else 1] //= rows_n
    return pl.pallas_call(
        functools.partial(expert_grads_kernel, units_n, rows_n, cut_left),
        grid=(EXP_DEV,),
        in_specs=specs,
        out_specs=pl.BlockSpec((rows_n, 1) + tuple(sizes), lambda e: (0, e, 0, 0)),
        out_shape=jax.ShapeDtypeStruct((rows_n, EXP_DEV) + tuple(sizes), BF),
        compiler_params=pltpu.CompilerParams(vmem_limit_bytes=60 * 1024 * 1024),
        cost_estimate=pl.CostEstimate(
            flops=7_000_000_000, bytes_accessed=30_000_000, transcendentals=0
        ),
        name="expert_grads",
    )(*left, *right)


def on_device(
    tokens,
    g_attn,
    w_query,
    key_projection,
    value_projection,
    w_out,
    g_moe,
    w_router,
    e_gate,
    e_up,
    e_down,
    s_gate,
    s_up,
    s_down,
    routes,
    deal,
    lengths,
    cotangent,
):
    rows_n = lax.axis_size("row")
    cols_n = lax.axis_size("col")
    row_here = lax.axis_index("row")
    col_here = lax.axis_index("col")
    both = ("row", "col")
    total = tokens.shape[0]
    width = MODEL_WIDTH
    experts = EXP_DEV * cols_n

    q_w, k_w = w_query.shape[1], key_projection.shape[1]
    inner = w_query.shape[0]
    gains = jnp.stack([g_attn, g_moe])
    gains = jnp.pad(gains, ((0, 0), (0, inner - gains.shape[1])))
    tail = jnp.concatenate([w_router.T, gains], axis=0)
    tail = jnp.pad(tail, ((0, 16 - tail.shape[0]), (0, 0)))
    bundle = jnp.concatenate(
        [w_query.T, key_projection.T, value_projection.T, w_out.T, tail], axis=0
    )
    routes_t = jnp.pad(routes.T, ((0, 8 - TOP), (0, 0)), constant_values=-1)
    units = s_gate.shape[1]
    shared = jnp.concatenate([s_gate, s_up], axis=1)
    per_row = s_down.shape[0] // units
    downs = s_down.reshape(per_row, units * s_down.shape[1] // 128, 128)
    full, dy_all, routes_all, sgu, sdown, egate, e_up, e_down, _ = first_gather(
        bundle, cotangent, routes_t, shared, downs, e_gate, [e_up, e_down], 0, rows_n, cols_n
    )
    sdown = sdown.reshape(cols_n, units, width // cols_n)
    sdown = jnp.swapaxes(sdown, 0, 1).reshape(units, width)
    sgu = sgu.reshape(width, 2 * units)

    t_at = 2 * q_w + 2 * k_w
    extents = [q_w, k_w, k_w, q_w, 16]
    n_gain = g_attn.shape[0]
    gains = full[:, :, t_at + EXP_DEV : t_at + EXP_DEV + 2, :n_gain].transpose(2, 0, 1, 3)
    gains = gains.reshape(2, width).astype(F32)
    eup = lax.all_gather(e_up, "row", axis=1, tiled=True)
    edown = lax.all_gather(e_down, "row", axis=2, tiled=True)
    by_row = lengths.reshape(rows_n, cols_n, rows_n)
    by_row = lax.dynamic_slice(by_row, (0, col_here, row_here), (rows_n, 1, 1)).reshape(1, rows_n)
    row_ids = jnp.arange(rows_n, dtype=jnp.int32)
    own_lens = jnp.sum(jnp.where(deal.reshape(-1, 1) == row_ids, by_row, 0), axis=1)
    seq_ends = jnp.sum(jnp.where(row_ids[None, :] <= row_ids[:, None], own_lens, 0), axis=1)
    places = jnp.arange(total, dtype=jnp.int32)
    segment = jnp.sum((places[:, None] >= seq_ends[None, :]).astype(jnp.int32), axis=1)

    (
        normed_one, queries, keys, values, mixed, log_totals, after_attn, normed_two, scale_one,
        scale_two, gates, gates_t,
    ) = block_start(tokens, full, extents, gains, segment, routes)

    x_all, gates_all = line_gather([normed_two, gates_t], 1, rows_n, cols_n)
    chips = cols_n // 2
    my_order = jnp.array(round_tables(chips)[0], jnp.int32)[col_here // 2]
    routes_rows = jnp.swapaxes(routes_all, 1, 2)
    moe_sum = LineRounds(cols_n)
    saved, calls, before, ggw, grad_sh = [], [], (), [], 0.0
    for call in range(chips):
        own, other, *keep = routed(
            call, rows_n, x_all, dy_all, routes_all, routes_rows, gates_all, egate, eup, edown,
            sgu, sdown, calls, before,
        )
        saved.append(keep[:5])
        ggw_part, sh_part, *arrivals = keep[5:]
        before = tuple(arrivals)
        grad_sh = grad_sh + sh_part
        ggw.append(ggw_part)
        calls.append((own, other))
    xs, dys, hid, gg, gu = zip(*saved)
    grad_edown = expert_grads(hid, dys, rows_n, False)
    grad_egate = expert_grads(xs, gg, rows_n, True)
    grad_eup = expert_grads(xs, gu, rows_n, True)
    ggw = jnp.stack(ggw)[:, None, :, :EXP_DEV]
    is_unit = my_order[:, None] == jnp.arange(chips, dtype=jnp.int32)
    ggw = jnp.sum(jnp.where(is_unit[:, :, None, None, None], ggw, 0.0), axis=0)
    ggw = ggw.reshape(cols_n, EXP_DEV, total)

    ggw_home = lax.all_to_all(ggw, "col", split_axis=0, concat_axis=0, tiled=True)
    grad_tokens, gq, gk, gv, grad_attn_b, logits_left, gain_grads = block_end(
        tokens, cotangent, full, extents, gains, segment, routes, gates,
        ggw_home.reshape(experts, total),
        (calls[-1][0][1], calls[-1][1][1], *before),
        queries, keys, values, log_totals, after_attn, scale_one, scale_two,
    )

    def gain_rows(grad):
        part = grad.reshape(rows_n, cols_n, 1, n_gain)
        return jnp.pad(part, ((0, 0),) * 3 + ((0, inner - n_gain),))

    tails = jnp.concatenate([gain_rows(gain_grads[0]), gain_rows(gain_grads[1])], axis=2)
    tails = jnp.pad(tails, ((0, 0), (0, 0), (EXP_DEV, 16 - EXP_DEV - 2), (0, 0)))
    tails = tails.reshape(rows_n, cols_n * 16, inner)
    grads_sh = grad_sh.astype(BF).reshape(rows_n, inner, 3 * units)
    dense, dense_sh, sd_parts, arrivals = dense_sum(
        [gq, gk, gv, grad_attn_b, logits_left],
        [normed_one, normed_one, normed_one, mixed, normed_two],
        tails, grads_sh, calls, 2, rows_n, cols_n,
    )
    moe_sum.add(calls[-1][0][0], calls[-1][1][0])
    moe_sum.arrived(arrivals[-1, 0], arrivals[-1, 1])
    output = (after_attn + moe_sum.result()).astype(BF)
    out_wq = dense[:q_w].T
    out_wk = dense[q_w : q_w + k_w].T
    out_wv = dense[q_w + k_w : q_w + 2 * k_w].T
    out_wo = dense[q_w + 2 * k_w : t_at].T
    out_router = dense[t_at : t_at + EXP_DEV].T
    out_g_attn = dense[t_at + EXP_DEV, :n_gain]
    out_g_moe = dense[t_at + EXP_DEV + 1, :n_gain]
    out_sg = dense_sh[:, :units]
    out_su = dense_sh[:, units:]
    out_sd = sd_parts.transpose(0, 2, 1).reshape(per_row * units, inner // per_row)

    def row_sum(grad):
        return lax.psum_scatter(grad, "row", scatter_dimension=0).astype(F32)

    out_eg = row_sum(grad_egate)
    out_eu = row_sum(grad_eup)
    out_ed = row_sum(grad_edown)
    return (
        output,
        grad_tokens,
        out_g_attn,
        out_wq,
        out_wk,
        out_wv,
        out_wo,
        out_g_moe,
        out_router,
        out_eg,
        out_eu,
        out_ed,
        out_sg,
        out_su,
        out_sd,
    )


def solution(mesh):
    both = P(("row", "col"), None)
    flat = P(("row", "col"))
    tile = P("row", "col")
    wide = P("col", "row", None)
    down = P("col", None, "row")
    return jax.shard_map(
        on_device,
        mesh=mesh,
        in_specs=(
            both, flat, tile, tile, tile, tile, flat, tile, wide, wide, down,
            tile, tile, tile, both, both, P(), both,
        ),
        out_specs=(
            both, both, flat, tile, tile, tile, tile, flat, tile, wide, wide, down,
            tile, tile, tile,
        ),
        check_vma=False,
    )
```
